32 devices in a mesh: sec: 2 (over x), ep: 16 (over z, y, core).
Axes of the slice: x: 2, y: 2, z: 4, core: 2. Of those that a mesh axis runs over, the one named last changes fastest.
Arguments:
- queries: bfloat16 [32, 4, 32, 576], P(('sec', 'ep')), may hold values from -24 to 24, as said below
- new_latent: bfloat16 [32, 4, 576], P(('sec', 'ep')), may hold values from -5 to 5
- cache_latent: bfloat16 [32, 8192, 576], P(('sec', 'ep')), may hold values from -5 to 5
- cache_len: int32 [32], P(('sec', 'ep')), may hold values from 1 to 8192, 131072 in all
- route_ids: int32 [32, 4, 8], P(('sec', 'ep')), may hold values from 0 to 15, all different within a row; in each aligned block of 4 rows (0 to 3, 4 to 7, ..., all dimensions but the last counted through in order) at most 2 rows name the same one
- route_scores: float32 [32, 4, 8], P(('sec', 'ep')), may hold values from 0.02 to 1
- residual: bfloat16 [32, 4, 7168], P(('sec', 'ep')), may hold values from -6 to 6
- norm_gain: bfloat16 [7168], replicated, may hold values from 0.099609375 to 1.8984375
- w_uv: bfloat16 [32, 512, 128], P(('sec', 'ep')), may hold values from -0.25 to 0.25
- w_out: bfloat16 [32, 128, 7168], P(('sec', 'ep')), may hold values from -0.09375 to 0.09375
- w_gate: bfloat16 [16, 7168, 1024], P('ep', None, 'sec'), may hold values from -0.0625 to 0.0625
- w_up: bfloat16 [16, 7168, 1024], P('ep', None, 'sec'), may hold values from -0.0625 to 0.0625
- w_down: bfloat16 [16, 1024, 7168], P('ep', 'sec'), may hold values from -0.1875 to 0.1875
Outputs:
- mixed: bfloat16 [32, 4, 7168], P(('sec', 'ep'))
The draws below stay inside these ranges and needn't reach their ends.
Inputs may be any that keep to these rules, and one draw needn't show every extreme that they name: `queries`: A few heads of some rows may have a query that is a multiple of that row's new latent entry. `route_ids`: each row and step names 8 different experts; over the 4 steps of one row no expert is named more than 2 times, and in some rows one expert is named exactly 2 times.
All inputs are finite; a program needn't handle non-finite values. No bound on the sum of `cache_len` on one device may be relied on, other than what follows from the above.
Results may differ from the reference program's by a relative error of at most 0.015.
Values may be sent and summed in bfloat16 or wider, within the bound.
No kernel may reach another device: no remote copies, remote signals or barrier semaphores. Data moves between devices by JAX's collectives and lax.ppermute only.
A program may use at most 128 MiB of HBM per device.

```python
import math
import jax
import jax.numpy as jnp
import numpy as np
from jax import lax

D = 7168
LAT = 512
ROPE = 64
KV = 576
VDIM = 128
HEADS = 32
TOPK = 8
EXPERTS = 16
FF = 1024
STEPS = 4
ROWS = 32
CACHE = 8192
CAP = 2


def shared_latent(key):
    base_rows = jax.random.normal(jax.random.fold_in(key, 11), (ROWS, KV), jnp.float32)
    offsets = jax.random.normal(jax.random.fold_in(key, 12), (ROWS, KV), jnp.float32)
    return (jnp.clip(base_rows, -4.0, 4.0), jnp.clip(offsets, -4.0, 4.0))


def draw_new_latent(key, part):
    base_rows, offsets = shared_latent(key)
    factors = 0.2 * jnp.arange(STEPS, dtype=jnp.float32) / (STEPS - 1)
    return (base_rows[:, None, :] + factors[None, :, None] * offsets[:, None, :]).astype(jnp.bfloat16)


def draw_queries(key, part):
    drawn = jax.random.normal(jax.random.fold_in(key, 24), (ROWS, STEPS, HEADS, KV), jnp.float32)
    return (1.5 * jnp.clip(drawn, -6.0, 6.0)).astype(jnp.bfloat16)


def steps_of(rng, shape, shards, low, high):
    loudness = 1.0
    for position, blocks in shards:
        heights = jax.random.uniform(jax.random.fold_in(jax.random.fold_in(rng, 6), position), (blocks,), jnp.float32, low / len(shards), high / len(shards))
        loudness = loudness * jnp.repeat(jnp.exp(heights), shape[position] // blocks).reshape((-1,) + (1,) * (len(shape) - 1 - position))
    return loudness


def length_profile(count, total, bound, skew):
    portions = [(1 << 20) // math.isqrt(standing ** skew) + 1 for standing in range(2, count + 1)]
    spare, counts = total - bound - (count - 1), [1] * (count - 1)
    while spare > 0:
        movable = [i for i in range(count - 1) if counts[i] < bound]
        mass, left = sum([portions[i] for i in movable]), spare
        for i in movable:
            addition = min(bound - counts[i], max(1, left * portions[i] // mass), spare)
            counts[i] = counts[i] + addition
            spare = spare - addition
    return np.array([bound] + counts)


def ragged_sizes(rng, amount, total, bound, skew):
    if amount == 2:
        one = jax.random.randint(rng, (), max(1, total - bound), min(bound, total - 1) + 1)
        return jnp.stack([one, total - one])
    sizes = jnp.asarray(length_profile(amount, total, bound, skew), jnp.int32)
    twos = (amount - 1) // 2
    donor, taker = sizes[1:1 + 2 * twos:2], sizes[2:2 + 2 * twos:2]
    slack = jnp.minimum(donor - 1, bound - taker)
    passed = jax.random.randint(jax.random.fold_in(rng, 1), (twos,), 0, 1 << 20) % (slack + 1)
    sizes = sizes.at[1:1 + 2 * twos:2].set(donor - passed).at[2:2 + 2 * twos:2].set(taker + passed)
    return sizes[jax.random.permutation(jax.random.fold_in(rng, 2), amount)]


def routed_block(stream_key, own, number, rows, amount, top, bound, skew):
    sequence = jax.random.permutation(stream_key, amount)
    crowded, common = portions_of(amount, rows * top, bound, skew, True), portions_of(amount, rows * top, bound, skew, False)
    places = jnp.arange(amount)

    def named(sizes, rotation):
        used = int((sizes > 0).sum())
        fixed = max(1, used // 4)
        moved = fixed + (places - fixed + rotation * (used - fixed)) % max(1, amount - fixed)
        return jnp.zeros((amount,), jnp.int32).at[sequence[jnp.where(places < fixed, places, moved)]].set(jnp.asarray(sizes, jnp.int32))

    sizes = jnp.where(number % 4 == 0, named(crowded, number // 4), named(common, number - number // 4 - 1))
    mixed = jax.random.permutation(jax.random.fold_in(own, 3), amount)
    donor, taker = mixed[0:amount // 2 * 2:2], mixed[1:amount // 2 * 2:2]
    margin = jnp.minimum(sizes[donor] - 1, bound - sizes[taker]) // 2
    margin = jnp.where((donor == sequence[0]) | (taker == sequence[0]) | (sizes[taker] == 0), 0, jnp.maximum(margin, 0))
    moved = jax.random.randint(jax.random.fold_in(own, 4), (amount // 2,), 0, 1 << 20) % (margin + 1)
    sizes = sizes.at[donor].add(-moved).at[taker].add(moved)
    items = jnp.searchsorted(jnp.cumsum(sizes), jnp.arange(rows * top), side="right").astype(jnp.int32)
    grid = items.reshape(top, rows).T
    grid = grid[jax.random.permutation(jax.random.fold_in(own, 1), rows)]
    rotation = jax.random.randint(jax.random.fold_in(own, 2), (rows, 1), 0, top)
    return jnp.take_along_axis(grid, (jnp.arange(top)[None, :] + rotation) % top, axis=1)


def portions_of(amount, total, most, skew, full):
    portions = [(1 << 20) // math.isqrt(rank ** skew) + 1 for rank in range(1, amount + 1)]
    largest = most if full else min(most, max(-(-total // amount), total * portions[0] // sum(portions)))
    least = 1 if total - largest >= amount - 1 else 0
    given, rest = [largest] + [least] * (amount - 1), total - largest - least * (amount - 1)
    while rest > 0:
        candidates = [i for i in range(1, amount) if given[i] < largest] or [i for i in range(1, amount) if given[i] < most]
        pool, remaining = sum([portions[i] for i in candidates]), rest
        for i in candidates:
            more = min(most - given[i], max(1, remaining * portions[i] // pool), rest)
            given[i] = given[i] + more
            rest = rest - more
    return np.array(given)


def noise(rng, shape, deviation, bound, shards=(), kind=jnp.bfloat16):
    entries = jax.random.normal(rng, shape, jnp.float32) * deviation
    if len(shards) > 0:
        entries = steps_of(rng, shape, shards, -0.22, 0.18) * entries
    return jnp.clip(entries, min=-bound, max=bound).astype(kind)


def setup_inputs(seed: int = 0) -> dict:
    arg_keys = jax.random.split(jax.random.key(seed), 14)
    queries = draw_queries(jax.random.fold_in(arg_keys[13], 71), 0)
    new_latent = draw_new_latent(jax.random.fold_in(arg_keys[13], 71), 0)
    cache_latent = noise(arg_keys[2], (ROWS, CACHE, KV), 1.0, 5.0, ((0, 32),))
    cache_len = ragged_sizes(arg_keys[3], ROWS, ROWS * CACHE // 2, CACHE, 2).astype(jnp.int32)
    route_ids_keys = jax.random.split(jax.random.fold_in(arg_keys[4], 1), ROWS * STEPS // STEPS)
    route_ids_turns = jax.random.permutation(jax.random.fold_in(arg_keys[4], 3), ROWS * STEPS // STEPS)
    route_ids = jax.vmap(lambda own, number: routed_block(jax.random.fold_in(arg_keys[4], 2), own, number, STEPS, EXPERTS, TOPK, CAP, 2))(route_ids_keys, route_ids_turns).reshape((ROWS, STEPS, TOPK))
    route_scores = jnp.clip(jnp.exp(math.log(1.0) - 3.912023 * jax.random.uniform(arg_keys[5], (ROWS, STEPS, TOPK), jnp.float32) ** steps_of(arg_keys[5], (ROWS, STEPS, TOPK), ((0, 32),), -0.2, 0.2)), 0.02, 1.0)
    residual = noise(arg_keys[6], (ROWS, STEPS, D), 1.0, 6.0, ((0, 32),))
    norm_gain = jnp.clip(1.0 + 0.18 * jax.random.normal(arg_keys[7], (D,), jnp.float32), 0.099609375, 1.8984375).astype(jnp.bfloat16)
    w_uv = noise(arg_keys[8], (HEADS, LAT, VDIM), LAT ** -0.5, 0.25, ((0, 32),))
    w_out = noise(arg_keys[9], (HEADS, VDIM, D), (HEADS * VDIM) ** -0.5, 0.09375, ((0, 32),))
    w_gate = noise(arg_keys[10], (EXPERTS, D, FF), D ** -0.5, 0.0625, ((0, 16), (2, 2)))
    w_up = noise(arg_keys[11], (EXPERTS, D, FF), D ** -0.5, 0.0625, ((0, 16), (2, 2)))
    w_down = noise(arg_keys[12], (EXPERTS, FF, D), FF ** -0.5, 0.1875, ((0, 16), (1, 2)))
    return {"queries": queries, "new_latent": new_latent, "cache_latent": cache_latent, "cache_len": cache_len, "route_ids": route_ids, "route_scores": route_scores, "residual": residual, "norm_gain": norm_gain, "w_uv": w_uv, "w_out": w_out, "w_gate": w_gate, "w_up": w_up, "w_down": w_down}


def reference(queries, new_latent, cache_latent, cache_len, route_ids, route_scores, residual, norm_gain, w_uv, w_out, w_gate, w_up, w_down):
    score_scale = (VDIM + ROPE) ** (-0.5)
    key_count = CACHE + STEPS

    def one_row(packed):
        query_rows, new_keys, cached_rows, length = packed
        key_rows = jnp.concatenate([cached_rows, new_keys], 0).astype(jnp.float32)
        positions = jnp.arange(key_count, dtype=jnp.int32)
        step_ids = jnp.arange(STEPS, dtype=jnp.int32)
        old_ok = jnp.broadcast_to(positions[None, :] < length, (STEPS, key_count))
        new_ok = positions[None, :] - CACHE <= step_ids[:, None]
        visible = jnp.where(positions[None, :] < CACHE, old_ok, new_ok)
        scores = jnp.einsum('shk,tk->sht', query_rows.astype(jnp.float32), key_rows) * score_scale
        scores = jnp.where(visible[:, None, :], scores, -jnp.inf)
        largest = lax.optimization_barrier(jnp.max(scores, axis=-1, keepdims=True))
        weights = jnp.exp(scores - largest)
        denominator = lax.optimization_barrier(jnp.sum(weights, axis=-1, keepdims=True))
        rounded = lax.optimization_barrier(weights.astype(jnp.bfloat16)).astype(jnp.float32)
        summed = jnp.einsum('sht,tl->shl', rounded, key_rows[:, :LAT])
        return (summed / denominator).astype(jnp.bfloat16)
    latent_out = lax.map(one_row, (queries, new_latent, cache_latent, cache_len))
    head_values = jnp.einsum('rshl,hlv->rshv', latent_out.astype(jnp.float32), w_uv.astype(jnp.float32)).astype(jnp.bfloat16)
    flat_values = head_values.reshape(ROWS * STEPS, HEADS * VDIM)
    attended = jnp.dot(flat_values, w_out.reshape(HEADS * VDIM, D), preferred_element_type=jnp.float32)
    hidden = residual.reshape(ROWS * STEPS, D).astype(jnp.float32) + attended
    mean_square = lax.optimization_barrier(jnp.mean(hidden * hidden, axis=-1, keepdims=True))
    normed = (hidden * lax.rsqrt(mean_square + 1e-06) * norm_gain.astype(jnp.float32)).astype(jnp.bfloat16)
    shares = route_scores / lax.optimization_barrier(jnp.sum(route_scores, axis=-1, keepdims=True)) * 2.5
    matches = route_ids[..., None] == jnp.arange(EXPERTS, dtype=jnp.int32)
    coefficient = lax.optimization_barrier(jnp.sum(jnp.where(matches, shares[..., None], 0.0), axis=2)).reshape(ROWS * STEPS, EXPERTS)

    def expert_step(summed, packed):
        gate_matrix, up_matrix, down_matrix, column = packed
        gate_value = jnp.dot(normed, gate_matrix, preferred_element_type=jnp.float32)
        up_value = jnp.dot(normed, up_matrix, preferred_element_type=jnp.float32)
        activated = (jax.nn.silu(gate_value) * up_value).astype(jnp.bfloat16)
        expert_out = jnp.dot(activated, down_matrix, preferred_element_type=jnp.float32).astype(jnp.bfloat16)
        expert_out = lax.optimization_barrier(expert_out).astype(jnp.float32)
        return (summed + column[:, None] * expert_out, None)
    start_sum = jnp.zeros((ROWS * STEPS, D), jnp.float32)
    summed, _ = lax.scan(expert_step, start_sum, (w_gate, w_up, w_down, coefficient.T))
    return (hidden + summed).astype(jnp.bfloat16).reshape(ROWS, STEPS, D)
```

```python
import functools

import jax
import jax.numpy as jnp
from jax import lax
from jax.experimental import pallas as pl
from jax.experimental.pallas import tpu as pltpu
from jax.sharding import PartitionSpec as P

LAT = 512
ROPE = 64
VDIM = 128
STEPS = 4
CAP = 2
BLK = 1024
SPAN = 8
AXES = ("sec", "ep")
NT = (((1,), (1,)), ((), ()))
BF = jnp.bfloat16
F32 = jnp.float32
VMEM_LIMIT = 40 * 1024 * 1024


def place_mask(j, n):
    return (j >> 2) * (n // 2) + (j & 3)


def swap(x, mask, n):
    return lax.ppermute(x, AXES, [(d, d ^ mask) for d in range(n)])


def iota2(shape, axis):
    return lax.broadcasted_iota(jnp.int32, shape, axis)


def one_hot(columns, count):
    return (iota2(columns.shape, 1) == columns).astype(BF)


def pick(matrix, rows):
    return jnp.dot(matrix, rows, preferred_element_type=F32)


def attend_kernel(n, len_ref, me_ref, q_ref, new_ref, keys_ref, *rest):
    planes = n // SPAN
    outs, (m_ref, l_ref, acc_ref) = rest[:planes], rest[planes:]
    rows = q_ref.shape[0]
    heads = rows // STEPS
    scale = (VDIM + ROPE) ** (-0.5)
    i = pl.program_id(0)
    length = len_ref[0]
    blk = keys_ref.shape[1]

    @pl.when(i == 0)
    def _():
        new = new_ref[...]
        s = lax.dot_general(q_ref[...], new, NT, preferred_element_type=F32) * scale
        step = iota2(s.shape, 0) // heads
        s = jnp.where(iota2(s.shape, 1) <= step, s, -1e30)
        m = jnp.max(s, axis=1, keepdims=True)
        p = jnp.exp(s - m)
        m_ref[...] = m
        l_ref[...] = jnp.sum(p, axis=1, keepdims=True)
        acc_ref[...] = jnp.dot(p.astype(BF), new[:, :LAT], preferred_element_type=F32)

    @pl.when(i * blk < length)
    def _():
        keys = keys_ref[...]
        s = jnp.dot(q_ref[...], keys, preferred_element_type=F32) * scale
        s = jnp.where(iota2(s.shape, 1) < length - i * blk, s, -1e30)
        m_old = m_ref[...]
        m = jnp.maximum(m_old, jnp.max(s, axis=1, keepdims=True))
        factor = jnp.exp(m_old - m)
        p = jnp.exp(s - m)
        m_ref[...] = m
        l_ref[...] = l_ref[...] * factor + jnp.sum(p, axis=1, keepdims=True)
        acc_ref[...] = acc_ref[...] * factor + lax.dot_general(
            p.astype(BF), keys[:LAT], NT, preferred_element_type=F32
        )

    @pl.when(i == pl.num_programs(0) - 1)
    def _():
        out = (acc_ref[...] / l_ref[...]).astype(BF)
        me = me_ref[0]
        r = iota2((rows, rows), 0)
        k, j, step = r // (SPAN * STEPS), (r // STEPS) % SPAN, r % STEPS
        head = me ^ (k * 4 + (j >> 2) * (n // 2) + (j & 3))
        moved = pick(one_hot(step * heads + head, rows), out).astype(BF)
        for k in range(planes):
            outs[k][...] = moved[k * SPAN * STEPS : (k + 1) * SPAN * STEPS]


def attend(n, length, me, q, new, keys):
    planes = n // SPAN
    rows, width = q.shape
    cached = keys.shape[1]
    blk = min(BLK, cached)

    def block(i, len_ref, me_ref):
        return (0, jnp.minimum(i, (len_ref[0] - 1) // blk))

    def whole(i, len_ref, me_ref):
        return (0, 0)

    return pl.pallas_call(
        functools.partial(attend_kernel, n),
        grid_spec=pltpu.PrefetchScalarGridSpec(
            num_scalar_prefetch=2,
            grid=(cached // blk,),
            in_specs=[
                pl.BlockSpec(q.shape, whole),
                pl.BlockSpec(new.shape, whole),
                pl.BlockSpec((width, blk), block),
            ],
            out_specs=[pl.BlockSpec((SPAN * STEPS, LAT), whole)] * planes,
            scratch_shapes=[
                pltpu.VMEM((rows, 1), F32),
                pltpu.VMEM((rows, 1), F32),
                pltpu.VMEM((rows, LAT), F32),
            ],
        ),
        out_shape=[jax.ShapeDtypeStruct((SPAN * STEPS, LAT), BF)] * planes,
        compiler_params=pltpu.CompilerParams(vmem_limit_bytes=VMEM_LIMIT),
        cost_estimate=pl.CostEstimate(
            flops=2 * rows * cached * (width + LAT),
            bytes_accessed=2 * cached * width,
            transcendentals=rows * cached,
        ),
        name="attend",
    )(length, me, q, new, keys)


def values_kernel(n, *refs):
    planes = n // SPAN
    latents, uvs, out_ref = refs[:planes], refs[planes : planes + SPAN], refs[-1]
    rows = n * STEPS
    group = planes * STEPS
    stacked = jnp.concatenate([ref[...] for ref in latents], axis=0)
    r = iota2((rows, rows), 0)
    j, k, step = r // group, (r // STEPS) % planes, r % STEPS
    by_head = pick(one_hot((k * SPAN + j) * STEPS + step, rows), stacked).astype(BF)
    for j in range(SPAN):
        out_ref[:, j * VDIM : (j + 1) * VDIM] = jnp.dot(
            by_head[j * group : (j + 1) * group], uvs[j][...], preferred_element_type=F32
        ).astype(BF)


def project_kernel(n, me_ref, *refs):
    planes = n // SPAN
    values, weights, outs = refs[:SPAN], refs[SPAN : 2 * SPAN], refs[2 * SPAN :]
    rows = n * STEPS
    group = planes * STEPS
    me = me_ref[0]
    place = (me // (n // 2)) * 4 + me % 4
    columns = [
        jnp.concatenate(
            [values[j][:, (i ^ j) * VDIM : ((i ^ j) + 1) * VDIM] for j in range(SPAN)], axis=0
        )
        for i in range(SPAN)
    ]
    stacked = jnp.concatenate(columns, axis=1)
    r = iota2((rows, rows), 0)
    k, p, step = r // (SPAN * STEPS), (r // STEPS) % SPAN, r % STEPS
    moved = pick(one_hot(((p ^ place) * planes + k) * STEPS + step, rows), stacked).astype(BF)
    total = jnp.zeros((rows, weights[0].shape[1]), F32)
    for i in range(SPAN):
        total += jnp.dot(
            moved[:, i * VDIM : (i + 1) * VDIM], weights[i][:VDIM], preferred_element_type=F32
        )
    extra = weights[0].shape[0] - VDIM
    carried = jnp.concatenate([weights[i][VDIM:] for i in range(SPAN)], axis=0)
    r = iota2((SPAN * STEPS, SPAN * extra), 0)
    own = pick(one_hot(((r // STEPS) ^ place) * extra + r % STEPS, SPAN * extra), carried)
    outs[0][...] = total[: SPAN * STEPS] + own
    for k in range(1, planes):
        outs[k][...] = total[k * SPAN * STEPS : (k + 1) * SPAN * STEPS].astype(BF)


def expert_kernel(n, me_ref, *refs):
    xs, refs = refs[:SPAN], refs[SPAN:]
    gain_ref, coef_ref, gate_ref, up_ref, down_ref = refs[:5]
    near_ref, far_ref, own_ref, gate_acc, up_acc, square_acc, act_ref = refs[5:]
    planes = n // SPAN
    rows = n * STEPS
    i = pl.program_id(0)
    me = me_ref[0]
    place = (me // (n // 2)) * 4 + me % 4
    width = gate_ref.shape[0] * SPAN

    @pl.when(i == 0)
    def _():
        gate_acc[...] = jnp.zeros_like(gate_acc)
        up_acc[...] = jnp.zeros_like(up_acc)
        square_acc[...] = jnp.zeros_like(square_acc)

    for j in range(SPAN):

        @pl.when(i == j)
        def _(j=j):
            raw = xs[j][...]
            x = raw.astype(F32)
            square_acc[...] += jnp.sum(x * x, axis=1, keepdims=True)
            scaled = (x * gain_ref[...].astype(F32)).astype(BF)
            gate_acc[...] += jnp.dot(scaled, gate_ref[...], preferred_element_type=F32)
            up_acc[...] += jnp.dot(scaled, up_ref[...], preferred_element_type=F32)
            r = iota2((own_ref.shape[0], rows), 0)
            mine = jnp.where(r < STEPS, place * STEPS + r, -1)
            own_ref[...] = pick(one_hot(mine, rows), raw).astype(BF)

    @pl.when(i == SPAN - 1)
    def _():
        norm = lax.rsqrt(square_acc[...] / width + 1e-06)
        gate = gate_acc[...] * norm
        act = (gate * jax.nn.sigmoid(gate) * (up_acc[...] * norm)).astype(BF)
        r = iota2((rows, rows), 0)
        c, q = r // (rows // 2), (r // (planes * STEPS)) % 4
        k, step = (r // STEPS) % planes, r % STEPS
        p = place ^ (q * 2 + c)
        act_ref[...] = pick(one_hot((k * SPAN + p) * STEPS + step, rows), act).astype(BF)

    @pl.when(i >= SPAN)
    def _():
        out = jnp.dot(act_ref[...], down_ref[...], preferred_element_type=F32) * coef_ref[...]
        near_ref[...] = out[: rows // 2].astype(BF)
        far_ref[...] = out[rows // 2 :].astype(BF)


def whole_specs(arrays):
    return [pl.BlockSpec(a.shape, lambda i, me_ref: (0, 0)) for a in arrays]


def run_experts(n, me, xs, gain, coef, w_gate, w_up, w_down):
    rows = n * STEPS
    width, hidden_units = w_gate.shape
    part = width // SPAN

    def place_of(me_ref):
        return (me_ref[0] // (n // 2)) * 4 + me_ref[0] % 4

    def depth(i, me_ref):
        return (jnp.minimum(i, SPAN - 1) ^ place_of(me_ref), 0)

    def depth_column(i, me_ref):
        return (0, jnp.minimum(i, SPAN - 1) ^ place_of(me_ref))

    def column(i, me_ref):
        return (0, jnp.maximum(i - SPAN, 0))

    return pl.pallas_call(
        functools.partial(expert_kernel, n),
        grid_spec=pltpu.PrefetchScalarGridSpec(
            num_scalar_prefetch=1,
            grid=(2 * SPAN,),
            in_specs=whole_specs(xs)
            + [
                pl.BlockSpec((1, part), depth_column),
                pl.BlockSpec(coef.shape, lambda i, me_ref: (0, 0)),
                pl.BlockSpec((part, hidden_units), depth),
                pl.BlockSpec((part, hidden_units), depth),
                pl.BlockSpec((hidden_units, part), column),
            ],
            out_specs=[
                pl.BlockSpec((rows // 2, part), column),
                pl.BlockSpec((rows // 2, part), column),
                pl.BlockSpec((16, part), depth_column),
            ],
            scratch_shapes=[
                pltpu.VMEM((rows, hidden_units), F32),
                pltpu.VMEM((rows, hidden_units), F32),
                pltpu.VMEM((rows, 1), F32),
                pltpu.VMEM((rows, hidden_units), BF),
            ],
        ),
        out_shape=[
            jax.ShapeDtypeStruct((rows // 2, width), BF),
            jax.ShapeDtypeStruct((rows // 2, width), BF),
            jax.ShapeDtypeStruct((16, width), BF),
        ],
        compiler_params=pltpu.CompilerParams(vmem_limit_bytes=VMEM_LIMIT),
        cost_estimate=pl.CostEstimate(
            flops=6 * rows * width * hidden_units,
            bytes_accessed=6 * width * hidden_units,
            transcendentals=rows * hidden_units,
        ),
        name="experts",
    )(me, *xs, gain, coef, w_gate, w_up, w_down)


def single(kernel, n, out_shape, me, arrays, name, flops):
    return pl.pallas_call(
        functools.partial(kernel, n),
        in_specs=([pl.BlockSpec(memory_space=pltpu.SMEM)] if me is not None else [])
        + [pl.BlockSpec(memory_space=pltpu.VMEM)] * len(arrays),
        out_shape=out_shape,
        compiler_params=pltpu.CompilerParams(vmem_limit_bytes=VMEM_LIMIT),
        cost_estimate=pl.CostEstimate(
            flops=flops, bytes_accessed=sum(2 * a.size for a in arrays), transcendentals=0
        ),
        name=name,
    )(*([me] if me is not None else []), *arrays)


def per_device(
    queries,
    new_latent,
    cache_latent,
    cache_len,
    route_ids,
    route_scores,
    residual,
    norm_gain,
    w_uv,
    w_out,
    w_gate,
    w_up,
    w_down,
):
    n_ep = lax.axis_size("ep")
    n = lax.axis_size("sec") * n_ep
    planes = n // SPAN
    heads = queries.shape[2]
    width = residual.shape[2]
    part = width // SPAN
    me = lax.axis_index(AXES).astype(jnp.int32)
    me_one = me.reshape(1)
    place = (me // (n // 2)) * 4 + me % 4

    with jax.named_scope("share_weights"):
        uvs = [w_uv[0]] + [swap(w_uv[0], place_mask(j, n), n) for j in range(1, SPAN)]
        extra = jnp.pad(residual[0], ((0, 16 - STEPS), (0, 0)))
        outs = []
        for j in range(SPAN):
            start = (place ^ j) * part
            piece = jnp.concatenate(
                [
                    lax.dynamic_slice(w_out[0], (0, start), (VDIM, part)),
                    lax.dynamic_slice(extra, (0, start), (16, part)),
                ],
                axis=0,
            )
            outs.append(piece if j == 0 else swap(piece, place_mask(j, n), n))

    with jax.named_scope("shares"):
        experts = n_ep * w_gate.shape[0]
        scores = route_scores[0]
        shares = scores / jnp.sum(scores, axis=1, keepdims=True) * 2.5
        matches = route_ids[0][:, :, None] == jnp.arange(experts, dtype=jnp.int32)[None, None, :]
        coef = jnp.sum(jnp.where(matches, shares[:, :, None], 0.0), axis=1)
        coef_all = lax.all_gather(coef, AXES, axis=0, tiled=False)
        mine = lax.dynamic_index_in_dim(coef_all, me % n_ep, axis=2, keepdims=False)
        order = jnp.array(
            [place_mask(q * 2 + c, n) ^ (k * 4) for c in range(2) for q in range(4) for k in range(planes)],
            dtype=jnp.int32,
        )
        coef_rows = mine[me ^ order].reshape(n * STEPS, 1)

    with jax.named_scope("attention"):
        latents = attend(
            n,
            cache_len,
            me_one,
            queries[0].reshape(STEPS * heads, queries.shape[3]),
            new_latent[0],
            jnp.swapaxes(cache_latent[0], 0, 1),
        )

    with jax.named_scope("to_heads"):
        latents = [latents[0]] + [swap(latents[k], 4 * k, n) for k in range(1, planes)]
        values = single(
            values_kernel,
            n,
            jax.ShapeDtypeStruct((planes * STEPS, SPAN * VDIM), BF),
            None,
            list(latents) + uvs,
            "head_values",
            2 * n * STEPS * LAT * VDIM,
        )
        values = [values] + [swap(values, place_mask(j, n), n) for j in range(1, SPAN)]

    with jax.named_scope("project"):
        parts = single(
            project_kernel,
            n,
            [jax.ShapeDtypeStruct((SPAN * STEPS, part), F32 if k == 0 else BF) for k in range(planes)],
            me_one,
            values + outs,
            "project",
            2 * n * STEPS * SPAN * VDIM * part,
        )
        total = parts[0]
        for k in range(1, planes):
            total = total + swap(parts[k], 4 * k, n).astype(F32)
        hidden = total.astype(BF)

    with jax.named_scope("spread_hidden"):
        along = jnp.concatenate(
            [hidden] + [swap(hidden, 4 * k, n) for k in range(1, planes)], axis=0
        )
        xs = [None] * SPAN
        for j in (0, 2, 4, 6):
            xs[j] = along if j == 0 else swap(along, place_mask(j, n), n)
            xs[j + 1] = swap(xs[j], 1, n)

    with jax.named_scope("experts"):
        near, far, own = run_experts(
            n, me_one, xs, norm_gain.reshape(1, width), coef_rows, w_gate[0], w_up[0], w_down[0]
        )

    with jax.named_scope("collect"):
        total = (near.astype(F32) + swap(far, 1, n).astype(F32)).reshape(4, planes * STEPS, width)
        kept = total[0]
        for q in range(1, 4):
            kept = kept + swap(total[q].astype(BF), place_mask(2 * q, n), n).astype(F32)
        kept = kept.reshape(planes, STEPS, width)
        result = kept[0] + own[:STEPS].astype(F32)
        for k in range(1, planes):
            result = result + swap(kept[k].astype(BF), 4 * k, n).astype(F32)
        return result.astype(BF)[None]


def solution(mesh):
    placed = (
        P(("sec", "ep"), None, None, None),
        P(("sec", "ep"), None, None),
        P(("sec", "ep"), None, None),
        P(("sec", "ep")),
        P(("sec", "ep"), None, None),
        P(("sec", "ep"), None, None),
        P(("sec", "ep"), None, None),
        P(),
        P(("sec", "ep"), None, None),
        P(("sec", "ep"), None, None),
        P("ep", None, "sec"),
        P("ep", None, "sec"),
        P("ep", "sec", None),
    )
    return jax.shard_map(
        per_device,
        mesh=mesh,
        in_specs=placed,
        out_specs=P(("sec", "ep"), None, None),
        check_vma=False,
    )
```

```python
import functools
import math

import jax
import jax.numpy as jnp
from jax import lax
from jax.experimental import pallas as pl
from jax.experimental.pallas import tpu as pltpu
from jax.sharding import PartitionSpec as P

LAT = 512
ROPE = 64
VDIM = 128
STEPS = 4
TOPK = 8
BLK = 2048
SPAN = 8
AXES = ("sec", "ep")
NT = (((1,), (1,)), ((), ()))
BF = jnp.bfloat16
F32 = jnp.float32
VMEM_LIMIT = 16 * 1024 * 1024


def device_of(plane, place, n):
    return (place >> 2) * (n // 2) + plane * 4 + (place & 3)


def plane_groups(n):
    return [[device_of(b, p, n) for p in range(SPAN)] for b in range(n // SPAN)]


def line_groups(n):
    return [[device_of(b, p, n) for b in range(n // SPAN)] for p in range(SPAN)]


def chip_groups(n):
    return [[device_of(b, 2 * q + c, n) for q in range(4)] for b in range(n // SPAN) for c in range(2)]


def exchange(x, groups):
    return lax.all_to_all(x, AXES, 0, 0, axis_index_groups=groups, tiled=True)


def swap_core(x, n):
    return lax.ppermute(x, AXES, [(d, d ^ 1) for d in range(n)])


def iota2(shape, axis):
    return lax.broadcasted_iota(jnp.int32, shape, axis)


def one_hot(columns, count):
    return (iota2(columns.shape, 1) == columns).astype(BF)


def pick(matrix, rows):
    return jnp.dot(matrix, rows, preferred_element_type=F32)


def attend_kernel(n, len_ref, q_ref, new_ref, keys_ref, out_ref, m_ref, l_ref, acc_ref):
    rows = q_ref.shape[0]
    heads = rows // STEPS
    factor_base2 = (VDIM + ROPE) ** (-0.5) * math.log2(math.e)
    i = pl.program_id(0)
    length = len_ref[0]
    blk = keys_ref.shape[1]

    @pl.when(i == 0)
    def _():
        new = new_ref[...]
        s = lax.dot_general(q_ref[...], new, NT, preferred_element_type=F32)
        step = iota2(s.shape, 0) // heads
        s = jnp.where(iota2(s.shape, 1) <= step, s, -1e30)
        m = jnp.max(s, axis=1, keepdims=True)
        p = jnp.exp2((s - m) * factor_base2)
        m_ref[...] = m
        l_ref[...] = jnp.sum(p, axis=1, keepdims=True)
        acc_ref[...] = jnp.dot(p.astype(BF), new[:, :LAT], preferred_element_type=F32)

    def update(masked):
        keys = keys_ref[...]
        s = jnp.dot(q_ref[...], keys, preferred_element_type=F32)
        if masked:
            s = jnp.where(iota2(s.shape, 1) < length - i * blk, s, -1e30)
        m_old = m_ref[...]
        m = jnp.maximum(m_old, jnp.max(s, axis=1, keepdims=True))
        factor = jnp.exp2((m_old - m) * factor_base2)
        p = jnp.exp2((s - m) * factor_base2)
        m_ref[...] = m
        l_ref[...] = l_ref[...] * factor + jnp.sum(p, axis=1, keepdims=True)
        acc_ref[...] = acc_ref[...] * factor + lax.dot_general(
            p.astype(BF), keys[:LAT], NT, preferred_element_type=F32
        )

    pl.when((i + 1) * blk <= length)(functools.partial(update, False))
    pl.when((i * blk < length) & ((i + 1) * blk > length))(functools.partial(update, True))

    @pl.when(i == pl.num_programs(0) - 1)
    def _():
        out = (acc_ref[...] / l_ref[...]).astype(BF)
        r = iota2((rows, rows), 0)
        out_ref[...] = pick(one_hot((r % STEPS) * heads + r // STEPS, rows), out).astype(BF)


def attend(n, length, q, new, keys):
    rows, width = q.shape
    cached = keys.shape[1]
    blk = min(BLK, cached)

    def block(i, len_ref):
        return (0, jnp.minimum(i, (len_ref[0] - 1) // blk))

    def whole(i, len_ref):
        return (0, 0)

    return pl.pallas_call(
        functools.partial(attend_kernel, n),
        grid_spec=pltpu.PrefetchScalarGridSpec(
            num_scalar_prefetch=1,
            grid=(cached // blk,),
            in_specs=[
                pl.BlockSpec(q.shape, whole),
                pl.BlockSpec(new.shape, whole),
                pl.BlockSpec((width, blk), block),
            ],
            out_specs=pl.BlockSpec((rows, LAT), whole),
            scratch_shapes=[
                pltpu.VMEM((rows, 1), F32),
                pltpu.VMEM((rows, 1), F32),
                pltpu.VMEM((rows, LAT), F32),
            ],
        ),
        out_shape=jax.ShapeDtypeStruct((rows, LAT), BF),
        compiler_params=pltpu.CompilerParams(vmem_limit_bytes=58 * 1024 * 1024),
        cost_estimate=pl.CostEstimate(
            flops=2 * rows * cached * (width + LAT),
            bytes_accessed=2 * cached * width,
            transcendentals=rows * cached,
        ),
        name="attend",
    )(length, q, new, keys)


def values_kernel(n, latents_ref, uv_ref, out_ref):
    values = jnp.dot(latents_ref[...], uv_ref[...], preferred_element_type=F32).astype(BF)
    for p in range(SPAN):
        out_ref[p] = values


def project_kernel(n, values_ref, weights_ref, out_ref):
    planes = n // SPAN
    group = 4 * STEPS
    total = jnp.zeros((n * STEPS, weights_ref.shape[2]), F32)
    for p in range(SPAN):
        total += jnp.dot(values_ref[p], weights_ref[p, :VDIM], preferred_element_type=F32)
    total = total.astype(BF)
    for b in range(planes):
        for top in range(2):
            start = (top * planes + b) * group
            out_ref[b, top * group : (top + 1) * group] = total[start : start + group]


def expert_kernel(n, me_ref, here_ref, there_ref, gain_ref, routes_ref, gate_ref, up_ref, down_ref, near_ref, far_ref):
    planes = n // SPAN
    rows = n * STEPS
    me = me_ref[0]
    core = me % 2
    expert = me_ref[1]
    part = here_ref.shape[2]
    width = gate_ref.shape[0]
    gate = jnp.zeros((rows, gate_ref.shape[1]), F32)
    up = jnp.zeros((rows, up_ref.shape[1]), F32)
    square = jnp.zeros((rows, 1), F32)
    for ref, side in ((here_ref, core), (there_ref, 1 - core)):
        for q in range(4):
            start = pl.multiple_of((2 * q + side) * part, part)
            x = ref[q].astype(F32)
            square += jnp.sum(x * x, axis=1, keepdims=True)
            scaled = (x * gain_ref[:, pl.ds(start, part)].astype(F32)).astype(BF)
            gate += jnp.dot(scaled, gate_ref[pl.ds(start, part)], preferred_element_type=F32)
            up += jnp.dot(scaled, up_ref[pl.ds(start, part)], preferred_element_type=F32)
    norm = lax.rsqrt(square / width + 1e-06)
    gate = gate * norm
    act = (gate * jax.nn.sigmoid(gate) * (up * norm)).astype(BF)
    r = iota2((rows, rows), 0)
    c, q = r // (rows // 2), (r // (planes * STEPS)) % 4
    k, step = (r // STEPS) % planes, r % STEPS
    order = one_hot((k * SPAN + 2 * q + (c ^ core)) * STEPS + step, rows)
    act = pick(order, act).astype(BF)
    routes = pick(order, routes_ref[...])
    scores = routes[:, TOPK : 2 * TOPK] + routes[:, 2 * TOPK : 3 * TOPK]
    chosen = jnp.where(routes[:, :TOPK] == expert.astype(F32), scores, 0.0)
    coef = jnp.sum(chosen, axis=1, keepdims=True) / jnp.sum(scores, axis=1, keepdims=True) * 2.5
    for p in range(SPAN):
        out = jnp.dot(act, down_ref[:, p * part : (p + 1) * part], preferred_element_type=F32) * coef
        near_ref[:, p * part : (p + 1) * part] = out[: rows // 2].astype(BF)
        far_ref[:, p * part : (p + 1) * part] = out[rows // 2 :].astype(BF)


def single(kernel, n, out_shape, scalars, arrays, name, flops):
    return pl.pallas_call(
        functools.partial(kernel, n),
        in_specs=[pl.BlockSpec(memory_space=pltpu.SMEM)] * len(scalars)
        + [pl.BlockSpec(memory_space=pltpu.VMEM)] * len(arrays),
        out_shape=out_shape,
        compiler_params=pltpu.CompilerParams(vmem_limit_bytes=VMEM_LIMIT),
        cost_estimate=pl.CostEstimate(
            flops=flops, bytes_accessed=sum(2 * a.size for a in arrays), transcendentals=0
        ),
        name=name,
    )(*scalars, *arrays)


def per_device(
    queries,
    new_latent,
    cache_latent,
    cache_len,
    route_ids,
    route_scores,
    residual,
    norm_gain,
    w_uv,
    w_out,
    w_gate,
    w_up,
    w_down,
):
    n_ep = lax.axis_size("ep")
    n = lax.axis_size("sec") * n_ep
    planes = n // SPAN
    heads = queries.shape[2]
    width = residual.shape[2]
    part = width // SPAN
    rows = n * STEPS
    me = lax.axis_index(AXES).astype(jnp.int32)
    everyone, planes_of, lines, chips = None, plane_groups(n), line_groups(n), chip_groups(n)

    with jax.named_scope("share_weights"):
        high = route_scores[0].astype(BF)
        low = (route_scores[0] - high.astype(F32)).astype(BF)
        routes = jnp.concatenate([route_ids[0].astype(BF), high, low], axis=1)
        routes = jnp.pad(routes, ((0, 0), (0, part - 3 * TOPK)))
        by_part = jnp.concatenate(
            [
                w_out[0].reshape(VDIM, SPAN, part),
                residual[0].reshape(STEPS, SPAN, part),
                jnp.broadcast_to(routes[:, None], (STEPS, SPAN, part)),
                jnp.zeros((16 - 2 * STEPS, SPAN, part), BF),
            ],
            axis=0,
        )
        shared = exchange(jnp.swapaxes(by_part, 0, 1), planes_of)

    with jax.named_scope("attention"):
        latents = attend(
            n,
            cache_len,
            queries[0].reshape(STEPS * heads, queries.shape[3]),
            new_latent[0],
            jnp.swapaxes(cache_latent[0], 0, 1),
        )

    with jax.named_scope("to_heads"):
        latents = exchange(latents.reshape(n, STEPS, LAT), everyone)
        values = single(
            values_kernel,
            n,
            jax.ShapeDtypeStruct((SPAN, rows, VDIM), BF),
            [],
            [latents.reshape(rows, LAT), w_uv[0]],
            "head_values",
            2 * rows * LAT * VDIM,
        )
        values = exchange(values, planes_of)

    with jax.named_scope("project"):
        parts = single(
            project_kernel,
            n,
            jax.ShapeDtypeStruct((planes, SPAN * STEPS, part), BF),
            [],
            [values, shared],
            "project",
            2 * rows * SPAN * VDIM * part,
        )
        parts = exchange(parts, lines)
        own = shared[:, VDIM : VDIM + STEPS].reshape(SPAN * STEPS, part)
        hidden = (jnp.sum(parts.astype(F32), axis=0) + own.astype(F32)).astype(BF)
        routes = shared[:, VDIM + STEPS : VDIM + 2 * STEPS, :128].reshape(SPAN * STEPS, 128)

    with jax.named_scope("spread_hidden"):
        along = jnp.concatenate([hidden, routes], axis=1)
        along = exchange(jnp.broadcast_to(along[None], (planes,) + along.shape), lines)
        along = along.reshape(rows, part + 128)
        routes = along[:, part:]
        here = exchange(jnp.broadcast_to(along[None, :, :part], (4, rows, part)), chips)
        there = swap_core(here, n)

    with jax.named_scope("experts"):
        near, far = single(
            expert_kernel,
            n,
            [jax.ShapeDtypeStruct((rows // 2, width), BF)] * 2,
            [jnp.stack([me, me % n_ep])],
            [here, there, norm_gain.reshape(1, width), routes, w_gate[0], w_up[0], w_down[0]],
            "experts",
            6 * rows * width * w_gate.shape[2],
        )

    with jax.named_scope("own_hidden"):
        core = me % 2
        plane, place = (me // 4) % planes, (me // (n // 2)) * 4 + me % 4
        start = (plane * SPAN + place) * STEPS
        own = [lax.dynamic_slice_in_dim(x, start, STEPS, axis=1) for x in (here, there)]
        own = [jnp.where(core == c, own[0], own[1]) for c in range(2)]
        own = jnp.stack(own, axis=1).reshape(SPAN, STEPS, part)
        own = jnp.swapaxes(own, 0, 1).reshape(STEPS, width)

    with jax.named_scope("collect"):
        total = (near.astype(F32) + swap_core(far, n).astype(F32)).astype(BF)
        total = exchange(total.reshape(4, planes * STEPS, width), chips)
        total = jnp.sum(total.astype(F32), axis=0).astype(BF)
        total = exchange(total.reshape(planes, STEPS, width), lines)
        result = jnp.sum(total.astype(F32), axis=0) + own.astype(F32)
        return result.astype(BF)[None]


def solution(mesh):
    placed = (
        P(("sec", "ep"), None, None, None),
        P(("sec", "ep"), None, None),
        P(("sec", "ep"), None, None),
        P(("sec", "ep")),
        P(("sec", "ep"), None, None),
        P(("sec", "ep"), None, None),
        P(("sec", "ep"), None, None),
        P(),
        P(("sec", "ep"), None, None),
        P(("sec", "ep"), None, None),
        P("ep", None, "sec"),
        P("ep", None, "sec"),
        P("ep", "sec", None),
    )
    return jax.shard_map(
        per_device,
        mesh=mesh,
        in_specs=placed,
        out_specs=P(("sec", "ep"), None, None),
        check_vma=False,
    )
```

```python
import functools
import math

import jax
import jax.numpy as jnp
from jax import lax
from jax.experimental import pallas as pl
from jax.experimental.pallas import tpu as pltpu
from jax.sharding import PartitionSpec as P

LAT = 512
ROPE = 64
VDIM = 128
STEPS = 4
TOPK = 8
BLK = 2048
SPAN = 8
AXES = ("sec", "ep")
NT = (((1,), (1,)), ((), ()))
BF = jnp.bfloat16
F32 = jnp.float32
VMEM_LIMIT = 16 * 1024 * 1024


def mask_of(n, q=0, c=0, k=0):
    return (q >> 1) * (n // 2) + k * 4 + (q & 1) * 2 + c


def swap(x, n, **differ):
    mask = mask_of(n, **differ)
    return lax.ppermute(x, AXES, [(d, d ^ mask) for d in range(n)])


def iota2(shape, axis):
    return lax.broadcasted_iota(jnp.int32, shape, axis)


def one_hot(columns, count):
    return (iota2(columns.shape, 1) == columns).astype(BF)


def pick(matrix, rows):
    return jnp.dot(matrix, rows, preferred_element_type=F32)


def attend_kernel(n, len_ref, q_ref, new_ref, keys_ref, out_ref, m_ref, l_ref, acc_ref):
    rows = q_ref.shape[0]
    heads = rows // STEPS
    factor_base2 = (VDIM + ROPE) ** (-0.5) * math.log2(math.e)
    i = pl.program_id(0)
    length = len_ref[0]
    blk = keys_ref.shape[1]

    @pl.when(i == 0)
    def _():
        new = new_ref[...]
        s = lax.dot_general(q_ref[...], new, NT, preferred_element_type=F32)
        step = iota2(s.shape, 0) // heads
        s = jnp.where(iota2(s.shape, 1) <= step, s, -1e30)
        m = jnp.max(s, axis=1, keepdims=True)
        p = jnp.exp2((s - m) * factor_base2)
        m_ref[...] = m
        l_ref[...] = jnp.sum(p, axis=1, keepdims=True)
        acc_ref[...] = jnp.dot(p.astype(BF), new[:, :LAT], preferred_element_type=F32)

    def update(masked):
        keys = keys_ref[...]
        s = jnp.dot(q_ref[...], keys, preferred_element_type=F32)
        if masked:
            s = jnp.where(iota2(s.shape, 1) < length - i * blk, s, -1e30)
        m_old = m_ref[...]
        m = jnp.maximum(m_old, jnp.max(s, axis=1, keepdims=True))
        factor = jnp.exp2((m_old - m) * factor_base2)
        p = jnp.exp2((s - m) * factor_base2)
        m_ref[...] = m
        l_ref[...] = l_ref[...] * factor + jnp.sum(p, axis=1, keepdims=True)
        acc_ref[...] = acc_ref[...] * factor + lax.dot_general(
            p.astype(BF), keys[:LAT], NT, preferred_element_type=F32
        )

    pl.when((i + 1) * blk <= length)(functools.partial(update, False))
    pl.when((i * blk < length) & ((i + 1) * blk > length))(functools.partial(update, True))

    @pl.when(i == pl.num_programs(0) - 1)
    def _():
        out = (acc_ref[...] / l_ref[...]).astype(BF)
        r = iota2((rows, rows), 0)
        moved = pick(one_hot((r % STEPS) * heads + r // STEPS, rows), out)
        out_ref[...] = moved.reshape(out_ref.shape).astype(BF)


def attend(n, length, q, new, keys):
    rows, width = q.shape
    cached = keys.shape[1]
    blk = min(BLK, cached)

    def block(i, len_ref):
        return (0, jnp.minimum(i, (len_ref[0] - 1) // blk))

    def whole(i, len_ref):
        return (0, 0)

    return pl.pallas_call(
        functools.partial(attend_kernel, n),
        grid_spec=pltpu.PrefetchScalarGridSpec(
            num_scalar_prefetch=1,
            grid=(cached // blk,),
            in_specs=[
                pl.BlockSpec(q.shape, whole),
                pl.BlockSpec(new.shape, whole),
                pl.BlockSpec((width, blk), block),
            ],
            out_specs=pl.BlockSpec((rows // STEPS, STEPS, LAT), lambda i, len_ref: (0, 0, 0)),
            scratch_shapes=[
                pltpu.VMEM((rows, 1), F32),
                pltpu.VMEM((rows, 1), F32),
                pltpu.VMEM((rows, LAT), F32),
            ],
        ),
        out_shape=jax.ShapeDtypeStruct((rows // STEPS, STEPS, LAT), BF),
        compiler_params=pltpu.CompilerParams(vmem_limit_bytes=56 * 1024 * 1024),
        cost_estimate=pl.CostEstimate(
            flops=2 * rows * cached * (width + LAT),
            bytes_accessed=2 * cached * width,
            transcendentals=rows * cached,
        ),
        name="attend",
    )(length, q, new, keys)


def values_kernel(n, latents_ref, uv_ref, *refs):
    out_ref = refs[-1]
    out_ref[...] = jnp.dot(latents_ref[...], uv_ref[...], preferred_element_type=F32).astype(BF)


def project_kernel(n, me_ref, *refs):
    values, weights, (keep_ref, give_ref, total_ref) = refs[:4], refs[4:8], refs[8:]
    planes = n // SPAN
    rows = n * STEPS
    group = 4 * STEPS
    me = me_ref[0]
    core, plane = me % 2, (me // 4) % planes
    part = keep_ref.shape[1]
    carried = jnp.concatenate([weights[q][VDIM:] for q in range(4)], axis=0)
    extra = carried.shape[0] // 4
    r = iota2((rows, 4 * extra), 0)
    differ = (r // STEPS) ^ me
    q = (differ // (n // 2)) * 2 + (differ // 2) % 2
    same = (differ % 2 == 0) & ((differ // 4) % planes == 0)
    total = pick(one_hot(jnp.where(same, q * extra + r % STEPS, -1), 4 * extra), carried)
    for q in range(4):
        total += jnp.dot(values[q][...], weights[q][:VDIM], preferred_element_type=F32)
    total_ref[...] = total
    for k in range(planes):
        for top in range(2):
            start = pl.multiple_of((top * planes + (plane ^ k)) * group, group)
            block = total_ref[pl.ds(start, group)]
            here = pl.ds((2 * k + top) * group, group)
            keep_ref[here] = jnp.where(core == 0, block[:, :part], block[:, part:])
            give_ref[here] = jnp.where(core == 0, block[:, part:], block[:, :part]).astype(BF)


def expert_kernel(n, me_ref, *refs):
    blocks, refs = refs[:8], refs[8:]
    gain_ref, gate_hbm, up_hbm, down_hbm, near_ref, far_ref, own_ref = refs[:7]
    gate_ref, up_ref, down_ref, gate_sem, up_sem, down_sem = refs[7:]
    planes = n // SPAN
    rows = n * STEPS
    me = me_ref[0]
    core, chip = me % 2, (me // (n // 2)) * 2 + (me // 2) % 2
    place = chip * 2 + core
    expert = me_ref[1]
    width = gate_ref.shape[0]
    part = width // SPAN

    starts = [
        pl.multiple_of(((chip ^ (i % 4)) * 2 + (core ^ (i // 4))) * part, part) for i in range(SPAN)
    ]
    copies = []
    for i in range(SPAN):
        here = pl.ds(starts[i], part)
        copies.append(
            (
                pltpu.make_async_copy(gate_hbm.at[here], gate_ref.at[here], gate_sem.at[i]),
                pltpu.make_async_copy(up_hbm.at[here], up_ref.at[here], up_sem.at[i]),
            )
        )
    downs = []
    for i in range(SPAN):
        here = (slice(None), pl.ds(i * part, part))
        downs.append(
            pltpu.make_async_copy(down_hbm.at[here], down_ref.at[here], down_sem.at[i])
        )
    for pair in copies:
        for copy in pair:
            copy.start()
    for copy in downs:
        copy.start()

    gate = jnp.zeros((rows, gate_ref.shape[1]), F32)
    up = jnp.zeros((rows, up_ref.shape[1]), F32)
    square = jnp.zeros((rows, 1), F32)
    r = iota2((own_ref.shape[0], rows), 0)
    mine = one_hot(jnp.where(r < STEPS, place * STEPS + r, -1), rows)
    for i in range(SPAN):
        here = pl.ds(starts[i], part)
        raw = blocks[i][:, :part]
        x = raw.astype(F32)
        square += jnp.sum(x * x, axis=1, keepdims=True)
        scaled = (x * gain_ref[:, here].astype(F32)).astype(BF)
        own_ref[:, here] = pick(mine, raw).astype(BF)
        copies[i][0].wait()
        gate += jnp.dot(scaled, gate_ref[here], preferred_element_type=F32)
        copies[i][1].wait()
        up += jnp.dot(scaled, up_ref[here], preferred_element_type=F32)
    norm = lax.rsqrt(square / width + 1e-06)
    gate = gate * norm
    act = (gate * jax.nn.sigmoid(gate) * (up * norm)).astype(BF)
    r = iota2((rows, rows), 0)
    c, q = r // (rows // 2), (r // (planes * STEPS)) % 4
    k, step = (r // STEPS) % planes, r % STEPS
    order = one_hot((k * SPAN + (place ^ (2 * q + c))) * STEPS + step, rows)
    act = pick(order, act).astype(BF)
    routes = pick(order, blocks[0][:, part:] + blocks[4][:, part:])
    scores = routes[:, TOPK : 2 * TOPK] + routes[:, 2 * TOPK : 3 * TOPK]
    chosen = jnp.where(routes[:, :TOPK] == expert.astype(F32), scores, 0.0)
    coef = jnp.sum(chosen, axis=1, keepdims=True) / jnp.sum(scores, axis=1, keepdims=True) * 2.5
    for p in range(SPAN):
        here = slice(p * part, (p + 1) * part)
        downs[p].wait()
        out = jnp.dot(act, down_ref[:, here], preferred_element_type=F32) * coef
        near_ref[:, here] = out[: rows // 2].astype(BF)
        far_ref[:, here] = out[rows // 2 :].astype(BF)


def run_experts(n, scalars, blocks, gain, w_gate, w_up, w_down):
    rows = n * STEPS
    width, units = w_gate.shape
    half = jax.ShapeDtypeStruct((rows // 2, width), BF)
    return pl.pallas_call(
        functools.partial(expert_kernel, n),
        in_specs=[pl.BlockSpec(memory_space=pltpu.SMEM)]
        + [pl.BlockSpec(memory_space=pltpu.VMEM)] * (len(blocks) + 1)
        + [pl.BlockSpec(memory_space=pl.ANY)] * 3,
        out_shape=[half, half, jax.ShapeDtypeStruct((16, width), BF)],
        scratch_shapes=[
            pltpu.VMEM((width, units), BF),
            pltpu.VMEM((width, units), BF),
            pltpu.VMEM((units, width), BF),
            pltpu.SemaphoreType.DMA((SPAN,)),
            pltpu.SemaphoreType.DMA((SPAN,)),
            pltpu.SemaphoreType.DMA((SPAN,)),
        ],
        compiler_params=pltpu.CompilerParams(vmem_limit_bytes=36 * 1024 * 1024),
        cost_estimate=pl.CostEstimate(
            flops=6 * rows * width * units,
            bytes_accessed=6 * width * units,
            transcendentals=rows * units,
        ),
        name="experts",
    )(scalars, *blocks, gain, w_gate, w_up, w_down)


def single(kernel, n, out_shape, scalars, arrays, name, flops, scratch=(), awaited=()):
    return pl.pallas_call(
        functools.partial(kernel, n),
        in_specs=[pl.BlockSpec(memory_space=pltpu.SMEM)] * len(scalars)
        + [pl.BlockSpec(memory_space=pltpu.VMEM)] * len(arrays)
        + [pl.BlockSpec(memory_space=pl.ANY)] * len(awaited),
        out_shape=out_shape,
        scratch_shapes=scratch,
        compiler_params=pltpu.CompilerParams(vmem_limit_bytes=VMEM_LIMIT),
        cost_estimate=pl.CostEstimate(
            flops=flops, bytes_accessed=sum(2 * a.size for a in arrays), transcendentals=0
        ),
        name=name,
    )(*scalars, *arrays, *awaited)


def per_device(
    queries,
    new_latent,
    cache_latent,
    cache_len,
    route_ids,
    route_scores,
    residual,
    norm_gain,
    w_uv,
    w_out,
    w_gate,
    w_up,
    w_down,
):
    n_ep = lax.axis_size("ep")
    n = lax.axis_size("sec") * n_ep
    planes = n // SPAN
    heads = queries.shape[2]
    width = residual.shape[2]
    part = width // SPAN
    rows = n * STEPS
    me = lax.axis_index(AXES).astype(jnp.int32)
    scalars = jnp.stack([me, me % n_ep])
    chip = (me // (n // 2)) * 2 + (me // 2) % 2

    with jax.named_scope("share_weights"):
        high = route_scores[0].astype(BF)
        low = (route_scores[0] - high.astype(F32)).astype(BF)
        routes = jnp.concatenate([route_ids[0].astype(BF), high, low], axis=1)
        routes = jnp.pad(routes, ((0, 16 - 2 * STEPS), (0, 2 * part - 3 * TOPK)))
        weights = []
        for q in range(4):
            start = (chip ^ q) * 2 * part
            piece = jnp.concatenate(
                [
                    lax.dynamic_slice(w_out[0], (0, start), (VDIM, 2 * part)),
                    lax.dynamic_slice(residual[0], (0, start), (STEPS, 2 * part)),
                    routes,
                ],
                axis=0,
            )
            weights.append(piece if q == 0 else swap(piece, n, q=q))

    with jax.named_scope("attention"):
        latents = attend(
            n,
            cache_len,
            queries[0].reshape(STEPS * heads, queries.shape[3]),
            new_latent[0],
            jnp.swapaxes(cache_latent[0], 0, 1),
        )

    with jax.named_scope("to_heads"):
        latents = lax.all_to_all(latents, AXES, 0, 0, tiled=True)
        values = single(
            values_kernel,
            n,
            jax.ShapeDtypeStruct((rows, VDIM), BF),
            [],
            [latents.reshape(rows, LAT), w_uv[0]],
            "head_values",
            2 * rows * LAT * VDIM,
            awaited=weights[1:],
        )
        values = [values] + [swap(values, n, q=q) for q in range(1, 4)]

    with jax.named_scope("project"):
        keep, give = single(
            project_kernel,
            n,
            [jax.ShapeDtypeStruct((rows, part), F32), jax.ShapeDtypeStruct((rows, part), BF)],
            [scalars],
            values + weights,
            "project",
            4 * rows * 4 * VDIM * part,
            [pltpu.VMEM((rows, 2 * part), F32)],
        )
        total = keep + swap(give, n, c=1).astype(F32)
        total = total.reshape(planes, SPAN * STEPS, part)
        hidden = total[0]
        for k in range(1, planes):
            hidden = hidden + swap(total[k].astype(BF), n, k=k).astype(F32)
        hidden = hidden.astype(BF)

    with jax.named_scope("spread_hidden"):
        routes = jnp.stack([w[VDIM + STEPS : VDIM + 2 * STEPS, :128] for w in weights])
        routes = routes[chip ^ jnp.arange(4)]
        routes = jnp.stack([jnp.where(me % 2 == c, routes, 0) for c in range(2)], axis=1)
        along = jnp.concatenate([hidden, routes.reshape(SPAN * STEPS, 128)], axis=1)
        along = jnp.concatenate([along] + [swap(along, n, k=k) for k in range(1, planes)], axis=0)
        blocks = [along] + [swap(along[:, :part], n, q=q) for q in range(1, 4)]
        blocks = blocks + [swap(x, n, c=1) for x in blocks]

    with jax.named_scope("experts"):
        near, far, own = run_experts(
            n, scalars, blocks, norm_gain.reshape(1, width), w_gate[0], w_up[0], w_down[0]
        )

    with jax.named_scope("collect"):
        total = near.astype(F32) + swap(far, n, c=1).astype(F32)
        total = total.reshape(4, planes * STEPS, width)
        kept = total[0]
        for q in range(1, 4):
            kept = kept + swap(total[q].astype(BF), n, q=q).astype(F32)
        kept = kept.reshape(planes, STEPS, width)
        result = kept[0] + own[:STEPS].astype(F32)
        for k in range(1, planes):
            result = result + swap(kept[k].astype(BF), n, k=k).astype(F32)
        return result.astype(BF)[None]


def solution(mesh):
    placed = (
        P(("sec", "ep"), None, None, None),
        P(("sec", "ep"), None, None),
        P(("sec", "ep"), None, None),
        P(("sec", "ep")),
        P(("sec", "ep"), None, None),
        P(("sec", "ep"), None, None),
        P(("sec", "ep"), None, None),
        P(),
        P(("sec", "ep"), None, None),
        P(("sec", "ep"), None, None),
        P("ep", None, "sec"),
        P("ep", None, "sec"),
        P("ep", "sec", None),
    )
    return jax.shard_map(
        per_device,
        mesh=mesh,
        in_specs=placed,
        out_specs=P(("sec", "ep"), None, None),
        check_vma=False,
    )
```

```python
import functools
import math

import jax
import jax.numpy as jnp
from jax import lax
from jax.experimental import pallas as pl
from jax.experimental.pallas import tpu as pltpu
from jax.sharding import PartitionSpec as P

LAT = 512
ROPE = 64
VDIM = 128
STEPS = 4
TOPK = 8
BLK = 2048
SPAN = 8
AXES = ("sec", "ep")
NT = (((1,), (1,)), ((), ()))
BF = jnp.bfloat16
F32 = jnp.float32
VMEM_LIMIT = 16 * 1024 * 1024


def mask_of(n, q=0, c=0, k=0):
    return (q >> 1) * (n // 2) + k * 4 + (q & 1) * 2 + c


def swap(x, n, **differ):
    mask = mask_of(n, **differ)
    return lax.ppermute(x, AXES, [(d, d ^ mask) for d in range(n)])


def iota2(shape, axis):
    return lax.broadcasted_iota(jnp.int32, shape, axis)


def one_hot(columns, count):
    return (iota2(columns.shape, 1) == columns).astype(BF)


def pick(matrix, rows):
    return jnp.dot(matrix, rows, preferred_element_type=F32)


def attend_kernel(n, len_ref, q_ref, new_ref, keys_ref, out_ref, m_ref, l_ref, acc_ref):
    rows = q_ref.shape[0]
    heads = rows // STEPS
    factor_base2 = (VDIM + ROPE) ** (-0.5) * math.log2(math.e)
    i = pl.program_id(0)
    length = len_ref[0]
    blk = keys_ref.shape[1]

    @pl.when(i == 0)
    def _():
        new = new_ref[...]
        s = lax.dot_general(q_ref[...], new, NT, preferred_element_type=F32)
        step = iota2(s.shape, 0) // heads
        s = jnp.where(iota2(s.shape, 1) <= step, s, -1e30)
        m = jnp.max(s, axis=1, keepdims=True)
        p = jnp.exp2((s - m) * factor_base2)
        m_ref[...] = m
        l_ref[...] = jnp.sum(p, axis=1, keepdims=True)
        acc_ref[...] = jnp.dot(p.astype(BF), new[:, :LAT], preferred_element_type=F32)

    def update(masked):
        keys = keys_ref[...]
        s = jnp.dot(q_ref[...], keys, preferred_element_type=F32)
        if masked:
            s = jnp.where(iota2(s.shape, 1) < length - i * blk, s, -1e30)
        m_old = m_ref[...]
        m = jnp.maximum(m_old, jnp.max(s, axis=1, keepdims=True))
        factor = jnp.exp2((m_old - m) * factor_base2)
        p = jnp.exp2((s - m) * factor_base2)
        m_ref[...] = m
        l_ref[...] = l_ref[...] * factor + jnp.sum(p, axis=1, keepdims=True)
        acc_ref[...] = acc_ref[...] * factor + lax.dot_general(
            p.astype(BF), keys[:LAT], NT, preferred_element_type=F32
        )

    pl.when((i + 1) * blk <= length)(functools.partial(update, False))
    pl.when((i * blk < length) & ((i + 1) * blk > length))(functools.partial(update, True))

    @pl.when(i == pl.num_programs(0) - 1)
    def _():
        out = (acc_ref[...] / l_ref[...]).astype(BF)
        r = iota2((rows, rows), 0)
        moved = pick(one_hot((r % STEPS) * heads + r // STEPS, rows), out)
        out_ref[...] = moved.reshape(out_ref.shape).astype(BF)


def attend(n, length, q, new, keys):
    rows, width = q.shape
    cached = keys.shape[1]
    blk = min(BLK, cached)

    def block(i, len_ref):
        return (0, jnp.minimum(i, (len_ref[0] - 1) // blk))

    def whole(i, len_ref):
        return (0, 0)

    return pl.pallas_call(
        functools.partial(attend_kernel, n),
        grid_spec=pltpu.PrefetchScalarGridSpec(
            num_scalar_prefetch=1,
            grid=(cached // blk,),
            in_specs=[
                pl.BlockSpec(q.shape, whole),
                pl.BlockSpec(new.shape, whole),
                pl.BlockSpec((width, blk), block),
            ],
            out_specs=pl.BlockSpec((rows // STEPS, STEPS, LAT), lambda i, len_ref: (0, 0, 0)),
            scratch_shapes=[
                pltpu.VMEM((rows, 1), F32),
                pltpu.VMEM((rows, 1), F32),
                pltpu.VMEM((rows, LAT), F32),
            ],
        ),
        out_shape=jax.ShapeDtypeStruct((rows // STEPS, STEPS, LAT), BF),
        compiler_params=pltpu.CompilerParams(vmem_limit_bytes=56 * 1024 * 1024),
        cost_estimate=pl.CostEstimate(
            flops=2 * rows * cached * (width + LAT),
            bytes_accessed=2 * cached * width,
            transcendentals=rows * cached,
        ),
        name="attend",
    )(length, q, new, keys)


def partner_order(n, me, rows):
    planes = n // SPAN
    r = iota2((rows, rows), 0)
    c, q = r // (rows // 2), (r // (planes * STEPS)) % 4
    k, step = (r // STEPS) % planes, r % STEPS
    return me ^ ((q >> 1) * (n // 2) + k * 4 + (q & 1) * 2 + c), step


def heads_kernel(n, me_ref, latents_ref, uv_ref, out_ref, near_ref, far_ref):
    rows = n * STEPS
    values = jnp.dot(latents_ref[...], uv_ref[...], preferred_element_type=F32).astype(BF)
    device, step = partner_order(n, me_ref[0], rows)
    values = pick(one_hot(device * STEPS + step, rows), values).astype(BF)
    part = out_ref.shape[1] // SPAN
    for p in range(SPAN):
        here = slice(p * part, (p + 1) * part)
        out = jnp.dot(values, out_ref[:, here], preferred_element_type=F32)
        near_ref[:, here] = out[: rows // 2]
        far_ref[:, here] = out[rows // 2 :].astype(BF)


def norm_kernel(n, *refs):
    parts, (residual_ref, gain_ref, routes_ref, hidden_ref, out_ref) = refs[:-5], refs[-5:]
    hidden = residual_ref[...].astype(F32)
    for ref in parts:
        hidden += ref[...].astype(F32)
    hidden_ref[...] = hidden
    width = hidden.shape[1]
    mean_square = jnp.sum(hidden * hidden, axis=1, keepdims=True) / width
    normed = hidden * lax.rsqrt(mean_square + 1e-06) * gain_ref[...].astype(F32)
    out_ref[:, :width] = normed.astype(BF)
    out_ref[:, width:] = routes_ref[...]


def load_kernel(n, *refs):
    sources, targets, sem = refs[1:4], refs[5:8], refs[8]
    copies = [pltpu.make_async_copy(refs[0], refs[4], sem.at[12])]
    for i in range(3):
        step = sources[i].shape[0] // 4
        for j in range(4):
            here = pl.ds(j * step, step)
            copies.append(
                pltpu.make_async_copy(sources[i].at[here], targets[i].at[here], sem.at[4 * i + j])
            )
    for copy in copies:
        copy.start()
    for copy in copies:
        copy.wait()


def load(n, passed, arrays):
    return pl.pallas_call(
        functools.partial(load_kernel, n),
        in_specs=[pl.BlockSpec(memory_space=pltpu.VMEM)] + [pl.BlockSpec(memory_space=pl.ANY)] * 3,
        out_specs=[pl.BlockSpec(memory_space=pltpu.VMEM)] * 4,
        out_shape=[jax.ShapeDtypeStruct(a.shape, a.dtype) for a in [passed] + arrays],
        scratch_shapes=[pltpu.SemaphoreType.DMA((13,))],
        compiler_params=pltpu.CompilerParams(vmem_limit_bytes=26 * 1024 * 1024),
        cost_estimate=pl.CostEstimate(
            flops=0, bytes_accessed=sum(4 * a.size for a in arrays), transcendentals=0
        ),
        name="load_experts",
    )(passed, *arrays)


def expert_kernel(n, expert_ref, *refs):
    blocks, (gate_ref, up_ref, down_ref, near_ref, far_ref) = refs[:8], refs[8:]
    rows = n * STEPS
    width, units = gate_ref.shape
    part = width // SPAN
    gate = jnp.zeros((rows, units), F32)
    up = jnp.zeros((rows, units), F32)
    for p in range(SPAN):
        here = slice(p * part, (p + 1) * part)
        x = jnp.concatenate([ref[:, here] for ref in blocks], axis=0)
        gate += jnp.dot(x, gate_ref[here], preferred_element_type=F32)
        up += jnp.dot(x, up_ref[here], preferred_element_type=F32)
    act = (gate * jax.nn.sigmoid(gate) * up).astype(BF)
    routes = jnp.concatenate([ref[:, width:] for ref in blocks], axis=0).astype(F32)
    scores = routes[:, TOPK : 2 * TOPK] + routes[:, 2 * TOPK : 3 * TOPK]
    chosen = jnp.where(routes[:, :TOPK] == expert_ref[0].astype(F32), scores, 0.0)
    coef = jnp.sum(chosen, axis=1, keepdims=True) / jnp.sum(scores, axis=1, keepdims=True) * 2.5
    for p in range(SPAN):
        here = slice(p * part, (p + 1) * part)
        out = jnp.dot(act, down_ref[:, here], preferred_element_type=F32) * coef
        near_ref[:, here] = out[: rows // 2]
        far_ref[:, here] = out[rows // 2 :].astype(BF)


def single(kernel, n, out_shape, scalars, arrays, name, flops):
    return pl.pallas_call(
        functools.partial(kernel, n),
        in_specs=[pl.BlockSpec(memory_space=pltpu.SMEM)] * len(scalars)
        + [pl.BlockSpec(memory_space=pltpu.VMEM)] * len(arrays),
        out_shape=out_shape,
        compiler_params=pltpu.CompilerParams(vmem_limit_bytes=VMEM_LIMIT),
        cost_estimate=pl.CostEstimate(
            flops=flops, bytes_accessed=sum(2 * a.size for a in arrays), transcendentals=0
        ),
        name=name,
    )(*scalars, *arrays)


def reduce_rows(near, far, n):
    planes = n // SPAN
    width = near.shape[1]
    total = (near + swap(far, n, c=1).astype(F32)).reshape(4, planes * STEPS, width)
    kept = total[0]
    for q in range(1, 4):
        kept = kept + swap(total[q].astype(BF), n, q=q).astype(F32)
    kept = kept.reshape(planes, STEPS, width)
    return [kept[0]] + [swap(kept[k].astype(BF), n, k=k) for k in range(1, planes)]


def per_device(
    queries,
    new_latent,
    cache_latent,
    cache_len,
    route_ids,
    route_scores,
    residual,
    norm_gain,
    w_uv,
    w_out,
    w_gate,
    w_up,
    w_down,
):
    n_ep = lax.axis_size("ep")
    n = lax.axis_size("sec") * n_ep
    planes = n // SPAN
    heads = queries.shape[2]
    width = residual.shape[2]
    rows = n * STEPS
    me = lax.axis_index(AXES).astype(jnp.int32)

    with jax.named_scope("attention"):
        latents = attend(
            n,
            cache_len,
            queries[0].reshape(STEPS * heads, queries.shape[3]),
            new_latent[0],
            jnp.swapaxes(cache_latent[0], 0, 1),
        )

    with jax.named_scope("heads"):
        latents = lax.all_to_all(latents, AXES, 0, 0, tiled=True)
        near, far = single(
            heads_kernel,
            n,
            [jax.ShapeDtypeStruct((rows // 2, width), dtype) for dtype in (F32, BF)],
            [me.reshape(1)],
            [latents.reshape(rows, LAT), w_uv[0], w_out[0]],
            "heads",
            2 * rows * VDIM * (LAT + width),
        )
        parts = reduce_rows(near, far, n)

    with jax.named_scope("norm"):
        high = route_scores[0].astype(BF)
        low = (route_scores[0] - high.astype(F32)).astype(BF)
        routes = jnp.concatenate([route_ids[0].astype(BF), high, low], axis=1)
        routes = jnp.pad(routes, ((0, 0), (0, 128 - 3 * TOPK)))
        hidden, normed = single(
            norm_kernel,
            n,
            [
                jax.ShapeDtypeStruct((STEPS, width), F32),
                jax.ShapeDtypeStruct((STEPS, width + 128), BF),
            ],
            [],
            parts + [residual[0], norm_gain.reshape(1, width), routes],
            "norm",
            8 * STEPS * width,
        )

    with jax.named_scope("spread"):
        along = jnp.concatenate([normed] + [swap(normed, n, k=k) for k in range(1, planes)], axis=0)
        blocks = [along] + [swap(along, n, q=q) for q in range(1, 4)]
        along, *weights = load(n, along, [w_gate[0], w_up[0], w_down[0]])
        blocks = blocks + [swap(x, n, c=1) for x in [along] + blocks[1:]]

    with jax.named_scope("experts"):
        near, far = single(
            expert_kernel,
            n,
            [jax.ShapeDtypeStruct((rows // 2, width), dtype) for dtype in (F32, BF)],
            [(me % n_ep).reshape(1)],
            blocks + weights,
            "experts",
            6 * rows * width * w_gate.shape[2],
        )

    with jax.named_scope("collect"):
        result = hidden
        for term in reduce_rows(near, far, n):
            result = result + term.astype(F32)
        return result.astype(BF)[None]


def solution(mesh):
    placed = (
        P(("sec", "ep"), None, None, None),
        P(("sec", "ep"), None, None),
        P(("sec", "ep"), None, None),
        P(("sec", "ep")),
        P(("sec", "ep"), None, None),
        P(("sec", "ep"), None, None),
        P(("sec", "ep"), None, None),
        P(),
        P(("sec", "ep"), None, None),
        P(("sec", "ep"), None, None),
        P("ep", None, "sec"),
        P("ep", None, "sec"),
        P("ep", "sec", None),
    )
    return jax.shard_map(
        per_device,
        mesh=mesh,
        in_specs=placed,
        out_specs=P(("sec", "ep"), None, None),
        check_vma=False,
    )
```

```python
import functools
import math

import jax
import jax.numpy as jnp
from jax import lax
from jax.experimental import pallas as pl
from jax.experimental.pallas import tpu as pltpu
from jax.sharding import PartitionSpec as P

LAT = 512
ROPE = 64
VDIM = 128
STEPS = 4
TOPK = 8
BLK = 2048
SPAN = 8
AXES = ("sec", "ep")
NT = (((1,), (1,)), ((), ()))
BF = jnp.bfloat16
F32 = jnp.float32
VMEM_LIMIT = 16 * 1024 * 1024


def mask_of(n, q=0, c=0, k=0):
    return (q >> 1) * (n // 2) + k * 4 + (q & 1) * 2 + c


def swap(x, n, **differ):
    mask = mask_of(n, **differ)
    return lax.ppermute(x, AXES, [(d, d ^ mask) for d in range(n)])


def iota2(shape, axis):
    return lax.broadcasted_iota(jnp.int32, shape, axis)


def one_hot(columns, count):
    return (iota2(columns.shape, 1) == columns).astype(BF)


def pick(matrix, rows):
    return jnp.dot(matrix, rows, preferred_element_type=F32)


def attend_kernel(n, len_ref, q_hbm, new_hbm, keys_hbm, out_ref, q_ref, new_ref, keys_ref, m_ref, l_ref, acc_ref, small_sem, sem):
    rows = q_ref.shape[0]
    heads = rows // STEPS
    factor_base2 = (VDIM + ROPE) ** (-0.5) * math.log2(math.e)
    length = len_ref[0]
    blk = min(BLK, keys_ref.shape[1])

    def block_at(i):
        return pl.ds(pl.multiple_of(i * blk, blk), blk)

    def block_copy(i):
        return pltpu.make_async_copy(
            keys_hbm.at[:, block_at(i)], keys_ref.at[:, block_at(i)], sem.at[i]
        )

    def start(i):
        @pl.when(i * blk < length)
        def _():
            block_copy(i).start()

    q_copy = pltpu.make_async_copy(q_hbm, q_ref, small_sem.at[0])
    new_copy = pltpu.make_async_copy(new_hbm, new_ref, small_sem.at[1])
    q_copy.start()
    new_copy.start()
    start(0)
    start(1)
    r = iota2((rows, rows), 0)
    order = one_hot((r % STEPS) * heads + r // STEPS, rows)
    q_copy.wait()
    new_copy.wait()

    new = new_ref[...]
    s = lax.dot_general(q_ref[...], new, NT, preferred_element_type=F32)
    step = iota2(s.shape, 0) // heads
    s = jnp.where(iota2(s.shape, 1) <= step, s, -1e30)
    m = jnp.max(s, axis=1, keepdims=True)
    p = jnp.exp2((s - m) * factor_base2)
    m_ref[...] = m
    l_ref[...] = jnp.sum(p, axis=1, keepdims=True)
    acc_ref[...] = jnp.dot(p.astype(BF), new[:, :LAT], preferred_element_type=F32)

    def update(i, masked):
        start(i + 2)
        block_copy(i).wait()
        keys = keys_ref[:, block_at(i)]
        s = jnp.dot(q_ref[...], keys, preferred_element_type=F32)
        if masked:
            s = jnp.where(iota2(s.shape, 1) < length - i * blk, s, -1e30)
        m_old = m_ref[...]
        m = jnp.maximum(m_old, jnp.max(s, axis=1, keepdims=True))
        factor = jnp.exp2((m_old - m) * factor_base2)
        p = jnp.exp2((s - m) * factor_base2)
        m_ref[...] = m
        l_ref[...] = l_ref[...] * factor + jnp.sum(p, axis=1, keepdims=True)
        acc_ref[...] = acc_ref[...] * factor + lax.dot_general(
            p.astype(BF), keys[:LAT], NT, preferred_element_type=F32
        )

    full = length // blk

    @pl.loop(0, full)
    def _(i):
        update(i, False)

    @pl.when(full * blk < length)
    def _():
        update(full, True)

    out = (acc_ref[...] / l_ref[...]).astype(BF)
    out_ref[...] = pick(order, out).reshape(out_ref.shape).astype(BF)


def attend(n, length, q, new, keys):
    rows, width = q.shape
    cached = keys.shape[1]
    blocks = cached // min(BLK, cached)
    return pl.pallas_call(
        functools.partial(attend_kernel, n),
        in_specs=[pl.BlockSpec(memory_space=pltpu.SMEM)]
        + [pl.BlockSpec(memory_space=pl.ANY)] * 3,
        out_specs=pl.BlockSpec(memory_space=pltpu.VMEM),
        scratch_shapes=[
            pltpu.VMEM(q.shape, BF),
            pltpu.VMEM(new.shape, BF),
            pltpu.VMEM(keys.shape, BF),
            pltpu.VMEM((rows, 1), F32),
            pltpu.VMEM((rows, 1), F32),
            pltpu.VMEM((rows, LAT), F32),
            pltpu.SemaphoreType.DMA((2,)),
            pltpu.SemaphoreType.DMA((blocks,)),
        ],
        out_shape=jax.ShapeDtypeStruct((rows // STEPS, STEPS, LAT), BF),
        compiler_params=pltpu.CompilerParams(vmem_limit_bytes=56 * 1024 * 1024),
        cost_estimate=pl.CostEstimate(
            flops=2 * rows * cached * (width + LAT),
            bytes_accessed=2 * cached * width,
            transcendentals=rows * cached,
        ),
        name="attend",
    )(length, q, new, keys)


def partner_order(n, me, rows):
    planes = n // SPAN
    r = iota2((rows, rows), 0)
    c, q = r // (rows // 2), (r // (planes * STEPS)) % 4
    k, step = (r // STEPS) % planes, r % STEPS
    return me ^ ((q >> 1) * (n // 2) + k * 4 + (q & 1) * 2 + c), step


def heads_kernel(n, me_ref, latents_ref, uv_ref, out_ref, near_ref, far_ref):
    rows = n * STEPS
    values = jnp.dot(latents_ref[...], uv_ref[...], preferred_element_type=F32).astype(BF)
    device, step = partner_order(n, me_ref[0], rows)
    values = pick(one_hot(device * STEPS + step, rows), values).astype(BF)
    part = out_ref.shape[1] // SPAN
    for p in range(SPAN):
        here = slice(p * part, (p + 1) * part)
        out = jnp.dot(values, out_ref[:, here], preferred_element_type=F32)
        near_ref[:, here] = out[: rows // 2]
        far_ref[:, here] = out[rows // 2 :].astype(BF)


def norm_kernel(n, *refs):
    parts, (residual_ref, gain_ref, routes_ref, hidden_ref, out_ref) = refs[:-5], refs[-5:]
    hidden = residual_ref[...].astype(F32)
    for ref in parts:
        hidden += ref[...].astype(F32)
    hidden_ref[...] = hidden
    width = hidden.shape[1]
    mean_square = jnp.sum(hidden * hidden, axis=1, keepdims=True) / width
    normed = hidden * lax.rsqrt(mean_square + 1e-06) * gain_ref[...].astype(F32)
    out_ref[:, :width] = normed.astype(BF)
    out_ref[:, width:] = routes_ref[...]


def load_kernel(n, *refs):
    sources, targets, sem = refs[1:4], refs[5:8], refs[8]
    copies = [pltpu.make_async_copy(refs[0], refs[4], sem.at[12])]
    for i in range(3):
        step = sources[i].shape[0] // 4
        for j in range(4):
            here = pl.ds(j * step, step)
            copies.append(
                pltpu.make_async_copy(sources[i].at[here], targets[i].at[here], sem.at[4 * i + j])
            )
    for copy in copies:
        copy.start()
    for copy in copies:
        copy.wait()


def load(n, passed, arrays):
    return pl.pallas_call(
        functools.partial(load_kernel, n),
        in_specs=[pl.BlockSpec(memory_space=pltpu.VMEM)] + [pl.BlockSpec(memory_space=pl.ANY)] * 3,
        out_specs=[pl.BlockSpec(memory_space=pltpu.VMEM)] * 4,
        out_shape=[jax.ShapeDtypeStruct(a.shape, a.dtype) for a in [passed] + arrays],
        scratch_shapes=[pltpu.SemaphoreType.DMA((13,))],
        compiler_params=pltpu.CompilerParams(vmem_limit_bytes=36 * 1024 * 1024),
        cost_estimate=pl.CostEstimate(
            flops=0, bytes_accessed=sum(4 * a.size for a in arrays), transcendentals=0
        ),
        name="load_experts",
    )(passed, *arrays)


def expert_kernel(n, me_ref, *refs, n_ep):
    blocks, (gate_ref, up_ref, down_ref, near_ref, far_ref) = refs[:8], refs[8:]
    rows = n * STEPS
    width, units = gate_ref.shape
    part = width // SPAN
    gate = jnp.zeros((rows, units), F32)
    up = jnp.zeros((rows, units), F32)
    for p in range(SPAN):
        here = slice(p * part, (p + 1) * part)
        x = jnp.concatenate([ref[:, here] for ref in blocks], axis=0)
        gate += jnp.dot(x, gate_ref[here], preferred_element_type=F32)
        up += jnp.dot(x, up_ref[here], preferred_element_type=F32)
    act = (gate * jax.nn.sigmoid(gate) * up).astype(BF)
    routes = jnp.concatenate([ref[:, width:] for ref in blocks], axis=0).astype(F32)
    scores = routes[:, TOPK : 2 * TOPK] + routes[:, 2 * TOPK : 3 * TOPK]
    chosen = jnp.where(routes[:, :TOPK] == (me_ref[0] % n_ep).astype(F32), scores, 0.0)
    coef = jnp.sum(chosen, axis=1, keepdims=True) / jnp.sum(scores, axis=1, keepdims=True) * 2.5
    for p in range(SPAN):
        here = slice(p * part, (p + 1) * part)
        out = jnp.dot(act, down_ref[:, here], preferred_element_type=F32) * coef
        near_ref[:, here] = out[: rows // 2]
        far_ref[:, here] = out[rows // 2 :].astype(BF)


def single(kernel, n, out_shape, scalars, arrays, name, flops):
    return pl.pallas_call(
        functools.partial(kernel, n),
        in_specs=[pl.BlockSpec(memory_space=pltpu.SMEM)] * len(scalars)
        + [pl.BlockSpec(memory_space=pltpu.VMEM)] * len(arrays),
        out_shape=out_shape,
        compiler_params=pltpu.CompilerParams(vmem_limit_bytes=VMEM_LIMIT),
        cost_estimate=pl.CostEstimate(
            flops=flops, bytes_accessed=sum(2 * a.size for a in arrays), transcendentals=0
        ),
        name=name,
    )(*scalars, *arrays)


def reduce_rows(near, far, n):
    planes = n // SPAN
    width = near.shape[1]
    total = (near + swap(far, n, c=1).astype(F32)).reshape(4, planes * STEPS, width)
    kept = total[0]
    for q in range(1, 4):
        kept = kept + swap(total[q].astype(BF), n, q=q).astype(F32)
    kept = kept.reshape(planes, STEPS, width)
    return [kept[0]] + [swap(kept[k].astype(BF), n, k=k) for k in range(1, planes)]


def per_device(
    queries,
    new_latent,
    cache_latent,
    cache_len,
    route_ids,
    route_scores,
    residual,
    norm_gain,
    w_uv,
    w_out,
    w_gate,
    w_up,
    w_down,
):
    n_ep = lax.axis_size("ep")
    n = lax.axis_size("sec") * n_ep
    planes = n // SPAN
    heads = queries.shape[2]
    width = residual.shape[2]
    rows = n * STEPS
    me_one = lax.axis_index(AXES).astype(jnp.int32).reshape(1)

    with jax.named_scope("attention"):
        latents = attend(
            n,
            cache_len,
            queries[0].reshape(STEPS * heads, queries.shape[3]),
            new_latent[0],
            jnp.swapaxes(cache_latent[0], 0, 1),
        )

    with jax.named_scope("heads"):
        latents = lax.all_to_all(latents, AXES, 0, 0, tiled=True)
        near, far = single(
            heads_kernel,
            n,
            [jax.ShapeDtypeStruct((rows // 2, width), dtype) for dtype in (F32, BF)],
            [me_one],
            [latents.reshape(rows, LAT), w_uv[0], w_out[0]],
            "heads",
            2 * rows * VDIM * (LAT + width),
        )
        parts = reduce_rows(near, far, n)

    with jax.named_scope("norm"):
        high = route_scores[0].astype(BF)
        low = (route_scores[0] - high.astype(F32)).astype(BF)
        routes = jnp.concatenate([route_ids[0].astype(BF), high, low], axis=1)
        routes = jnp.pad(routes, ((0, 0), (0, 128 - 3 * TOPK)))
        hidden, normed = single(
            norm_kernel,
            n,
            [
                jax.ShapeDtypeStruct((STEPS, width), F32),
                jax.ShapeDtypeStruct((STEPS, width + 128), BF),
            ],
            [],
            parts + [residual[0], norm_gain.reshape(1, width), routes],
            "norm",
            8 * STEPS * width,
        )

    with jax.named_scope("spread"):
        along = jnp.concatenate([normed] + [swap(normed, n, k=k) for k in range(1, planes)], axis=0)
        blocks = [along] + [swap(along, n, q=q) for q in range(1, 4)]
        along, *weights = load(n, along, [w_gate[0], w_up[0], w_down[0]])
        blocks = blocks + [swap(x, n, c=1) for x in [along] + blocks[1:]]

    with jax.named_scope("experts"):
        near, far = single(
            functools.partial(expert_kernel, n_ep=n_ep),
            n,
            [jax.ShapeDtypeStruct((rows // 2, width), dtype) for dtype in (F32, BF)],
            [me_one],
            blocks + weights,
            "experts",
            6 * rows * width * w_gate.shape[2],
        )

    with jax.named_scope("collect"):
        result = hidden
        for term in reduce_rows(near, far, n):
            result = result + term.astype(F32)
        return result.astype(BF)[None]


def solution(mesh):
    placed = (
        P(("sec", "ep"), None, None, None),
        P(("sec", "ep"), None, None),
        P(("sec", "ep"), None, None),
        P(("sec", "ep")),
        P(("sec", "ep"), None, None),
        P(("sec", "ep"), None, None),
        P(("sec", "ep"), None, None),
        P(),
        P(("sec", "ep"), None, None),
        P(("sec", "ep"), None, None),
        P("ep", None, "sec"),
        P("ep", None, "sec"),
        P("ep", "sec", None),
    )
    return jax.shard_map(
        per_device,
        mesh=mesh,
        in_specs=placed,
        out_specs=P(("sec", "ep"), None, None),
        check_vma=False,
    )
```

```python
import functools
import math

import jax
import jax.numpy as jnp
from jax import lax
from jax.experimental import pallas as pl
from jax.experimental.pallas import tpu as pltpu
from jax.sharding import PartitionSpec as P

LAT = 512
ROPE = 64
VDIM = 128
STEPS = 4
TOPK = 8
BLK = 2048
CHUNKS = 2
SPAN = 8
AXES = ("sec", "ep")
NT = (((1,), (1,)), ((), ()))
BF = jnp.bfloat16
F32 = jnp.float32
VMEM_LIMIT = 16 * 1024 * 1024


def mask_of(n, q=0, c=0, k=0):
    return (q >> 1) * (n // 2) + k * 4 + (q & 1) * 2 + c


def swap(x, n, **differ):
    mask = mask_of(n, **differ)
    return lax.ppermute(x, AXES, [(d, d ^ mask) for d in range(n)])


def iota2(shape, axis):
    return lax.broadcasted_iota(jnp.int32, shape, axis)


def one_hot(columns, count):
    return (iota2(columns.shape, 1) == columns).astype(BF)


def pick(matrix, rows):
    return jnp.dot(matrix, rows, preferred_element_type=F32)


def attend_kernel(n, len_ref, q_hbm, new_hbm, keys_hbm, out_ref, q_ref, new_ref, keys_ref, m_ref, l_ref, acc_ref, small_sem, sem):
    rows = q_ref.shape[0]
    heads = rows // STEPS
    factor_base2 = (VDIM + ROPE) ** (-0.5) * math.log2(math.e)
    length = len_ref[0]
    blk = min(BLK, keys_ref.shape[1])

    def block_at(i):
        return pl.ds(pl.multiple_of(i * blk, blk), blk)

    def block_copy(i):
        return pltpu.make_async_copy(
            keys_hbm.at[:, block_at(i)], keys_ref.at[:, block_at(i)], sem.at[i]
        )

    def start(i):
        @pl.when(i * blk < length)
        def _():
            block_copy(i).start()

    q_copy = pltpu.make_async_copy(q_hbm, q_ref, small_sem.at[0])
    new_copy = pltpu.make_async_copy(new_hbm, new_ref, small_sem.at[1])
    q_copy.start()
    new_copy.start()
    start(0)
    start(1)
    r = iota2((rows, rows), 0)
    order = one_hot((r % STEPS) * heads + r // STEPS, rows)
    q_copy.wait()
    new_copy.wait()

    new = new_ref[...]
    s = lax.dot_general(q_ref[...], new, NT, preferred_element_type=F32)
    step = iota2(s.shape, 0) // heads
    s = jnp.where(iota2(s.shape, 1) <= step, s, -1e30)
    m = jnp.max(s, axis=1, keepdims=True)
    p = jnp.exp2((s - m) * factor_base2)
    m_ref[...] = m
    l_ref[...] = jnp.sum(p, axis=1, keepdims=True)
    acc_ref[...] = jnp.dot(p.astype(BF), new[:, :LAT], preferred_element_type=F32)

    def update(i, masked):
        start(i + 2)
        block_copy(i).wait()
        keys = keys_ref[:, block_at(i)]
        s = jnp.dot(q_ref[...], keys, preferred_element_type=F32)
        if masked:
            s = jnp.where(iota2(s.shape, 1) < length - i * blk, s, -1e30)
        m_old = m_ref[...]
        m = jnp.maximum(m_old, jnp.max(s, axis=1, keepdims=True))
        factor = jnp.exp2((m_old - m) * factor_base2)
        p = jnp.exp2((s - m) * factor_base2)
        m_ref[...] = m
        l_ref[...] = l_ref[...] * factor + jnp.sum(p, axis=1, keepdims=True)
        acc_ref[...] = acc_ref[...] * factor + lax.dot_general(
            p.astype(BF), keys[:LAT], NT, preferred_element_type=F32
        )

    full = length // blk

    @pl.loop(0, full)
    def _(i):
        update(i, False)

    @pl.when(full * blk < length)
    def _():
        update(full, True)

    out = (acc_ref[...] / l_ref[...]).astype(BF)
    out_ref[...] = pick(order, out).reshape(out_ref.shape).astype(BF)


def attend(n, length, q, new, keys):
    rows, width = q.shape
    cached = keys.shape[1]
    blocks = cached // min(BLK, cached)
    return pl.pallas_call(
        functools.partial(attend_kernel, n),
        in_specs=[pl.BlockSpec(memory_space=pltpu.SMEM)]
        + [pl.BlockSpec(memory_space=pl.ANY)] * 3,
        out_specs=pl.BlockSpec(memory_space=pltpu.VMEM),
        scratch_shapes=[
            pltpu.VMEM(q.shape, BF),
            pltpu.VMEM(new.shape, BF),
            pltpu.VMEM(keys.shape, BF),
            pltpu.VMEM((rows, 1), F32),
            pltpu.VMEM((rows, 1), F32),
            pltpu.VMEM((rows, LAT), F32),
            pltpu.SemaphoreType.DMA((2,)),
            pltpu.SemaphoreType.DMA((blocks,)),
        ],
        out_shape=jax.ShapeDtypeStruct((rows // STEPS, STEPS, LAT), BF),
        compiler_params=pltpu.CompilerParams(vmem_limit_bytes=56 * 1024 * 1024),
        cost_estimate=pl.CostEstimate(
            flops=2 * rows * cached * (width + LAT),
            bytes_accessed=2 * cached * width,
            transcendentals=rows * cached,
        ),
        name="attend",
    )(length, q, new, keys)


def partner_order(n, me, rows):
    planes = n // SPAN
    r = iota2((rows, rows), 0)
    c, q = r // (rows // 2), (r // (planes * STEPS)) % 4
    k, step = (r // STEPS) % planes, r % STEPS
    return me ^ ((q >> 1) * (n // 2) + k * 4 + (q & 1) * 2 + c), step


def store_halves(out, p, near_refs, far_refs):
    rows, part = out.shape
    chunk, place = p // (SPAN // CHUNKS), p % (SPAN // CHUNKS)
    here = slice(place * part, (place + 1) * part)
    near_refs[chunk][:, here] = out[: rows // 2]
    far_refs[chunk][:, here] = out[rows // 2 :].astype(BF)


def heads_kernel(n, me_ref, latents_ref, uv_ref, out_ref, *refs):
    rows = n * STEPS
    values = jnp.dot(latents_ref[...], uv_ref[...], preferred_element_type=F32).astype(BF)
    device, step = partner_order(n, me_ref[0], rows)
    values = pick(one_hot(device * STEPS + step, rows), values).astype(BF)
    part = out_ref.shape[1] // SPAN
    for p in range(SPAN):
        here = slice(p * part, (p + 1) * part)
        out = jnp.dot(values, out_ref[:, here], preferred_element_type=F32)
        store_halves(out, p, refs[:CHUNKS], refs[CHUNKS:])


def norm_kernel(n, *refs):
    planes = n // SPAN
    parts, refs = refs[: planes * CHUNKS], refs[planes * CHUNKS :]
    residual_ref, gain_ref, routes_ref, hidden_ref, out_refs = *refs[:4], refs[4:]
    width = residual_ref.shape[1]
    chunk = width // CHUNKS
    square = 0.0
    for c in range(CHUNKS):
        here = slice(c * chunk, (c + 1) * chunk)
        hidden = residual_ref[:, here].astype(F32)
        for ref in parts[c * planes : (c + 1) * planes]:
            hidden += ref[...].astype(F32)
        hidden_ref[:, here] = hidden
        square += jnp.sum(hidden * hidden, axis=1, keepdims=True)
    factor = lax.rsqrt(square / width + 1e-06)
    for c in range(CHUNKS):
        here = slice(c * chunk, (c + 1) * chunk)
        normed = hidden_ref[:, here] * factor * gain_ref[:, here].astype(F32)
        out_refs[c][:, :chunk] = normed.astype(BF)
    out_refs[-1][:, chunk:] = routes_ref[...]


def load_kernel(n, *refs):
    sources, targets, sem = refs[1:3], refs[4:6], refs[6]
    copies = [pltpu.make_async_copy(refs[0], refs[3], sem.at[8])]
    for i in range(2):
        step = sources[i].shape[0] // 4
        for j in range(4):
            here = pl.ds(j * step, step)
            copies.append(
                pltpu.make_async_copy(sources[i].at[here], targets[i].at[here], sem.at[4 * i + j])
            )
    for copy in copies:
        copy.start()
    for copy in copies:
        copy.wait()


def load(n, passed, arrays):
    return pl.pallas_call(
        functools.partial(load_kernel, n),
        in_specs=[pl.BlockSpec(memory_space=pltpu.VMEM)] + [pl.BlockSpec(memory_space=pl.ANY)] * 2,
        out_specs=[pl.BlockSpec(memory_space=pltpu.VMEM)] * 3,
        out_shape=[jax.ShapeDtypeStruct(a.shape, a.dtype) for a in [passed] + arrays],
        scratch_shapes=[pltpu.SemaphoreType.DMA((9,))],
        compiler_params=pltpu.CompilerParams(vmem_limit_bytes=44 * 1024 * 1024),
        cost_estimate=pl.CostEstimate(
            flops=0, bytes_accessed=sum(4 * a.size for a in arrays), transcendentals=0
        ),
        name="load_experts",
    )(passed, *arrays)


def expert_kernel(n, n_ep, me_ref, *refs):
    blocks, refs = refs[: 8 * CHUNKS], refs[8 * CHUNKS :]
    gate_ref, up_ref, down_hbm, refs = *refs[:3], refs[3:]
    near_refs, far_refs, down_ref, sem = refs[:CHUNKS], refs[CHUNKS : 2 * CHUNKS], *refs[2 * CHUNKS :]
    rows = n * STEPS
    width, units = gate_ref.shape
    part = width // SPAN
    down_copies = []
    for p in range(SPAN):
        here = pl.ds(p * part, part)
        down_copies.append(
            pltpu.make_async_copy(down_hbm.at[:, here], down_ref.at[:, here], sem.at[p])
        )
    for copy in down_copies:
        copy.start()
    gate = jnp.zeros((rows, units), F32)
    up = jnp.zeros((rows, units), F32)
    for p in range(SPAN):
        chunk, place = p // (SPAN // CHUNKS), p % (SPAN // CHUNKS)
        here = slice(place * part, (place + 1) * part)
        x = jnp.concatenate([ref[:, here] for ref in blocks[8 * chunk : 8 * chunk + 8]], axis=0)
        here = slice(p * part, (p + 1) * part)
        gate += jnp.dot(x, gate_ref[here], preferred_element_type=F32)
        up += jnp.dot(x, up_ref[here], preferred_element_type=F32)
    act = (gate * jax.nn.sigmoid(gate) * up).astype(BF)
    routes = [ref[:, width // CHUNKS :] for ref in blocks[-8:]]
    routes = jnp.concatenate(routes, axis=0).astype(F32)
    scores = routes[:, TOPK : 2 * TOPK] + routes[:, 2 * TOPK : 3 * TOPK]
    chosen = jnp.where(routes[:, :TOPK] == (me_ref[0] % n_ep).astype(F32), scores, 0.0)
    coef = jnp.sum(chosen, axis=1, keepdims=True) / jnp.sum(scores, axis=1, keepdims=True) * 2.5
    for p in range(SPAN):
        down_copies[p].wait()
        down = down_ref[:, p * part : (p + 1) * part]
        out = jnp.dot(act, down, preferred_element_type=F32) * coef
        store_halves(out, p, near_refs, far_refs)


def halves(n, width):
    shape = (n * STEPS // 2, width // CHUNKS)
    return [jax.ShapeDtypeStruct(shape, dtype) for dtype in [F32] * CHUNKS + [BF] * CHUNKS]


def run_experts(n, n_ep, me, blocks, gate, up, down):
    rows = n * STEPS
    units, width = down.shape
    return pl.pallas_call(
        functools.partial(expert_kernel, n, n_ep),
        in_specs=[pl.BlockSpec(memory_space=pltpu.SMEM)]
        + [pl.BlockSpec(memory_space=pltpu.VMEM)] * (len(blocks) + 2)
        + [pl.BlockSpec(memory_space=pl.ANY)],
        out_shape=halves(n, width),
        scratch_shapes=[pltpu.VMEM(down.shape, BF), pltpu.SemaphoreType.DMA((SPAN,))],
        compiler_params=pltpu.CompilerParams(vmem_limit_bytes=40 * 1024 * 1024),
        cost_estimate=pl.CostEstimate(
            flops=6 * rows * width * units,
            bytes_accessed=6 * width * units,
            transcendentals=rows * units,
        ),
        name="experts",
    )(me, *blocks, gate, up, down)


def single(kernel, n, out_shape, scalars, arrays, name, flops):
    return pl.pallas_call(
        functools.partial(kernel, n),
        in_specs=[pl.BlockSpec(memory_space=pltpu.SMEM)] * len(scalars)
        + [pl.BlockSpec(memory_space=pltpu.VMEM)] * len(arrays),
        out_shape=out_shape,
        compiler_params=pltpu.CompilerParams(vmem_limit_bytes=VMEM_LIMIT),
        cost_estimate=pl.CostEstimate(
            flops=flops, bytes_accessed=sum(2 * a.size for a in arrays), transcendentals=0
        ),
        name=name,
    )(*scalars, *arrays)


def reduce_rows(near, far, n):
    planes = n // SPAN
    width = near.shape[1]
    total = (near + swap(far, n, c=1).astype(F32)).reshape(4, planes * STEPS, width)
    kept = total[0]
    for q in range(1, 4):
        kept = kept + swap(total[q].astype(BF), n, q=q).astype(F32)
    kept = kept.reshape(planes, STEPS, width)
    return [kept[0]] + [swap(kept[k].astype(BF), n, k=k) for k in range(1, planes)]


def per_device(
    queries,
    new_latent,
    cache_latent,
    cache_len,
    route_ids,
    route_scores,
    residual,
    norm_gain,
    w_uv,
    w_out,
    w_gate,
    w_up,
    w_down,
):
    n_ep = lax.axis_size("ep")
    n = lax.axis_size("sec") * n_ep
    planes = n // SPAN
    heads = queries.shape[2]
    width = residual.shape[2]
    rows = n * STEPS
    me_one = lax.axis_index(AXES).astype(jnp.int32).reshape(1)

    with jax.named_scope("attention"):
        latents = attend(
            n,
            cache_len,
            queries[0].reshape(STEPS * heads, queries.shape[3]),
            new_latent[0],
            jnp.swapaxes(cache_latent[0], 0, 1),
        )

    with jax.named_scope("heads"):
        latents = lax.all_to_all(latents, AXES, 0, 0, tiled=True)
        out = single(
            heads_kernel,
            n,
            halves(n, width),
            [me_one],
            [latents.reshape(rows, LAT), w_uv[0], w_out[0]],
            "heads",
            2 * rows * VDIM * (LAT + width),
        )
        parts = [reduce_rows(out[c], out[CHUNKS + c], n) for c in range(CHUNKS)]

    with jax.named_scope("norm"):
        high = route_scores[0].astype(BF)
        low = (route_scores[0] - high.astype(F32)).astype(BF)
        routes = jnp.concatenate([route_ids[0].astype(BF), high, low], axis=1)
        routes = jnp.pad(routes, ((0, 0), (0, 128 - 3 * TOPK)))
        widths = [width // CHUNKS] * (CHUNKS - 1) + [width // CHUNKS + 128]
        hidden, *normed = single(
            norm_kernel,
            n,
            [jax.ShapeDtypeStruct((STEPS, width), F32)]
            + [jax.ShapeDtypeStruct((STEPS, w), BF) for w in widths],
            [],
            sum(parts, []) + [residual[0], norm_gain.reshape(1, width), routes],
            "norm",
            8 * STEPS * width,
        )

    with jax.named_scope("spread"):
        blocks = []
        for c in range(CHUNKS):
            x = normed[c]
            along = jnp.concatenate([x] + [swap(x, n, k=k) for k in range(1, planes)], axis=0)
            others = [swap(along, n, q=q) for q in range(1, 4)]
            if c == CHUNKS - 1:
                along, gate, up = load(n, along, [w_gate[0], w_up[0]])
            here = [along] + others
            blocks += here + [swap(x, n, c=1) for x in here]

    with jax.named_scope("experts"):
        out = run_experts(n, n_ep, me_one, blocks, gate, up, w_down[0])

    with jax.named_scope("collect"):
        results = []
        for c in range(CHUNKS):
            result = hidden[:, c * (width // CHUNKS) : (c + 1) * (width // CHUNKS)]
            for term in reduce_rows(out[c], out[CHUNKS + c], n):
                result = result + term.astype(F32)
            results.append(result.astype(BF))
        return jnp.concatenate(results, axis=1)[None]


def solution(mesh):
    placed = (
        P(("sec", "ep"), None, None, None),
        P(("sec", "ep"), None, None),
        P(("sec", "ep"), None, None),
        P(("sec", "ep")),
        P(("sec", "ep"), None, None),
        P(("sec", "ep"), None, None),
        P(("sec", "ep"), None, None),
        P(),
        P(("sec", "ep"), None, None),
        P(("sec", "ep"), None, None),
        P("ep", None, "sec"),
        P("ep", None, "sec"),
        P("ep", "sec", None),
    )
    return jax.shard_map(
        per_device,
        mesh=mesh,
        in_specs=placed,
        out_specs=P(("sec", "ep"), None, None),
        check_vma=False,
    )
```

```python
import functools
import math

import jax
import jax.numpy as jnp
from jax import lax
from jax.experimental import pallas as pl
from jax.experimental.pallas import tpu as pltpu
from jax.sharding import PartitionSpec as P

LAT = 512
ROPE = 64
VDIM = 128
STEPS = 4
TOPK = 8
BLK = 2048
LOADS = 8
SECOND_ORDER = [(c, j, i) for c in (0, 2) for j in range(2) for i in range(2)]
SPAN = 8
AXES = ("sec", "ep")
NT = (((1,), (1,)), ((), ()))
BF = jnp.bfloat16
F32 = jnp.float32
VMEM_LIMIT = 16 * 1024 * 1024


def mask_of(n, q=0, c=0, k=0):
    return (q >> 1) * (n // 2) + k * 4 + (q & 1) * 2 + c


def swap(x, n, **differ):
    mask = mask_of(n, **differ)
    return lax.ppermute(x, AXES, [(d, d ^ mask) for d in range(n)])


def iota2(shape, axis):
    return lax.broadcasted_iota(jnp.int32, shape, axis)


def one_hot(columns, count):
    return (iota2(columns.shape, 1) == columns).astype(BF)


def pick(matrix, rows):
    return jnp.dot(matrix, rows, preferred_element_type=F32)


def attend_kernel(n, len_ref, q_hbm, new_hbm, keys_hbm, out_ref, q_ref, new_ref, keys_ref, m_ref, l_ref, acc_ref, small_sem, sem):
    rows = q_ref.shape[0]
    heads = rows // STEPS
    factor_base2 = (VDIM + ROPE) ** (-0.5) * math.log2(math.e)
    length = len_ref[0]
    blk = min(BLK, keys_ref.shape[1])

    def block_at(i):
        return pl.ds(pl.multiple_of(i * blk, blk), blk)

    def block_copy(i):
        return pltpu.make_async_copy(
            keys_hbm.at[:, block_at(i)], keys_ref.at[:, block_at(i)], sem.at[i]
        )

    def start(i):
        @pl.when(i * blk < length)
        def _():
            block_copy(i).start()

    q_copy = pltpu.make_async_copy(q_hbm, q_ref, small_sem.at[0])
    new_copy = pltpu.make_async_copy(new_hbm, new_ref, small_sem.at[1])
    q_copy.start()
    new_copy.start()
    start(0)
    start(1)
    r = iota2((rows, rows), 0)
    order = one_hot((r % STEPS) * heads + r // STEPS, rows)
    q_copy.wait()
    new_copy.wait()

    new = new_ref[...]
    s = lax.dot_general(q_ref[...], new, NT, preferred_element_type=F32)
    step = iota2(s.shape, 0) // heads
    s = jnp.where(iota2(s.shape, 1) <= step, s, -1e30)
    m = jnp.max(s, axis=1, keepdims=True)
    p = jnp.exp2((s - m) * factor_base2)
    m_ref[...] = m
    l_ref[...] = jnp.sum(p, axis=1, keepdims=True)
    acc_ref[...] = jnp.dot(p.astype(BF), new[:, :LAT], preferred_element_type=F32)

    def update(i, masked):
        start(i + 2)
        block_copy(i).wait()
        keys = keys_ref[:, block_at(i)]
        s = jnp.dot(q_ref[...], keys, preferred_element_type=F32)
        if masked:
            s = jnp.where(iota2(s.shape, 1) < length - i * blk, s, -1e30)
        m_old = m_ref[...]
        m = jnp.maximum(m_old, jnp.max(s, axis=1, keepdims=True))
        factor = jnp.exp2((m_old - m) * factor_base2)
        p = jnp.exp2((s - m) * factor_base2)
        m_ref[...] = m
        l_ref[...] = l_ref[...] * factor + jnp.sum(p, axis=1, keepdims=True)
        acc_ref[...] = acc_ref[...] * factor + lax.dot_general(
            p.astype(BF), keys[:LAT], NT, preferred_element_type=F32
        )

    full = length // blk

    @pl.loop(0, full)
    def _(i):
        update(i, False)

    @pl.when(full * blk < length)
    def _():
        update(full, True)

    out = (acc_ref[...] / l_ref[...]).astype(BF)
    out_ref[...] = pick(order, out).reshape(out_ref.shape).astype(BF)


def attend(n, length, q, new, keys):
    rows, width = q.shape
    cached = keys.shape[1]
    blocks = cached // min(BLK, cached)
    return pl.pallas_call(
        functools.partial(attend_kernel, n),
        in_specs=[pl.BlockSpec(memory_space=pltpu.SMEM)]
        + [pl.BlockSpec(memory_space=pl.ANY)] * 3,
        out_specs=pl.BlockSpec(memory_space=pltpu.VMEM),
        scratch_shapes=[
            pltpu.VMEM(q.shape, BF),
            pltpu.VMEM(new.shape, BF),
            pltpu.VMEM(keys.shape, BF),
            pltpu.VMEM((rows, 1), F32),
            pltpu.VMEM((rows, 1), F32),
            pltpu.VMEM((rows, LAT), F32),
            pltpu.SemaphoreType.DMA((2,)),
            pltpu.SemaphoreType.DMA((blocks,)),
        ],
        out_shape=jax.ShapeDtypeStruct((rows // STEPS, STEPS, LAT), BF),
        compiler_params=pltpu.CompilerParams(vmem_limit_bytes=56 * 1024 * 1024),
        cost_estimate=pl.CostEstimate(
            flops=2 * rows * cached * (width + LAT),
            bytes_accessed=2 * cached * width,
            transcendentals=rows * cached,
        ),
        name="attend",
    )(length, q, new, keys)


def partner_order(n, me, rows):
    planes = n // SPAN
    r = iota2((rows, rows), 0)
    c, q = r // (rows // 2), (r // (planes * STEPS)) % 4
    k, step = (r // STEPS) % planes, r % STEPS
    return me ^ ((q >> 1) * (n // 2) + k * 4 + (q & 1) * 2 + c), step


def heads_kernel(n, me_ref, latents_ref, uv_ref, out_ref, near_ref, far_ref):
    rows = n * STEPS
    values = jnp.dot(latents_ref[...], uv_ref[...], preferred_element_type=F32).astype(BF)
    device, step = partner_order(n, me_ref[0], rows)
    values = pick(one_hot(device * STEPS + step, rows), values).astype(BF)
    part = out_ref.shape[1] // SPAN
    for p in range(SPAN):
        here = slice(p * part, (p + 1) * part)
        out = jnp.dot(values, out_ref[:, here], preferred_element_type=F32)
        near_ref[:, here] = out[: rows // 2]
        far_ref[:, here] = out[rows // 2 :].astype(BF)


def norm_kernel(n, *refs):
    parts, (residual_ref, gain_ref, routes_ref, hidden_ref, out_ref) = refs[:-5], refs[-5:]
    hidden = residual_ref[...].astype(F32)
    for ref in parts:
        hidden += ref[...].astype(F32)
    hidden_ref[...] = hidden
    width = hidden.shape[1]
    mean_square = jnp.sum(hidden * hidden, axis=1, keepdims=True) / width
    normed = hidden * lax.rsqrt(mean_square + 1e-06) * gain_ref[...].astype(F32)
    out_ref[:, :width] = normed.astype(BF)
    out_ref[:, width:] = routes_ref[...]


def load_kernel(n, ranges, *refs):
    count = len(ranges)
    sources, targets, sem = refs[1 : 1 + count], refs[2 + count : 2 + 2 * count], refs[-1]
    copies = [pltpu.make_async_copy(refs[0], refs[1 + count], sem.at[0])]
    for source, target, (first, rows) in zip(sources, targets, ranges):
        step = rows // LOADS
        for j in range(LOADS):
            copies.append(
                pltpu.make_async_copy(
                    source.at[pl.ds(first + j * step, step)],
                    target.at[pl.ds(j * step, step)],
                    sem.at[len(copies)],
                )
            )
    for copy in copies:
        copy.start()
    for copy in copies:
        copy.wait()


def load(n, passed, arrays, ranges, limit):
    shapes = [(rows, a.shape[1]) for a, (_, rows) in zip(arrays, ranges)]
    return pl.pallas_call(
        functools.partial(load_kernel, n, ranges),
        in_specs=[pl.BlockSpec(memory_space=pltpu.VMEM)]
        + [pl.BlockSpec(memory_space=pl.ANY)] * len(arrays),
        out_specs=[pl.BlockSpec(memory_space=pltpu.VMEM)] * (1 + len(arrays)),
        out_shape=[jax.ShapeDtypeStruct(passed.shape, passed.dtype)]
        + [jax.ShapeDtypeStruct(shape, BF) for shape in shapes],
        scratch_shapes=[pltpu.SemaphoreType.DMA((1 + LOADS * len(arrays),))],
        compiler_params=pltpu.CompilerParams(vmem_limit_bytes=limit * 1024 * 1024),
        cost_estimate=pl.CostEstimate(
            flops=0, bytes_accessed=sum(4 * r * c for r, c in shapes), transcendentals=0
        ),
        name="load",
    )(passed, *arrays)


def expert_kernel(n, me_ref, *refs, n_ep):
    firsts, seconds = refs[:4], refs[4:8]
    gate_ref, first_up_ref, second_up_ref, down_ref, near_ref, far_ref = refs[8:]
    rows = n * STEPS
    group = rows // 8
    width, units = gate_ref.shape
    part = width // SPAN
    gate = jnp.zeros((rows, units), F32)
    up = jnp.zeros((rows, units), F32)
    for p in range(SPAN):
        half, place = p // 4, p % 4
        here = slice(place * part, (place + 1) * part)
        if half == 0:
            x = [ref[:, here] for ref in firsts]
        else:
            x = [seconds[c + i][j * group : (j + 1) * group, here] for c, j, i in SECOND_ORDER]
        x = jnp.concatenate(x, axis=0)
        up_part = (first_up_ref, second_up_ref)[half][here]
        gate += jnp.dot(x, gate_ref[p * part : (p + 1) * part], preferred_element_type=F32)
        up += jnp.dot(x, up_part, preferred_element_type=F32)
    act = (gate * jax.nn.sigmoid(gate) * up).astype(BF)
    routes = [seconds[c + i][j * group : (j + 1) * group, width // 2 :] for c, j, i in SECOND_ORDER]
    routes = jnp.concatenate(routes, axis=0).astype(F32)
    scores = routes[:, TOPK : 2 * TOPK] + routes[:, 2 * TOPK : 3 * TOPK]
    chosen = jnp.where(routes[:, :TOPK] == (me_ref[0] % n_ep).astype(F32), scores, 0.0)
    coef = jnp.sum(chosen, axis=1, keepdims=True) / jnp.sum(scores, axis=1, keepdims=True) * 2.5
    for p in range(SPAN):
        here = slice(p * part, (p + 1) * part)
        out = jnp.dot(act, down_ref[:, here], preferred_element_type=F32) * coef
        near_ref[:, here] = out[: rows // 2]
        far_ref[:, here] = out[rows // 2 :].astype(BF)


def single(kernel, n, out_shape, scalars, arrays, name, flops):
    return pl.pallas_call(
        functools.partial(kernel, n),
        in_specs=[pl.BlockSpec(memory_space=pltpu.SMEM)] * len(scalars)
        + [pl.BlockSpec(memory_space=pltpu.VMEM)] * len(arrays),
        out_shape=out_shape,
        compiler_params=pltpu.CompilerParams(vmem_limit_bytes=VMEM_LIMIT),
        cost_estimate=pl.CostEstimate(
            flops=flops, bytes_accessed=sum(2 * a.size for a in arrays), transcendentals=0
        ),
        name=name,
    )(*scalars, *arrays)


def reduce_rows(near, far, n, beside=lambda rows: rows):
    planes = n // SPAN
    group = planes * STEPS
    width = near.shape[1]
    total = (near + swap(far, n, c=1).astype(F32)).reshape(2, 2, group, width)
    first, second = total[..., : width // 2], total[..., width // 2 :]
    first_sent = swap(first[1].astype(BF), n, q=2)
    second_sent = swap(second[:, 1].astype(BF), n, q=1)
    kept = beside(first[0].reshape(2 * group, width // 2)).reshape(2, group, width // 2)
    first = kept + first_sent.astype(F32)
    second = second[:, 0] + second_sent.astype(F32)
    first = first[0] + swap(first[1].astype(BF), n, q=1).astype(F32)
    second = second[0] + swap(second[1].astype(BF), n, q=2).astype(F32)
    kept = jnp.concatenate([first, second], axis=1).reshape(planes, STEPS, width)
    return [kept[0]] + [swap(kept[k].astype(BF), n, k=k) for k in range(1, planes)]


def spread_rows(rows, n, width, beside):
    planes = n // SPAN
    along = jnp.concatenate([rows] + [swap(rows, n, k=k) for k in range(1, planes)], axis=0)
    first, second = along[:, : width // 2], along[:, width // 2 :]
    first = jnp.concatenate([first, swap(first, n, q=1)], axis=0)
    second = jnp.concatenate([second, swap(second, n, q=2)], axis=0)
    first_far, second_far = swap(first, n, q=2), swap(second, n, q=1)
    first = beside(first)
    firsts, seconds = [first, first_far], [second, second_far]
    return (
        firsts + [swap(x, n, c=1) for x in firsts] + seconds + [swap(x, n, c=1) for x in seconds]
    )


def per_device(
    queries,
    new_latent,
    cache_latent,
    cache_len,
    route_ids,
    route_scores,
    residual,
    norm_gain,
    w_uv,
    w_out,
    w_gate,
    w_up,
    w_down,
):
    n_ep = lax.axis_size("ep")
    n = lax.axis_size("sec") * n_ep
    planes = n // SPAN
    heads = queries.shape[2]
    width = residual.shape[2]
    rows = n * STEPS
    me_one = lax.axis_index(AXES).astype(jnp.int32).reshape(1)

    with jax.named_scope("attention"):
        latents = attend(
            n,
            cache_len,
            queries[0].reshape(STEPS * heads, queries.shape[3]),
            new_latent[0],
            jnp.swapaxes(cache_latent[0], 0, 1),
        )

    with jax.named_scope("heads"):
        latents = lax.all_to_all(latents, AXES, 0, 0, tiled=True)
        near, far = single(
            heads_kernel,
            n,
            [jax.ShapeDtypeStruct((rows // 2, width), dtype) for dtype in (F32, BF)],
            [me_one],
            [latents.reshape(rows, LAT), w_uv[0], w_out[0]],
            "heads",
            2 * rows * VDIM * (LAT + width),
        )
        loaded = []

        def load_first(rows):
            rows, *arrays = load(
                n, rows, [w_gate[0], w_up[0]], [(0, width), (0, width // 2)], 42
            )
            loaded.extend(arrays)
            return rows

        parts = reduce_rows(near, far, n, load_first)

    with jax.named_scope("norm"):
        high = route_scores[0].astype(BF)
        low = (route_scores[0] - high.astype(F32)).astype(BF)
        routes = jnp.concatenate([route_ids[0].astype(BF), high, low], axis=1)
        routes = jnp.pad(routes, ((0, 0), (0, 128 - 3 * TOPK)))
        hidden, normed = single(
            norm_kernel,
            n,
            [
                jax.ShapeDtypeStruct((STEPS, width), F32),
                jax.ShapeDtypeStruct((STEPS, width + 128), BF),
            ],
            [],
            parts + [residual[0], norm_gain.reshape(1, width), routes],
            "norm",
            8 * STEPS * width,
        )

    with jax.named_scope("spread"):

        def load_second(rows):
            units = w_down.shape[1]
            rows, *arrays = load(
                n, rows, [w_up[0], w_down[0]], [(width // 2, width // 2), (0, units)], 33
            )
            loaded.extend(arrays)
            return rows

        blocks = spread_rows(normed, n, width, load_second)

    with jax.named_scope("experts"):
        near, far = single(
            functools.partial(expert_kernel, n_ep=n_ep),
            n,
            [jax.ShapeDtypeStruct((rows // 2, width), dtype) for dtype in (F32, BF)],
            [me_one],
            blocks + loaded,
            "experts",
            6 * rows * width * w_gate.shape[2],
        )

    with jax.named_scope("collect"):
        result = hidden
        for term in reduce_rows(near, far, n):
            result = result + term.astype(F32)
        return result.astype(BF)[None]


def solution(mesh):
    placed = (
        P(("sec", "ep"), None, None, None),
        P(("sec", "ep"), None, None),
        P(("sec", "ep"), None, None),
        P(("sec", "ep")),
        P(("sec", "ep"), None, None),
        P(("sec", "ep"), None, None),
        P(("sec", "ep"), None, None),
        P(),
        P(("sec", "ep"), None, None),
        P(("sec", "ep"), None, None),
        P("ep", None, "sec"),
        P("ep", None, "sec"),
        P("ep", "sec", None),
    )
    return jax.shard_map(
        per_device,
        mesh=mesh,
        in_specs=placed,
        out_specs=P(("sec", "ep"), None, None),
        check_vma=False,
    )
```

```python
import functools
import math

import jax
import jax.numpy as jnp
from jax import lax
from jax.experimental import pallas as pl
from jax.experimental.pallas import tpu as pltpu
from jax.sharding import PartitionSpec as P

LAT = 512
ROPE = 64
VDIM = 128
STEPS = 4
TOPK = 8
BLK = 1024
AHEAD = 4
SPAN = 8
AXES = ("sec", "ep")
NT = (((1,), (1,)), ((), ()))
BF = jnp.bfloat16
F32 = jnp.float32
VMEM_LIMIT = 16 * 1024 * 1024


def mask_of(n, q=0, c=0, k=0):
    return (q >> 1) * (n // 2) + k * 4 + (q & 1) * 2 + c


def swap(x, n, **differ):
    mask = mask_of(n, **differ)
    return lax.ppermute(x, AXES, [(d, d ^ mask) for d in range(n)])


def iota2(shape, axis):
    return lax.broadcasted_iota(jnp.int32, shape, axis)


def one_hot(columns, count):
    return (iota2(columns.shape, 1) == columns).astype(BF)


def pick(matrix, rows):
    return jnp.dot(matrix, rows, preferred_element_type=F32)


def attend_kernel(n, len_ref, q_hbm, new_hbm, keys_hbm, out_ref, q_ref, new_ref, keys_ref, m_ref, l_ref, acc_ref, small_sem, sem):
    rows = q_ref.shape[0]
    heads = rows // STEPS
    factor_base2 = (VDIM + ROPE) ** (-0.5) * math.log2(math.e)
    length = len_ref[0]
    blk = min(BLK, keys_ref.shape[1])

    def block_at(i):
        return pl.ds(pl.multiple_of(i * blk, blk), blk)

    def block_copy(i):
        return pltpu.make_async_copy(
            keys_hbm.at[:, block_at(i)], keys_ref.at[:, block_at(i)], sem.at[i]
        )

    def start(i):
        @pl.when(i * blk < length)
        def _():
            block_copy(i).start()

    q_copy = pltpu.make_async_copy(q_hbm, q_ref, small_sem.at[0])
    new_copy = pltpu.make_async_copy(new_hbm, new_ref, small_sem.at[1])
    q_copy.start()
    new_copy.start()
    for i in range(AHEAD):
        start(i)
    r = iota2((rows, rows), 0)
    order = one_hot((r % STEPS) * heads + r // STEPS, rows)
    q_copy.wait()
    new_copy.wait()

    new = new_ref[...]
    s = lax.dot_general(q_ref[...], new, NT, preferred_element_type=F32)
    step = iota2(s.shape, 0) // heads
    s = jnp.where(iota2(s.shape, 1) <= step, s, -1e30)
    m = jnp.max(s, axis=1, keepdims=True)
    p = jnp.exp2((s - m) * factor_base2)
    m_ref[...] = m
    l_ref[...] = jnp.sum(p, axis=1, keepdims=True)
    acc_ref[...] = jnp.dot(p.astype(BF), new[:, :LAT], preferred_element_type=F32)

    def scores(i, masked):
        block_copy(i).wait()
        s = jnp.dot(q_ref[...], keys_ref[:, block_at(i)], preferred_element_type=F32)
        if masked:
            s = jnp.where(iota2(s.shape, 1) < length - i * blk, s, -1e30)
        return s

    def absorb(i, s):
        m_old = m_ref[...]
        m = jnp.maximum(m_old, jnp.max(s, axis=1, keepdims=True))
        factor = jnp.exp2((m_old - m) * factor_base2)
        p = jnp.exp2((s - m) * factor_base2)
        m_ref[...] = m
        l_ref[...] = l_ref[...] * factor + jnp.sum(p, axis=1, keepdims=True)
        acc_ref[...] = acc_ref[...] * factor + lax.dot_general(
            p.astype(BF), keys_ref[:LAT, block_at(i)], NT, preferred_element_type=F32
        )

    pairs = length // (2 * blk)

    @pl.loop(0, pairs)
    def _(i):
        for ahead in range(2):
            start(2 * i + AHEAD + ahead)
        first, second = scores(2 * i, False), scores(2 * i + 1, False)
        absorb(2 * i, first)
        absorb(2 * i + 1, second)

    for tail in range(2):

        @pl.when((2 * pairs + tail) * blk < length)
        def _(tail=tail):
            absorb(2 * pairs + tail, scores(2 * pairs + tail, True))

    out = (acc_ref[...] / l_ref[...]).astype(BF)
    out_ref[...] = pick(order, out).reshape(out_ref.shape).astype(BF)


def attend(n, length, q, new, keys):
    rows, width = q.shape
    cached = keys.shape[1]
    blocks = cached // min(BLK, cached)
    return pl.pallas_call(
        functools.partial(attend_kernel, n),
        in_specs=[pl.BlockSpec(memory_space=pltpu.SMEM)]
        + [pl.BlockSpec(memory_space=pl.ANY)] * 3,
        out_specs=pl.BlockSpec(memory_space=pltpu.VMEM),
        scratch_shapes=[
            pltpu.VMEM(q.shape, BF),
            pltpu.VMEM(new.shape, BF),
            pltpu.VMEM(keys.shape, BF),
            pltpu.VMEM((rows, 1), F32),
            pltpu.VMEM((rows, 1), F32),
            pltpu.VMEM((rows, LAT), F32),
            pltpu.SemaphoreType.DMA((2,)),
            pltpu.SemaphoreType.DMA((blocks,)),
        ],
        out_shape=jax.ShapeDtypeStruct((rows // STEPS, STEPS, LAT), BF),
        compiler_params=pltpu.CompilerParams(vmem_limit_bytes=56 * 1024 * 1024),
        cost_estimate=pl.CostEstimate(
            flops=2 * rows * cached * (width + LAT),
            bytes_accessed=2 * cached * width,
            transcendentals=rows * cached,
        ),
        name="attend",
    )(length, q, new, keys)


def partner_order(n, me, rows):
    planes = n // SPAN
    r = iota2((rows, rows), 0)
    c, q = r // (rows // 2), (r // (planes * STEPS)) % 4
    k, step = (r // STEPS) % planes, r % STEPS
    return me ^ ((q >> 1) * (n // 2) + k * 4 + (q & 1) * 2 + c), step


def heads_kernel(n, me_ref, latents_ref, uv_ref, out_ref, near_ref, far_ref):
    rows = n * STEPS
    values = jnp.dot(latents_ref[...], uv_ref[...], preferred_element_type=F32).astype(BF)
    device, step = partner_order(n, me_ref[0], rows)
    values = pick(one_hot(device * STEPS + step, rows), values).astype(BF)
    part = out_ref.shape[1] // SPAN
    for p in range(SPAN):
        here = slice(p * part, (p + 1) * part)
        out = jnp.dot(values, out_ref[:, here], preferred_element_type=F32)
        near_ref[:, here] = out[: rows // 2]
        far_ref[:, here] = out[rows // 2 :].astype(BF)


def norm_kernel(n, *refs):
    parts, (residual_ref, gain_ref, routes_ref, hidden_ref, out_ref) = refs[:-5], refs[-5:]
    hidden = residual_ref[...].astype(F32)
    for ref in parts:
        hidden += ref[...].astype(F32)
    hidden_ref[...] = hidden
    width = hidden.shape[1]
    mean_square = jnp.sum(hidden * hidden, axis=1, keepdims=True) / width
    normed = hidden * lax.rsqrt(mean_square + 1e-06) * gain_ref[...].astype(F32)
    out_ref[:, :width] = normed.astype(BF)
    out_ref[:, width:] = routes_ref[...]


def load_kernel(n, *refs):
    sources, targets, sem = refs[1:4], refs[5:8], refs[8]
    copies = [pltpu.make_async_copy(refs[0], refs[4], sem.at[12])]
    for i in range(3):
        step = sources[i].shape[0] // 4
        for j in range(4):
            here = pl.ds(j * step, step)
            copies.append(
                pltpu.make_async_copy(sources[i].at[here], targets[i].at[here], sem.at[4 * i + j])
            )
    for copy in copies:
        copy.start()
    for copy in copies:
        copy.wait()


def load(n, passed, arrays):
    return pl.pallas_call(
        functools.partial(load_kernel, n),
        in_specs=[pl.BlockSpec(memory_space=pltpu.VMEM)] + [pl.BlockSpec(memory_space=pl.ANY)] * 3,
        out_specs=[pl.BlockSpec(memory_space=pltpu.VMEM)] * 4,
        out_shape=[jax.ShapeDtypeStruct(a.shape, a.dtype) for a in [passed] + arrays],
        scratch_shapes=[pltpu.SemaphoreType.DMA((13,))],
        compiler_params=pltpu.CompilerParams(vmem_limit_bytes=28 * 1024 * 1024),
        cost_estimate=pl.CostEstimate(
            flops=0, bytes_accessed=sum(4 * a.size for a in arrays), transcendentals=0
        ),
        name="load_experts",
    )(passed, *arrays)


def expert_kernel(n, me_ref, *refs, n_ep):
    blocks, (gate_ref, up_ref, down_ref, near_ref, far_ref) = refs[:8], refs[8:]
    rows = n * STEPS
    width, units = gate_ref.shape
    part = width // SPAN
    gate = jnp.zeros((rows, units), F32)
    up = jnp.zeros((rows, units), F32)
    for p in range(SPAN):
        here = slice(p * part, (p + 1) * part)
        x = jnp.concatenate([ref[:, here] for ref in blocks], axis=0)
        gate += jnp.dot(x, gate_ref[here], preferred_element_type=F32)
        up += jnp.dot(x, up_ref[here], preferred_element_type=F32)
    act = (gate * jax.nn.sigmoid(gate) * up).astype(BF)
    routes = jnp.concatenate([ref[:, width:] for ref in blocks], axis=0).astype(F32)
    scores = routes[:, TOPK : 2 * TOPK] + routes[:, 2 * TOPK : 3 * TOPK]
    chosen = jnp.where(routes[:, :TOPK] == (me_ref[0] % n_ep).astype(F32), scores, 0.0)
    coef = jnp.sum(chosen, axis=1, keepdims=True) / jnp.sum(scores, axis=1, keepdims=True) * 2.5
    for p in range(SPAN):
        here = slice(p * part, (p + 1) * part)
        out = jnp.dot(act, down_ref[:, here], preferred_element_type=F32) * coef
        near_ref[:, here] = out[: rows // 2]
        far_ref[:, here] = out[rows // 2 :].astype(BF)


def single(kernel, n, out_shape, scalars, arrays, name, flops):
    return pl.pallas_call(
        functools.partial(kernel, n),
        in_specs=[pl.BlockSpec(memory_space=pltpu.SMEM)] * len(scalars)
        + [pl.BlockSpec(memory_space=pltpu.VMEM)] * len(arrays),
        out_shape=out_shape,
        compiler_params=pltpu.CompilerParams(vmem_limit_bytes=VMEM_LIMIT),
        cost_estimate=pl.CostEstimate(
            flops=flops, bytes_accessed=sum(2 * a.size for a in arrays), transcendentals=0
        ),
        name=name,
    )(*scalars, *arrays)


def reduce_rows(near, far, n):
    planes = n // SPAN
    width = near.shape[1]
    total = (near + swap(far, n, c=1).astype(F32)).reshape(4, planes * STEPS, width)
    kept = total[0]
    for q in (3, 2, 1):
        kept = kept + swap(total[q].astype(BF), n, q=q).astype(F32)
    kept = kept.reshape(planes, STEPS, width)
    return [kept[0]] + [swap(kept[k].astype(BF), n, k=k) for k in range(1, planes)]


def per_device(
    queries,
    new_latent,
    cache_latent,
    cache_len,
    route_ids,
    route_scores,
    residual,
    norm_gain,
    w_uv,
    w_out,
    w_gate,
    w_up,
    w_down,
):
    n_ep = lax.axis_size("ep")
    n = lax.axis_size("sec") * n_ep
    planes = n // SPAN
    heads = queries.shape[2]
    width = residual.shape[2]
    rows = n * STEPS
    me_one = lax.axis_index(AXES).astype(jnp.int32).reshape(1)

    with jax.named_scope("attention"):
        latents = attend(
            n,
            cache_len,
            queries[0].reshape(STEPS * heads, queries.shape[3]),
            new_latent[0],
            jnp.swapaxes(cache_latent[0], 0, 1),
        )

    with jax.named_scope("heads"):
        latents = lax.all_to_all(latents, AXES, 0, 0, tiled=True)
        near, far = single(
            heads_kernel,
            n,
            [jax.ShapeDtypeStruct((rows // 2, width), dtype) for dtype in (F32, BF)],
            [me_one],
            [latents.reshape(rows, LAT), w_uv[0], w_out[0]],
            "heads",
            2 * rows * VDIM * (LAT + width),
        )
        parts = reduce_rows(near, far, n)

    with jax.named_scope("norm"):
        high = route_scores[0].astype(BF)
        low = (route_scores[0] - high.astype(F32)).astype(BF)
        routes = jnp.concatenate([route_ids[0].astype(BF), high, low], axis=1)
        routes = jnp.pad(routes, ((0, 0), (0, 128 - 3 * TOPK)))
        hidden, normed = single(
            norm_kernel,
            n,
            [
                jax.ShapeDtypeStruct((STEPS, width), F32),
                jax.ShapeDtypeStruct((STEPS, width + 128), BF),
            ],
            [],
            parts + [residual[0], norm_gain.reshape(1, width), routes],
            "norm",
            8 * STEPS * width,
        )

    with jax.named_scope("spread"):
        along = jnp.concatenate([normed] + [swap(normed, n, k=k) for k in range(1, planes)], axis=0)
        blocks = [along] + [swap(along, n, q=q) for q in range(1, 4)]
        along, *weights = load(n, along, [w_gate[0], w_up[0], w_down[0]])
        blocks = blocks + [swap(x, n, c=1) for x in [along] + blocks[1:]]

    with jax.named_scope("experts"):
        near, far = single(
            functools.partial(expert_kernel, n_ep=n_ep),
            n,
            [jax.ShapeDtypeStruct((rows // 2, width), dtype) for dtype in (F32, BF)],
            [me_one],
            blocks + weights,
            "experts",
            6 * rows * width * w_gate.shape[2],
        )

    with jax.named_scope("collect"):
        result = hidden
        for term in reduce_rows(near, far, n):
            result = result + term.astype(F32)
        return result.astype(BF)[None]


def solution(mesh):
    placed = (
        P(("sec", "ep"), None, None, None),
        P(("sec", "ep"), None, None),
        P(("sec", "ep"), None, None),
        P(("sec", "ep")),
        P(("sec", "ep"), None, None),
        P(("sec", "ep"), None, None),
        P(("sec", "ep"), None, None),
        P(),
        P(("sec", "ep"), None, None),
        P(("sec", "ep"), None, None),
        P("ep", None, "sec"),
        P("ep", None, "sec"),
        P("ep", "sec", None),
    )
    return jax.shard_map(
        per_device,
        mesh=mesh,
        in_specs=placed,
        out_specs=P(("sec", "ep"), None, None),
        check_vma=False,
    )
```

```python
import functools
import math

import jax
import jax.numpy as jnp
from jax import lax
from jax.experimental import pallas as pl
from jax.experimental.pallas import tpu as pltpu
from jax.sharding import PartitionSpec as P

LAT = 512
ROPE = 64
VDIM = 128
STEPS = 4
TOPK = 8
BLK = 2048
LATE = 2
SPAN = 8
AXES = ("sec", "ep")
NT = (((1,), (1,)), ((), ()))
BF = jnp.bfloat16
F32 = jnp.float32
VMEM_LIMIT = 16 * 1024 * 1024


def mask_of(n, q=0, c=0, k=0):
    return (q >> 1) * (n // 2) + k * 4 + (q & 1) * 2 + c


def swap(x, n, **differ):
    mask = mask_of(n, **differ)
    return lax.ppermute(x, AXES, [(d, d ^ mask) for d in range(n)])


def iota2(shape, axis):
    return lax.broadcasted_iota(jnp.int32, shape, axis)


def one_hot(columns, count):
    return (iota2(columns.shape, 1) == columns).astype(BF)


def pick(matrix, rows):
    return jnp.dot(matrix, rows, preferred_element_type=F32)


def attend_kernel(n, len_ref, q_hbm, new_hbm, keys_hbm, out_ref, q_ref, new_ref, keys_ref, m_ref, l_ref, acc_ref, small_sem, sem):
    rows = q_ref.shape[0]
    heads = rows // STEPS
    factor_base2 = (VDIM + ROPE) ** (-0.5) * math.log2(math.e)
    length = len_ref[0]
    blk = min(BLK, keys_ref.shape[1])

    def block_at(i):
        return pl.ds(pl.multiple_of(i * blk, blk), blk)

    def block_copy(i):
        return pltpu.make_async_copy(
            keys_hbm.at[:, block_at(i)], keys_ref.at[:, block_at(i)], sem.at[i]
        )

    def start(i):
        @pl.when(i * blk < length)
        def _():
            block_copy(i).start()

    q_copy = pltpu.make_async_copy(q_hbm, q_ref, small_sem.at[0])
    new_copy = pltpu.make_async_copy(new_hbm, new_ref, small_sem.at[1])
    q_copy.start()
    new_copy.start()
    start(0)
    start(1)
    r = iota2((rows, rows), 0)
    order = one_hot((r % STEPS) * heads + r // STEPS, rows)
    q_copy.wait()
    new_copy.wait()

    new = new_ref[...]
    s = lax.dot_general(q_ref[...], new, NT, preferred_element_type=F32)
    step = iota2(s.shape, 0) // heads
    s = jnp.where(iota2(s.shape, 1) <= step, s, -1e30)
    m = jnp.max(s, axis=1, keepdims=True)
    p = jnp.exp2((s - m) * factor_base2)
    m_ref[...] = m
    l_ref[...] = jnp.sum(p, axis=1, keepdims=True)
    acc_ref[...] = jnp.dot(p.astype(BF), new[:, :LAT], preferred_element_type=F32)

    def update(i, masked):
        start(i + 2)
        block_copy(i).wait()
        keys = keys_ref[:, block_at(i)]
        s = jnp.dot(q_ref[...], keys, preferred_element_type=F32)
        if masked:
            s = jnp.where(iota2(s.shape, 1) < length - i * blk, s, -1e30)
        m_old = m_ref[...]
        m = jnp.maximum(m_old, jnp.max(s, axis=1, keepdims=True))
        factor = jnp.exp2((m_old - m) * factor_base2)
        p = jnp.exp2((s - m) * factor_base2)
        m_ref[...] = m
        l_ref[...] = l_ref[...] * factor + jnp.sum(p, axis=1, keepdims=True)
        acc_ref[...] = acc_ref[...] * factor + lax.dot_general(
            p.astype(BF), keys[:LAT], NT, preferred_element_type=F32
        )

    full = length // blk

    @pl.loop(0, full)
    def _(i):
        update(i, False)

    @pl.when(full * blk < length)
    def _():
        update(full, True)

    out = (acc_ref[...] / l_ref[...]).astype(BF)
    out_ref[...] = pick(order, out).reshape(out_ref.shape).astype(BF)


def attend(n, length, q, new, keys):
    rows, width = q.shape
    cached = keys.shape[1]
    blocks = cached // min(BLK, cached)
    return pl.pallas_call(
        functools.partial(attend_kernel, n),
        in_specs=[pl.BlockSpec(memory_space=pltpu.SMEM)]
        + [pl.BlockSpec(memory_space=pl.ANY)] * 3,
        out_specs=pl.BlockSpec(memory_space=pltpu.VMEM),
        scratch_shapes=[
            pltpu.VMEM(q.shape, BF),
            pltpu.VMEM(new.shape, BF),
            pltpu.VMEM(keys.shape, BF),
            pltpu.VMEM((rows, 1), F32),
            pltpu.VMEM((rows, 1), F32),
            pltpu.VMEM((rows, LAT), F32),
            pltpu.SemaphoreType.DMA((2,)),
            pltpu.SemaphoreType.DMA((blocks,)),
        ],
        out_shape=jax.ShapeDtypeStruct((rows // STEPS, STEPS, LAT), BF),
        compiler_params=pltpu.CompilerParams(vmem_limit_bytes=56 * 1024 * 1024),
        cost_estimate=pl.CostEstimate(
            flops=2 * rows * cached * (width + LAT),
            bytes_accessed=2 * cached * width,
            transcendentals=rows * cached,
        ),
        name="attend",
    )(length, q, new, keys)


def split_rows(n, r, planes_first):
    planes = n // SPAN
    c = r // (n * STEPS // 2)
    if planes_first:
        return c, (r // STEPS) % 4, (r // (4 * STEPS)) % planes, r % STEPS
    return c, (r // (planes * STEPS)) % 4, (r // STEPS) % planes, r % STEPS


def partner_order(n, me, rows, planes_first):
    c, q, k, step = split_rows(n, iota2((rows, rows), 0), planes_first)
    device = me ^ ((q >> 1) * (n // 2) + k * 4 + (q & 1) * 2 + c)
    return one_hot(device * STEPS + step, rows)


def store_block(out, p, near_ref, far_ref):
    rows, part = out.shape
    here = slice(p * part, (p + 1) * part)
    near_ref[:, here] = out[: rows // 2]
    far_ref[:, here] = out[rows // 2 :].astype(BF)


def halves(n, width):
    return [jax.ShapeDtypeStruct((n * STEPS // 2, width), dtype) for dtype in (F32, BF)]


def late_from(width):
    return width - width // SPAN * LATE


def core_kernel(n, near_ref, got_ref, *refs):
    early = late_from(near_ref.shape[1])
    total = near_ref[...] + got_ref[...].astype(F32)
    for here, parts in ((slice(0, early), refs[:4]), (slice(early, None), refs[4:])):
        rows = total.shape[0] // len(parts)
        for i, ref in enumerate(parts):
            ref[...] = total[i * rows : (i + 1) * rows, here].astype(ref.dtype)


def second_kernel(n, *refs):
    planes = n // SPAN
    terms, late_terms, refs = refs[:4], refs[4 : 4 + planes], refs[4 + planes :]
    for terms, parts in ((terms, refs[:planes]), (late_terms, refs[planes:])):
        total = terms[0][...]
        for ref in terms[1:]:
            total += ref[...].astype(F32)
        for i, ref in enumerate(parts):
            ref[...] = total[i * STEPS : (i + 1) * STEPS].astype(ref.dtype)


def heads_kernel(n, me_ref, latents_ref, uv_ref, out_ref, *refs):
    rows = n * STEPS
    values = jnp.dot(latents_ref[...], uv_ref[...], preferred_element_type=F32).astype(BF)
    moved = [pick(partner_order(n, me_ref[0], rows, f), values).astype(BF) for f in (False, True)]
    part = out_ref.shape[1] // SPAN
    for p in range(SPAN):
        weights = out_ref[:, p * part : (p + 1) * part]
        values = moved[p >= SPAN - LATE]
        store_block(jnp.dot(values, weights, preferred_element_type=F32), p, *refs)


def norm_kernel(n, *refs):
    planes = n // SPAN
    parts, late_parts, refs = refs[:planes], refs[planes : planes + 4], refs[planes + 4 :]
    residual_ref, gain_ref, routes_ref, hidden_ref, out_ref = refs
    width = residual_ref.shape[1]
    early = parts[0].shape[1]
    square = 0.0
    for here, terms in ((slice(0, early), parts), (slice(early, width), late_parts)):
        hidden = residual_ref[:, here].astype(F32)
        for ref in terms:
            hidden += ref[...].astype(F32)
        hidden_ref[:, here] = hidden
        square += jnp.sum(hidden * hidden, axis=1, keepdims=True)
    factor = lax.rsqrt(square / width + 1e-06)
    normed = hidden_ref[...] * factor * gain_ref[...].astype(F32)
    out_ref[:, :width] = normed.astype(BF)
    out_ref[:, width:] = routes_ref[...]


def load_kernel(n, *refs):
    sources, targets, sem = refs[1:4], refs[5:8], refs[8]
    copies = [pltpu.make_async_copy(refs[0], refs[4], sem.at[12])]
    for i in range(3):
        step = sources[i].shape[0] // 4
        for j in range(4):
            here = pl.ds(j * step, step)
            copies.append(
                pltpu.make_async_copy(sources[i].at[here], targets[i].at[here], sem.at[4 * i + j])
            )
    for copy in copies:
        copy.start()
    for copy in copies:
        copy.wait()


def load(n, passed, arrays):
    return pl.pallas_call(
        functools.partial(load_kernel, n),
        in_specs=[pl.BlockSpec(memory_space=pltpu.VMEM)] + [pl.BlockSpec(memory_space=pl.ANY)] * 3,
        out_specs=[pl.BlockSpec(memory_space=pltpu.VMEM)] * 4,
        out_shape=[jax.ShapeDtypeStruct(a.shape, a.dtype) for a in [passed] + arrays],
        scratch_shapes=[pltpu.SemaphoreType.DMA((13,))],
        compiler_params=pltpu.CompilerParams(vmem_limit_bytes=28 * 1024 * 1024),
        cost_estimate=pl.CostEstimate(
            flops=0, bytes_accessed=sum(4 * a.size for a in arrays), transcendentals=0
        ),
        name="load_experts",
    )(passed, *arrays)


def share_of(routes, expert):
    scores = routes[:, TOPK : 2 * TOPK] + routes[:, 2 * TOPK : 3 * TOPK]
    chosen = jnp.where(routes[:, :TOPK] == expert.astype(F32), scores, 0.0)
    return jnp.sum(chosen, axis=1, keepdims=True) / jnp.sum(scores, axis=1, keepdims=True) * 2.5


def expert_kernel(n, me_ref, *refs, n_ep):
    blocks, (gate_ref, up_ref, down_ref), refs = refs[:8], refs[8:11], refs[11:]
    rows = n * STEPS
    width, units = gate_ref.shape
    part = width // SPAN
    gate = jnp.zeros((rows, units), F32)
    up = jnp.zeros((rows, units), F32)
    for p in range(SPAN):
        here = slice(p * part, (p + 1) * part)
        x = jnp.concatenate([ref[:, here] for ref in blocks], axis=0)
        gate += jnp.dot(x, gate_ref[here], preferred_element_type=F32)
        up += jnp.dot(x, up_ref[here], preferred_element_type=F32)
    act = (gate * jax.nn.sigmoid(gate) * up).astype(BF)
    routes = jnp.concatenate([ref[:, width:] for ref in blocks], axis=0).astype(F32)
    c, q, k, step = split_rows(n, iota2((rows, rows), 0), True)
    late_order = one_hot(((c * 4 + q) * (n // SPAN) + k) * STEPS + step, rows)
    acts = [act, pick(late_order, act).astype(BF)]
    late_routes = pick(late_order, routes.astype(BF))
    coefs = [share_of(r, me_ref[0] % n_ep) for r in (routes, late_routes)]
    for p in range(SPAN):
        late = p >= SPAN - LATE
        down = down_ref[:, p * part : (p + 1) * part]
        out = jnp.dot(acts[late], down, preferred_element_type=F32) * coefs[late]
        store_block(out, p, *refs)


def single(kernel, n, out_shape, scalars, arrays, name, flops):
    return pl.pallas_call(
        functools.partial(kernel, n),
        in_specs=[pl.BlockSpec(memory_space=pltpu.SMEM)] * len(scalars)
        + [pl.BlockSpec(memory_space=pltpu.VMEM)] * len(arrays),
        out_shape=out_shape,
        compiler_params=pltpu.CompilerParams(vmem_limit_bytes=VMEM_LIMIT),
        cost_estimate=pl.CostEstimate(
            flops=flops, bytes_accessed=sum(2 * a.size for a in arrays), transcendentals=0
        ),
        name=name,
    )(*scalars, *arrays)


def kept_and_sent(count, rows, width):
    return [jax.ShapeDtypeStruct((rows, width), BF if i else F32) for i in range(count)]


def reduce_rows(near, far, n):
    planes = n // SPAN
    width = near.shape[1]
    early = late_from(width)
    late = width - early
    shapes = kept_and_sent(4, planes * STEPS, early) + kept_and_sent(planes, 4 * STEPS, late)
    parts = single(core_kernel, n, shapes, [], [near, swap(far, n, c=1)], "core_sum", near.size)
    chips, lines = parts[:4], parts[4:]
    chips = [chips[0]] + [swap(chips[q], n, q=q) for q in range(1, 4)]
    lines = [lines[0]] + [swap(lines[k], n, k=k) for k in range(1, planes)]
    shapes = kept_and_sent(planes, STEPS, early) + kept_and_sent(4, STEPS, late)
    parts = single(second_kernel, n, shapes, [], chips + lines, "second_sum", near.size)
    lines, chips = parts[:planes], parts[planes:]
    return (
        [lines[0]] + [swap(lines[k], n, k=k) for k in range(1, planes)],
        [chips[0]] + [swap(chips[q], n, q=q) for q in range(1, 4)],
    )


def per_device(
    queries,
    new_latent,
    cache_latent,
    cache_len,
    route_ids,
    route_scores,
    residual,
    norm_gain,
    w_uv,
    w_out,
    w_gate,
    w_up,
    w_down,
):
    n_ep = lax.axis_size("ep")
    n = lax.axis_size("sec") * n_ep
    planes = n // SPAN
    heads = queries.shape[2]
    width = residual.shape[2]
    rows = n * STEPS
    me_one = lax.axis_index(AXES).astype(jnp.int32).reshape(1)

    with jax.named_scope("attention"):
        latents = attend(
            n,
            cache_len,
            queries[0].reshape(STEPS * heads, queries.shape[3]),
            new_latent[0],
            jnp.swapaxes(cache_latent[0], 0, 1),
        )

    with jax.named_scope("heads"):
        latents = lax.all_to_all(latents, AXES, 0, 0, tiled=True)
        out = single(
            heads_kernel,
            n,
            halves(n, width),
            [me_one],
            [latents.reshape(rows, LAT), w_uv[0], w_out[0]],
            "heads",
            2 * rows * VDIM * (LAT + width),
        )
        parts, late_parts = reduce_rows(*out, n)

    with jax.named_scope("norm"):
        high = route_scores[0].astype(BF)
        low = (route_scores[0] - high.astype(F32)).astype(BF)
        routes = jnp.concatenate([route_ids[0].astype(BF), high, low], axis=1)
        routes = jnp.pad(routes, ((0, 0), (0, 128 - 3 * TOPK)))
        hidden, normed = single(
            norm_kernel,
            n,
            [
                jax.ShapeDtypeStruct((STEPS, width), F32),
                jax.ShapeDtypeStruct((STEPS, width + 128), BF),
            ],
            [],
            parts + late_parts + [residual[0], norm_gain.reshape(1, width), routes],
            "norm",
            8 * STEPS * width,
        )

    with jax.named_scope("spread"):
        along = jnp.concatenate([normed] + [swap(normed, n, k=k) for k in range(1, planes)], axis=0)
        blocks = [along] + [swap(along, n, q=q) for q in range(1, 4)]
        along, *weights = load(n, along, [w_gate[0], w_up[0], w_down[0]])
        blocks = blocks + [swap(x, n, c=1) for x in [along] + blocks[1:]]

    with jax.named_scope("experts"):
        out = single(
            functools.partial(expert_kernel, n_ep=n_ep),
            n,
            halves(n, width),
            [me_one],
            blocks + weights,
            "experts",
            6 * rows * width * w_gate.shape[2],
        )

    with jax.named_scope("collect"):
        results = []
        first = 0
        for terms in reduce_rows(*out, n):
            last = first + terms[0].shape[1]
            result = hidden[:, first:last]
            for term in terms:
                result = result + term.astype(F32)
            results.append(result.astype(BF))
            first = last
        return jnp.concatenate(results, axis=1)[None]


def solution(mesh):
    placed = (
        P(("sec", "ep"), None, None, None),
        P(("sec", "ep"), None, None),
        P(("sec", "ep"), None, None),
        P(("sec", "ep")),
        P(("sec", "ep"), None, None),
        P(("sec", "ep"), None, None),
        P(("sec", "ep"), None, None),
        P(),
        P(("sec", "ep"), None, None),
        P(("sec", "ep"), None, None),
        P("ep", None, "sec"),
        P("ep", None, "sec"),
        P("ep", "sec", None),
    )
    return jax.shard_map(
        per_device,
        mesh=mesh,
        in_specs=placed,
        out_specs=P(("sec", "ep"), None, None),
        check_vma=False,
    )
```

```python
import functools
import math

import jax
import jax.numpy as jnp
from jax import lax
from jax.experimental import pallas as pl
from jax.experimental.pallas import tpu as pltpu
from jax.sharding import PartitionSpec as P

LAT = 512
ROPE = 64
VDIM = 128
STEPS = 4
TOPK = 8
LOADS = 4
BLK = 2048
SPAN = 8
AXES = ("sec", "ep")
NT = (((1,), (1,)), ((), ()))
BF = jnp.bfloat16
F32 = jnp.float32
VMEM_LIMIT = 16 * 1024 * 1024


def bit_orders(n):
    top = n.bit_length() - 2
    rest = list(range(1, top))
    return [top] + rest, rest[:2] + [top] + rest[2:]


def swap(x, n, step):
    orders = bit_orders(n)
    return lax.ppermute(x, AXES, [(d, d ^ (1 if step < 0 else 1 << orders[d & 1][step])) for d in range(n)])


def iota2(shape, axis):
    return lax.broadcasted_iota(jnp.int32, shape, axis)


def one_hot(columns, count):
    return (iota2(columns.shape, 1) == columns).astype(BF)


def pick(matrix, rows):
    return jnp.dot(matrix, rows, preferred_element_type=F32)


def attend_kernel(n, len_ref, q_hbm, new_hbm, keys_hbm, out_ref, q_ref, new_ref, keys_ref, m_ref, l_ref, acc_ref, small_sem, sem):
    rows = q_ref.shape[0]
    heads = rows // STEPS
    factor_base2 = (VDIM + ROPE) ** (-0.5) * math.log2(math.e)
    length = len_ref[0]
    blk = min(BLK, keys_ref.shape[1])

    def block_at(i):
        return pl.ds(pl.multiple_of(i * blk, blk), blk)

    def block_copy(i):
        return pltpu.make_async_copy(
            keys_hbm.at[:, block_at(i)], keys_ref.at[:, block_at(i)], sem.at[i]
        )

    def start(i):
        @pl.when(i * blk < length)
        def _():
            block_copy(i).start()

    q_copy = pltpu.make_async_copy(q_hbm, q_ref, small_sem.at[0])
    new_copy = pltpu.make_async_copy(new_hbm, new_ref, small_sem.at[1])
    q_copy.start()
    new_copy.start()
    start(0)
    start(1)
    r = iota2((rows, rows), 0)
    order = one_hot((r % STEPS) * heads + r // STEPS, rows)
    q_copy.wait()
    new_copy.wait()

    new = new_ref[...]
    s = lax.dot_general(q_ref[...], new, NT, preferred_element_type=F32)
    step = iota2(s.shape, 0) // heads
    s = jnp.where(iota2(s.shape, 1) <= step, s, -1e30)
    m = jnp.max(s, axis=1, keepdims=True)
    p = jnp.exp2((s - m) * factor_base2)
    m_ref[...] = m
    l_ref[...] = jnp.sum(p, axis=1, keepdims=True)
    acc_ref[...] = jnp.dot(p.astype(BF), new[:, :LAT], preferred_element_type=F32)

    def update(i, masked):
        start(i + 2)
        block_copy(i).wait()
        keys = keys_ref[:, block_at(i)]
        s = jnp.dot(q_ref[...], keys, preferred_element_type=F32)
        if masked:
            s = jnp.where(iota2(s.shape, 1) < length - i * blk, s, -1e30)
        m_old = m_ref[...]
        m = jnp.maximum(m_old, jnp.max(s, axis=1, keepdims=True))
        factor = jnp.exp2((m_old - m) * factor_base2)
        p = jnp.exp2((s - m) * factor_base2)
        m_ref[...] = m
        l_ref[...] = l_ref[...] * factor + jnp.sum(p, axis=1, keepdims=True)
        acc_ref[...] = acc_ref[...] * factor + lax.dot_general(
            p.astype(BF), keys[:LAT], NT, preferred_element_type=F32
        )

    full = length // blk

    @pl.loop(0, full)
    def _(i):
        update(i, False)

    @pl.when(full * blk < length)
    def _():
        update(full, True)

    out = (acc_ref[...] / l_ref[...]).astype(BF)
    out_ref[...] = pick(order, out).reshape(out_ref.shape).astype(BF)


def attend(n, length, q, new, keys):
    rows, width = q.shape
    cached = keys.shape[1]
    blocks = cached // min(BLK, cached)
    return pl.pallas_call(
        functools.partial(attend_kernel, n),
        in_specs=[pl.BlockSpec(memory_space=pltpu.SMEM)]
        + [pl.BlockSpec(memory_space=pl.ANY)] * 3,
        out_specs=pl.BlockSpec(memory_space=pltpu.VMEM),
        scratch_shapes=[
            pltpu.VMEM(q.shape, BF),
            pltpu.VMEM(new.shape, BF),
            pltpu.VMEM(keys.shape, BF),
            pltpu.VMEM((rows, 1), F32),
            pltpu.VMEM((rows, 1), F32),
            pltpu.VMEM((rows, LAT), F32),
            pltpu.SemaphoreType.DMA((2,)),
            pltpu.SemaphoreType.DMA((blocks,)),
        ],
        out_shape=jax.ShapeDtypeStruct((rows // STEPS, STEPS, LAT), BF),
        compiler_params=pltpu.CompilerParams(vmem_limit_bytes=56 * 1024 * 1024),
        cost_estimate=pl.CostEstimate(
            flops=2 * rows * cached * (width + LAT),
            bytes_accessed=2 * cached * width,
            transcendentals=rows * cached,
        ),
        name="attend",
    )(length, q, new, keys)


def source_rows(n, me, rows):
    r = iota2((rows, rows), 0)
    other = r // (rows // 2)
    count = n.bit_length() - 2
    masks = []
    for order in bit_orders(n):
        mask = jnp.zeros_like(r)
        for i, bit in enumerate(order):
            mask = mask | (((r // STEPS) >> (count - 1 - i)) & 1) << bit
        masks.append(mask)
    mask = jnp.where((me & 1) ^ other == 0, masks[0], masks[1])
    return (me ^ mask ^ other) * STEPS + r % STEPS


def heads_kernel(n, me_ref, latents_ref, uv_ref, out_ref, near_ref, far_ref):
    rows = n * STEPS
    values = jnp.dot(latents_ref[...], uv_ref[...], preferred_element_type=F32).astype(BF)
    values = pick(one_hot(source_rows(n, me_ref[0], rows), rows), values).astype(BF)
    part = out_ref.shape[1] // SPAN
    for p in range(SPAN):
        here = slice(p * part, (p + 1) * part)
        out = jnp.dot(values, out_ref[:, here], preferred_element_type=F32)
        near_ref[:, here] = out[: rows // 2]
        far_ref[:, here] = out[rows // 2 :].astype(BF)


def norm_kernel(n, *refs):
    kept_ref, got_ref, residual_ref, gain_ref, routes_ref, hidden_ref, out_ref = refs
    hidden = residual_ref[...].astype(F32) + kept_ref[...] + got_ref[...].astype(F32)
    hidden_ref[...] = hidden
    width = hidden.shape[1]
    mean_square = jnp.sum(hidden * hidden, axis=1, keepdims=True) / width
    normed = hidden * lax.rsqrt(mean_square + 1e-06) * gain_ref[...].astype(F32)
    out_ref[:, :width] = normed.astype(BF)
    out_ref[:, width:] = routes_ref[...]


def load_kernel(n, count, *refs):
    sources, targets, sem = refs[1 : 1 + count], refs[2 + count : 2 + 2 * count], refs[-1]
    copies = [pltpu.make_async_copy(refs[0], refs[1 + count], sem.at[0])]
    for source, target in zip(sources, targets):
        step = source.shape[0] // LOADS
        for j in range(LOADS):
            here = pl.ds(j * step, step)
            copies.append(
                pltpu.make_async_copy(source.at[here], target.at[here], sem.at[len(copies)])
            )
    for copy in copies:
        copy.start()
    for copy in copies:
        copy.wait()


def load(n, passed, arrays):
    return pl.pallas_call(
        functools.partial(load_kernel, n, len(arrays)),
        in_specs=[pl.BlockSpec(memory_space=pltpu.VMEM)]
        + [pl.BlockSpec(memory_space=pl.ANY)] * len(arrays),
        out_specs=[pl.BlockSpec(memory_space=pltpu.VMEM)] * (1 + len(arrays)),
        out_shape=[jax.ShapeDtypeStruct(a.shape, a.dtype) for a in [passed] + arrays],
        scratch_shapes=[pltpu.SemaphoreType.DMA((1 + LOADS * len(arrays),))],
        compiler_params=pltpu.CompilerParams(vmem_limit_bytes=28 * 1024 * 1024),
        cost_estimate=pl.CostEstimate(
            flops=0, bytes_accessed=sum(4 * a.size for a in arrays), transcendentals=0
        ),
        name="load",
    )(passed, *arrays)


def expert_kernel(n, me_ref, *refs, n_ep):
    blocks, (gate_ref, up_ref, down_ref, near_ref, far_ref) = refs[:4], refs[4:]
    rows = n * STEPS
    width, units = gate_ref.shape
    part = width // SPAN
    gate = jnp.zeros((rows, units), F32)
    up = jnp.zeros((rows, units), F32)
    for p in range(SPAN):
        here = slice(p * part, (p + 1) * part)
        x = jnp.concatenate([ref[:, here] for ref in blocks], axis=0)
        gate += jnp.dot(x, gate_ref[here], preferred_element_type=F32)
        up += jnp.dot(x, up_ref[here], preferred_element_type=F32)
    act = (gate * jax.nn.sigmoid(gate) * up).astype(BF)
    routes = jnp.concatenate([ref[:, width:] for ref in blocks], axis=0).astype(F32)
    scores = routes[:, TOPK : 2 * TOPK] + routes[:, 2 * TOPK : 3 * TOPK]
    chosen = jnp.where(routes[:, :TOPK] == (me_ref[0] % n_ep).astype(F32), scores, 0.0)
    coef = jnp.sum(chosen, axis=1, keepdims=True) / jnp.sum(scores, axis=1, keepdims=True) * 2.5
    for p in range(SPAN):
        here = slice(p * part, (p + 1) * part)
        out = jnp.dot(act, down_ref[:, here], preferred_element_type=F32) * coef
        near_ref[:, here] = out[: rows // 2]
        far_ref[:, here] = out[rows // 2 :].astype(BF)


def single(kernel, n, out_shape, scalars, arrays, name, flops):
    return pl.pallas_call(
        functools.partial(kernel, n),
        in_specs=[pl.BlockSpec(memory_space=pltpu.SMEM)] * len(scalars)
        + [pl.BlockSpec(memory_space=pltpu.VMEM)] * len(arrays),
        out_shape=out_shape,
        compiler_params=pltpu.CompilerParams(vmem_limit_bytes=VMEM_LIMIT),
        cost_estimate=pl.CostEstimate(
            flops=flops, bytes_accessed=sum(2 * a.size for a in arrays), transcendentals=0
        ),
        name=name,
    )(*scalars, *arrays)


def reduce_rows(near, far, n):
    kept, got = near, swap(far, n, -1)
    for step in range(n.bit_length() - 2):
        total = kept + got.astype(F32)
        half = total.shape[0] // 2
        kept, got = total[:half], swap(total[half:].astype(BF), n, step)
    return kept, got


def spread_rows(rows, n, beside):
    for step in reversed(range(1, n.bit_length() - 2)):
        got = swap(rows, n, step)
        rows = jnp.concatenate([rows, got], axis=0)
    got = swap(rows, n, 0)
    rows = beside(rows)
    return [rows, got, swap(rows, n, -1), swap(got, n, -1)]


def per_device(
    queries,
    new_latent,
    cache_latent,
    cache_len,
    route_ids,
    route_scores,
    residual,
    norm_gain,
    w_uv,
    w_out,
    w_gate,
    w_up,
    w_down,
):
    n_ep = lax.axis_size("ep")
    n = lax.axis_size("sec") * n_ep
    heads = queries.shape[2]
    width = residual.shape[2]
    rows = n * STEPS
    me_one = lax.axis_index(AXES).astype(jnp.int32).reshape(1)

    with jax.named_scope("attention"):
        latents = attend(
            n,
            cache_len,
            queries[0].reshape(STEPS * heads, queries.shape[3]),
            new_latent[0],
            jnp.swapaxes(cache_latent[0], 0, 1),
        )

    with jax.named_scope("heads"):
        latents = lax.all_to_all(latents, AXES, 0, 0, tiled=True)
        near, far = single(
            heads_kernel,
            n,
            [jax.ShapeDtypeStruct((rows // 2, width), dtype) for dtype in (F32, BF)],
            [me_one],
            [latents.reshape(rows, LAT), w_uv[0], w_out[0]],
            "heads",
            2 * rows * VDIM * (LAT + width),
        )
        terms = reduce_rows(near, far, n)

    with jax.named_scope("norm"):
        high = route_scores[0].astype(BF)
        low = (route_scores[0] - high.astype(F32)).astype(BF)
        routes = jnp.concatenate([route_ids[0].astype(BF), high, low], axis=1)
        routes = jnp.pad(routes, ((0, 0), (0, 128 - 3 * TOPK)))
        hidden, normed = single(
            norm_kernel,
            n,
            [
                jax.ShapeDtypeStruct((STEPS, width), F32),
                jax.ShapeDtypeStruct((STEPS, width + 128), BF),
            ],
            [],
            [*terms, residual[0], norm_gain.reshape(1, width), routes],
            "norm",
            8 * STEPS * width,
        )

    with jax.named_scope("spread"):
        loaded = []

        def load_beside(rows):
            rows, *weights = load(n, rows, [w_gate[0], w_up[0], w_down[0]])
            loaded.extend(weights)
            return rows

        blocks = spread_rows(normed, n, load_beside)

    with jax.named_scope("experts"):
        near, far = single(
            functools.partial(expert_kernel, n_ep=n_ep),
            n,
            [jax.ShapeDtypeStruct((rows // 2, width), dtype) for dtype in (F32, BF)],
            [me_one],
            blocks + loaded,
            "experts",
            6 * rows * width * w_gate.shape[2],
        )

    with jax.named_scope("collect"):
        kept, got = reduce_rows(near, far, n)
        return (hidden + kept + got.astype(F32)).astype(BF)[None]


def solution(mesh):
    placed = (
        P(("sec", "ep"), None, None, None),
        P(("sec", "ep"), None, None),
        P(("sec", "ep"), None, None),
        P(("sec", "ep")),
        P(("sec", "ep"), None, None),
        P(("sec", "ep"), None, None),
        P(("sec", "ep"), None, None),
        P(),
        P(("sec", "ep"), None, None),
        P(("sec", "ep"), None, None),
        P("ep", None, "sec"),
        P("ep", None, "sec"),
        P("ep", "sec", None),
    )
    return jax.shard_map(
        per_device,
        mesh=mesh,
        in_specs=placed,
        out_specs=P(("sec", "ep"), None, None),
        check_vma=False,
    )
```

```python
import functools
import math

import jax
import jax.numpy as jnp
from jax import lax
from jax.experimental import pallas as pl
from jax.experimental.pallas import tpu as pltpu
from jax.sharding import PartitionSpec as P

LAT = 512
ROPE = 64
VDIM = 128
STEPS = 4
TOPK = 8
BLK = 2048
SPAN = 8
AXES = ("sec", "ep")
NT = (((1,), (1,)), ((), ()))
BF = jnp.bfloat16
F32 = jnp.float32
VMEM_LIMIT = 16 * 1024 * 1024


def partners(n):
    chips = [(q >> 1) * (n // 2) + (q & 1) * 2 for q in range(4)]
    planes = [k * 4 for k in range(n // SPAN)]
    return [(chips, planes), (planes, chips) if len(planes) == 4 else (chips, planes)]


def swap(x, n, stage, i):
    return lax.ppermute(x, AXES, [(d, d ^ partners(n)[d & 1][stage][i]) for d in range(n)])


def swap_core(x, n):
    return lax.ppermute(x, AXES, [(d, d ^ 1) for d in range(n)])


def iota2(shape, axis):
    return lax.broadcasted_iota(jnp.int32, shape, axis)


def one_hot(columns, count):
    return (iota2(columns.shape, 1) == columns).astype(BF)


def pick(matrix, rows):
    return jnp.dot(matrix, rows, preferred_element_type=F32)


def attend_kernel(n, len_ref, q_hbm, new_hbm, keys_hbm, out_ref, q_ref, new_ref, keys_ref, m_ref, l_ref, acc_ref, small_sem, sem):
    rows = q_ref.shape[0]
    heads = rows // STEPS
    factor_base2 = (VDIM + ROPE) ** (-0.5) * math.log2(math.e)
    length = len_ref[0]
    blk = min(BLK, keys_ref.shape[1])

    def block_at(i):
        return pl.ds(pl.multiple_of(i * blk, blk), blk)

    def block_copy(i):
        return pltpu.make_async_copy(
            keys_hbm.at[:, block_at(i)], keys_ref.at[:, block_at(i)], sem.at[i]
        )

    def start(i):
        @pl.when(i * blk < length)
        def _():
            block_copy(i).start()

    q_copy = pltpu.make_async_copy(q_hbm, q_ref, small_sem.at[0])
    new_copy = pltpu.make_async_copy(new_hbm, new_ref, small_sem.at[1])
    q_copy.start()
    new_copy.start()
    start(0)
    start(1)
    r = iota2((rows, rows), 0)
    order = one_hot((r % STEPS) * heads + r // STEPS, rows)
    q_copy.wait()
    new_copy.wait()

    new = new_ref[...]
    s = lax.dot_general(q_ref[...], new, NT, preferred_element_type=F32)
    step = iota2(s.shape, 0) // heads
    s = jnp.where(iota2(s.shape, 1) <= step, s, -1e30)
    m = jnp.max(s, axis=1, keepdims=True)
    p = jnp.exp2((s - m) * factor_base2)
    m_ref[...] = m
    l_ref[...] = jnp.sum(p, axis=1, keepdims=True)
    acc_ref[...] = jnp.dot(p.astype(BF), new[:, :LAT], preferred_element_type=F32)

    def update(i, masked):
        start(i + 2)
        block_copy(i).wait()
        keys = keys_ref[:, block_at(i)]
        s = jnp.dot(q_ref[...], keys, preferred_element_type=F32)
        if masked:
            s = jnp.where(iota2(s.shape, 1) < length - i * blk, s, -1e30)
        m_old = m_ref[...]
        m = jnp.maximum(m_old, jnp.max(s, axis=1, keepdims=True))
        factor = jnp.exp2((m_old - m) * factor_base2)
        p = jnp.exp2((s - m) * factor_base2)
        m_ref[...] = m
        l_ref[...] = l_ref[...] * factor + jnp.sum(p, axis=1, keepdims=True)
        acc_ref[...] = acc_ref[...] * factor + lax.dot_general(
            p.astype(BF), keys[:LAT], NT, preferred_element_type=F32
        )

    full = length // blk

    @pl.loop(0, full)
    def _(i):
        update(i, False)

    @pl.when(full * blk < length)
    def _():
        update(full, True)

    out = (acc_ref[...] / l_ref[...]).astype(BF)
    out_ref[...] = pick(order, out).reshape(out_ref.shape).astype(BF)


def attend(n, length, q, new, keys):
    rows, width = q.shape
    cached = keys.shape[1]
    blocks = cached // min(BLK, cached)
    return pl.pallas_call(
        functools.partial(attend_kernel, n),
        in_specs=[pl.BlockSpec(memory_space=pltpu.SMEM)]
        + [pl.BlockSpec(memory_space=pl.ANY)] * 3,
        out_specs=pl.BlockSpec(memory_space=pltpu.VMEM),
        scratch_shapes=[
            pltpu.VMEM(q.shape, BF),
            pltpu.VMEM(new.shape, BF),
            pltpu.VMEM(keys.shape, BF),
            pltpu.VMEM((rows, 1), F32),
            pltpu.VMEM((rows, 1), F32),
            pltpu.VMEM((rows, LAT), F32),
            pltpu.SemaphoreType.DMA((2,)),
            pltpu.SemaphoreType.DMA((blocks,)),
        ],
        out_shape=jax.ShapeDtypeStruct((rows // STEPS, STEPS, LAT), BF),
        compiler_params=pltpu.CompilerParams(vmem_limit_bytes=56 * 1024 * 1024),
        cost_estimate=pl.CostEstimate(
            flops=2 * rows * cached * (width + LAT),
            bytes_accessed=2 * cached * width,
            transcendentals=rows * cached,
        ),
        name="attend",
    )(length, q, new, keys)


def source_rows(n, me, rows):
    r = iota2((rows, rows), 0)
    other = r // (rows // 2)
    masks = []
    for firsts, seconds in partners(n):
        i, j = (r // (len(seconds) * STEPS)) % len(firsts), (r // STEPS) % len(seconds)
        mask = jnp.zeros_like(r)
        for index, options in ((i, firsts), (j, seconds)):
            for value, option in enumerate(options):
                mask = mask | jnp.where(index == value, option, 0)
        masks.append(mask)
    mask = jnp.where((me & 1) ^ other == 0, masks[0], masks[1])
    return (me ^ mask ^ other) * STEPS + r % STEPS


def heads_kernel(n, me_ref, latents_ref, uv_ref, out_ref, near_ref, far_ref):
    rows = n * STEPS
    values = jnp.dot(latents_ref[...], uv_ref[...], preferred_element_type=F32).astype(BF)
    values = pick(one_hot(source_rows(n, me_ref[0], rows), rows), values).astype(BF)
    part = out_ref.shape[1] // SPAN
    for p in range(SPAN):
        here = slice(p * part, (p + 1) * part)
        out = jnp.dot(values, out_ref[:, here], preferred_element_type=F32)
        near_ref[:, here] = out[: rows // 2]
        far_ref[:, here] = out[rows // 2 :].astype(BF)


def norm_kernel(n, *refs):
    parts, (residual_ref, gain_ref, routes_ref, hidden_ref, out_ref) = refs[:-5], refs[-5:]
    hidden = residual_ref[...].astype(F32)
    for ref in parts:
        hidden += ref[...].astype(F32)
    hidden_ref[...] = hidden
    width = hidden.shape[1]
    mean_square = jnp.sum(hidden * hidden, axis=1, keepdims=True) / width
    normed = hidden * lax.rsqrt(mean_square + 1e-06) * gain_ref[...].astype(F32)
    out_ref[:, :width] = normed.astype(BF)
    out_ref[:, width:] = routes_ref[...]


def load_kernel(n, *refs):
    sources, targets, sem = refs[1:4], refs[5:8], refs[8]
    copies = [pltpu.make_async_copy(refs[0], refs[4], sem.at[12])]
    for i in range(3):
        step = sources[i].shape[0] // 4
        for j in range(4):
            here = pl.ds(j * step, step)
            copies.append(
                pltpu.make_async_copy(sources[i].at[here], targets[i].at[here], sem.at[4 * i + j])
            )
    for copy in copies:
        copy.start()
    for copy in copies:
        copy.wait()


def load(n, passed, arrays):
    return pl.pallas_call(
        functools.partial(load_kernel, n),
        in_specs=[pl.BlockSpec(memory_space=pltpu.VMEM)] + [pl.BlockSpec(memory_space=pl.ANY)] * 3,
        out_specs=[pl.BlockSpec(memory_space=pltpu.VMEM)] * 4,
        out_shape=[jax.ShapeDtypeStruct(a.shape, a.dtype) for a in [passed] + arrays],
        scratch_shapes=[pltpu.SemaphoreType.DMA((13,))],
        compiler_params=pltpu.CompilerParams(vmem_limit_bytes=28 * 1024 * 1024),
        cost_estimate=pl.CostEstimate(
            flops=0, bytes_accessed=sum(4 * a.size for a in arrays), transcendentals=0
        ),
        name="load_experts",
    )(passed, *arrays)


def expert_kernel(n, me_ref, *refs, n_ep):
    blocks, (gate_ref, up_ref, down_ref, near_ref, far_ref) = refs[:8], refs[8:]
    rows = n * STEPS
    width, units = gate_ref.shape
    part = width // SPAN
    gate = jnp.zeros((rows, units), F32)
    up = jnp.zeros((rows, units), F32)
    for p in range(SPAN):
        here = slice(p * part, (p + 1) * part)
        x = jnp.concatenate([ref[:, here] for ref in blocks], axis=0)
        gate += jnp.dot(x, gate_ref[here], preferred_element_type=F32)
        up += jnp.dot(x, up_ref[here], preferred_element_type=F32)
    act = (gate * jax.nn.sigmoid(gate) * up).astype(BF)
    routes = jnp.concatenate([ref[:, width:] for ref in blocks], axis=0).astype(F32)
    scores = routes[:, TOPK : 2 * TOPK] + routes[:, 2 * TOPK : 3 * TOPK]
    chosen = jnp.where(routes[:, :TOPK] == (me_ref[0] % n_ep).astype(F32), scores, 0.0)
    coef = jnp.sum(chosen, axis=1, keepdims=True) / jnp.sum(scores, axis=1, keepdims=True) * 2.5
    for p in range(SPAN):
        here = slice(p * part, (p + 1) * part)
        out = jnp.dot(act, down_ref[:, here], preferred_element_type=F32) * coef
        near_ref[:, here] = out[: rows // 2]
        far_ref[:, here] = out[rows // 2 :].astype(BF)


def single(kernel, n, out_shape, scalars, arrays, name, flops):
    return pl.pallas_call(
        functools.partial(kernel, n),
        in_specs=[pl.BlockSpec(memory_space=pltpu.SMEM)] * len(scalars)
        + [pl.BlockSpec(memory_space=pltpu.VMEM)] * len(arrays),
        out_shape=out_shape,
        compiler_params=pltpu.CompilerParams(vmem_limit_bytes=VMEM_LIMIT),
        cost_estimate=pl.CostEstimate(
            flops=flops, bytes_accessed=sum(2 * a.size for a in arrays), transcendentals=0
        ),
        name=name,
    )(*scalars, *arrays)


def reduce_rows(near, far, n):
    firsts, seconds = (len(masks) for masks in partners(n)[0])
    width = near.shape[1]
    total = near + swap_core(far, n).astype(F32)
    total = total.reshape(firsts, seconds * STEPS, width)
    kept = total[0]
    for i in reversed(range(1, firsts)):
        kept = kept + swap(total[i].astype(BF), n, 0, i).astype(F32)
    kept = kept.reshape(seconds, STEPS, width)
    return [kept[0]] + [swap(kept[j].astype(BF), n, 1, j) for j in range(1, seconds)]


def per_device(
    queries,
    new_latent,
    cache_latent,
    cache_len,
    route_ids,
    route_scores,
    residual,
    norm_gain,
    w_uv,
    w_out,
    w_gate,
    w_up,
    w_down,
):
    n_ep = lax.axis_size("ep")
    n = lax.axis_size("sec") * n_ep
    heads = queries.shape[2]
    width = residual.shape[2]
    rows = n * STEPS
    me_one = lax.axis_index(AXES).astype(jnp.int32).reshape(1)

    with jax.named_scope("attention"):
        latents = attend(
            n,
            cache_len,
            queries[0].reshape(STEPS * heads, queries.shape[3]),
            new_latent[0],
            jnp.swapaxes(cache_latent[0], 0, 1),
        )

    with jax.named_scope("heads"):
        latents = lax.all_to_all(latents, AXES, 0, 0, tiled=True)
        near, far = single(
            heads_kernel,
            n,
            [jax.ShapeDtypeStruct((rows // 2, width), dtype) for dtype in (F32, BF)],
            [me_one],
            [latents.reshape(rows, LAT), w_uv[0], w_out[0]],
            "heads",
            2 * rows * VDIM * (LAT + width),
        )
        parts = reduce_rows(near, far, n)

    with jax.named_scope("norm"):
        high = route_scores[0].astype(BF)
        low = (route_scores[0] - high.astype(F32)).astype(BF)
        routes = jnp.concatenate([route_ids[0].astype(BF), high, low], axis=1)
        routes = jnp.pad(routes, ((0, 0), (0, 128 - 3 * TOPK)))
        hidden, normed = single(
            norm_kernel,
            n,
            [
                jax.ShapeDtypeStruct((STEPS, width), F32),
                jax.ShapeDtypeStruct((STEPS, width + 128), BF),
            ],
            [],
            parts + [residual[0], norm_gain.reshape(1, width), routes],
            "norm",
            8 * STEPS * width,
        )

    with jax.named_scope("spread"):
        along = [normed] + [swap(normed, n, 1, j) for j in range(1, n // SPAN)]
        along = jnp.concatenate(along, axis=0)
        blocks = [along] + [swap(along, n, 0, i) for i in range(1, 4)]
        along, *weights = load(n, along, [w_gate[0], w_up[0], w_down[0]])
        blocks = blocks + [swap_core(x, n) for x in [along] + blocks[1:]]

    with jax.named_scope("experts"):
        near, far = single(
            functools.partial(expert_kernel, n_ep=n_ep),
            n,
            [jax.ShapeDtypeStruct((rows // 2, width), dtype) for dtype in (F32, BF)],
            [me_one],
            blocks + weights,
            "experts",
            6 * rows * width * w_gate.shape[2],
        )

    with jax.named_scope("collect"):
        result = hidden
        for term in reduce_rows(near, far, n):
            result = result + term.astype(F32)
        return result.astype(BF)[None]


def solution(mesh):
    placed = (
        P(("sec", "ep"), None, None, None),
        P(("sec", "ep"), None, None),
        P(("sec", "ep"), None, None),
        P(("sec", "ep")),
        P(("sec", "ep"), None, None),
        P(("sec", "ep"), None, None),
        P(("sec", "ep"), None, None),
        P(),
        P(("sec", "ep"), None, None),
        P(("sec", "ep"), None, None),
        P("ep", None, "sec"),
        P("ep", None, "sec"),
        P("ep", "sec", None),
    )
    return jax.shard_map(
        per_device,
        mesh=mesh,
        in_specs=placed,
        out_specs=P(("sec", "ep"), None, None),
        check_vma=False,
    )
```

```python
import functools
import math

import jax
import jax.numpy as jnp
from jax import lax
from jax.experimental import pallas as pl
from jax.experimental.pallas import tpu as pltpu
from jax.sharding import PartitionSpec as P

LAT = 512
ROPE = 64
VDIM = 128
STEPS = 4
TOPK = 8
BLK = 2048
SPAN = 8
AXES = ("sec", "ep")
NT = (((1,), (1,)), ((), ()))
BF = jnp.bfloat16
F32 = jnp.float32
VMEM_LIMIT = 16 * 1024 * 1024
LOAD_LIMIT, EXPERT_LIMIT = 34, 30


def partners(n):
    chips = [(q >> 1) * (n // 2) + (q & 1) * 2 for q in range(4)]
    planes = [k * 4 for k in range(n // SPAN)]
    return [(chips, planes), (planes, chips) if len(planes) == 4 else (chips, planes)]


def swap(x, n, stage, i):
    return lax.ppermute(x, AXES, [(d, d ^ partners(n)[d & 1][stage][i]) for d in range(n)])


def swap_core(x, n):
    return lax.ppermute(x, AXES, [(d, d ^ 1) for d in range(n)])


def iota2(shape, axis):
    return lax.broadcasted_iota(jnp.int32, shape, axis)


def one_hot(columns, count):
    return (iota2(columns.shape, 1) == columns).astype(BF)


def pick(matrix, rows):
    return jnp.dot(matrix, rows, preferred_element_type=F32)


def attend_kernel(n, len_ref, q_hbm, new_hbm, keys_hbm, out_ref, q_ref, new_ref, keys_ref, m_ref, l_ref, acc_ref, small_sem, sem):
    rows = q_ref.shape[0]
    heads = rows // STEPS
    factor_base2 = (VDIM + ROPE) ** (-0.5) * math.log2(math.e)
    length = len_ref[0]
    blk = min(BLK, keys_ref.shape[1])

    def block_at(i):
        return pl.ds(pl.multiple_of(i * blk, blk), blk)

    def block_copy(i):
        return pltpu.make_async_copy(
            keys_hbm.at[:, block_at(i)], keys_ref.at[:, block_at(i)], sem.at[i]
        )

    def start(i):
        @pl.when(i * blk < length)
        def _():
            block_copy(i).start()

    q_copy = pltpu.make_async_copy(q_hbm, q_ref, small_sem.at[0])
    new_copy = pltpu.make_async_copy(new_hbm, new_ref, small_sem.at[1])
    q_copy.start()
    new_copy.start()
    start(0)
    start(1)
    r = iota2((rows, rows), 0)
    order = one_hot((r % STEPS) * heads + r // STEPS, rows)
    q_copy.wait()
    new_copy.wait()

    new = new_ref[...]
    s = lax.dot_general(q_ref[...], new, NT, preferred_element_type=F32)
    step = iota2(s.shape, 0) // heads
    s = jnp.where(iota2(s.shape, 1) <= step, s, -1e30)
    m = jnp.max(s, axis=1, keepdims=True)
    p = jnp.exp2((s - m) * factor_base2)
    m_ref[...] = m
    l_ref[...] = jnp.sum(p, axis=1, keepdims=True)
    acc_ref[...] = jnp.dot(p.astype(BF), new[:, :LAT], preferred_element_type=F32)

    def update(i, masked):
        start(i + 2)
        block_copy(i).wait()
        keys = keys_ref[:, block_at(i)]
        s = jnp.dot(q_ref[...], keys, preferred_element_type=F32)
        if masked:
            s = jnp.where(iota2(s.shape, 1) < length - i * blk, s, -1e30)
        m_old = m_ref[...]
        m = jnp.maximum(m_old, jnp.max(s, axis=1, keepdims=True))
        factor = jnp.exp2((m_old - m) * factor_base2)
        p = jnp.exp2((s - m) * factor_base2)
        m_ref[...] = m
        l_ref[...] = l_ref[...] * factor + jnp.sum(p, axis=1, keepdims=True)
        acc_ref[...] = acc_ref[...] * factor + lax.dot_general(
            p.astype(BF), keys[:LAT], NT, preferred_element_type=F32
        )

    full = length // blk

    @pl.loop(0, full)
    def _(i):
        update(i, False)

    @pl.when(full * blk < length)
    def _():
        update(full, True)

    out = (acc_ref[...] / l_ref[...]).astype(BF)
    out_ref[...] = pick(order, out).reshape(out_ref.shape).astype(BF)


def attend(n, length, q, new, keys):
    rows, width = q.shape
    cached = keys.shape[1]
    blocks = cached // min(BLK, cached)
    return pl.pallas_call(
        functools.partial(attend_kernel, n),
        in_specs=[pl.BlockSpec(memory_space=pltpu.SMEM)]
        + [pl.BlockSpec(memory_space=pl.ANY)] * 3,
        out_specs=pl.BlockSpec(memory_space=pltpu.VMEM),
        scratch_shapes=[
            pltpu.VMEM(q.shape, BF),
            pltpu.VMEM(new.shape, BF),
            pltpu.VMEM(keys.shape, BF),
            pltpu.VMEM((rows, 1), F32),
            pltpu.VMEM((rows, 1), F32),
            pltpu.VMEM((rows, LAT), F32),
            pltpu.SemaphoreType.DMA((2,)),
            pltpu.SemaphoreType.DMA((blocks,)),
        ],
        out_shape=jax.ShapeDtypeStruct((rows // STEPS, STEPS, LAT), BF),
        compiler_params=pltpu.CompilerParams(vmem_limit_bytes=56 * 1024 * 1024),
        cost_estimate=pl.CostEstimate(
            flops=2 * rows * cached * (width + LAT),
            bytes_accessed=2 * cached * width,
            transcendentals=rows * cached,
        ),
        name="attend",
    )(length, q, new, keys)


def source_rows(n, me, rows):
    r = iota2((rows, rows), 0)
    other = r // (rows // 2)
    masks = []
    for firsts, seconds in partners(n):
        i, j = (r // (len(seconds) * STEPS)) % len(firsts), (r // STEPS) % len(seconds)
        mask = jnp.zeros_like(r)
        for index, options in ((i, firsts), (j, seconds)):
            for value, option in enumerate(options):
                mask = mask | jnp.where(index == value, option, 0)
        masks.append(mask)
    mask = jnp.where((me & 1) ^ other == 0, masks[0], masks[1])
    return (me ^ mask ^ other) * STEPS + r % STEPS


def heads_kernel(n, me_ref, latents_ref, uv_ref, out_ref, near_ref, far_ref):
    rows = n * STEPS
    values = jnp.dot(latents_ref[...], uv_ref[...], preferred_element_type=F32).astype(BF)
    values = pick(one_hot(source_rows(n, me_ref[0], rows), rows), values).astype(BF)
    part = out_ref.shape[1] // SPAN
    for p in range(SPAN):
        here = slice(p * part, (p + 1) * part)
        out = jnp.dot(values, out_ref[:, here], preferred_element_type=F32)
        near_ref[:, here] = out[: rows // 2]
        far_ref[:, here] = out[rows // 2 :].astype(BF)


def norm_kernel(n, *refs):
    parts, (residual_ref, gain_ref, routes_ref, hidden_ref, out_ref) = refs[:-5], refs[-5:]
    hidden = residual_ref[...].astype(F32)
    for ref in parts:
        hidden += ref[...].astype(F32)
    hidden_ref[...] = hidden
    width = hidden.shape[1]
    mean_square = jnp.sum(hidden * hidden, axis=1, keepdims=True) / width
    normed = hidden * lax.rsqrt(mean_square + 1e-06) * gain_ref[...].astype(F32)
    out_ref[:, :width] = normed.astype(BF)
    out_ref[:, width:] = routes_ref[...]


def load_kernel(n, *refs):
    sources, targets, sem = refs[1:3], refs[4:6], refs[6]
    copies = [pltpu.make_async_copy(refs[0], refs[3], sem.at[16])]
    for i in range(2):
        step = sources[i].shape[0] // 8
        for j in range(8):
            here = pl.ds(j * step, step)
            copies.append(
                pltpu.make_async_copy(sources[i].at[here], targets[i].at[here], sem.at[8 * i + j])
            )
    for copy in copies:
        copy.start()
    for copy in copies:
        copy.wait()


def load(n, passed, arrays):
    return pl.pallas_call(
        functools.partial(load_kernel, n),
        in_specs=[pl.BlockSpec(memory_space=pltpu.VMEM)] + [pl.BlockSpec(memory_space=pl.ANY)] * 2,
        out_specs=[pl.BlockSpec(memory_space=pltpu.VMEM)] * 3,
        out_shape=[jax.ShapeDtypeStruct(a.shape, a.dtype) for a in [passed] + arrays],
        scratch_shapes=[pltpu.SemaphoreType.DMA((17,))],
        compiler_params=pltpu.CompilerParams(vmem_limit_bytes=LOAD_LIMIT * 1024 * 1024),
        cost_estimate=pl.CostEstimate(
            flops=0, bytes_accessed=sum(4 * a.size for a in arrays), transcendentals=0
        ),
        name="load_experts",
    )(passed, *arrays)


def expert_kernel(n, n_ep, me_ref, *refs):
    blocks, (gate_ref, up_ref, down_hbm, near_ref, far_ref, down_ref, sem) = refs[:8], refs[8:]
    step = down_ref.shape[0] // 8
    copies = []
    for j in range(8):
        here = pl.ds(j * step, step)
        copies.append(pltpu.make_async_copy(down_hbm.at[here], down_ref.at[here], sem.at[j]))
    for copy in copies:
        copy.start()
    rows = n * STEPS
    width, units = gate_ref.shape
    part = width // SPAN
    gate = jnp.zeros((rows, units), F32)
    up = jnp.zeros((rows, units), F32)
    for p in range(SPAN):
        here = slice(p * part, (p + 1) * part)
        x = jnp.concatenate([ref[:, here] for ref in blocks], axis=0)
        gate += jnp.dot(x, gate_ref[here], preferred_element_type=F32)
        up += jnp.dot(x, up_ref[here], preferred_element_type=F32)
    act = (gate * jax.nn.sigmoid(gate) * up).astype(BF)
    routes = jnp.concatenate([ref[:, width:] for ref in blocks], axis=0).astype(F32)
    scores = routes[:, TOPK : 2 * TOPK] + routes[:, 2 * TOPK : 3 * TOPK]
    chosen = jnp.where(routes[:, :TOPK] == (me_ref[0] % n_ep).astype(F32), scores, 0.0)
    coef = jnp.sum(chosen, axis=1, keepdims=True) / jnp.sum(scores, axis=1, keepdims=True) * 2.5
    for copy in copies:
        copy.wait()
    for p in range(SPAN):
        here = slice(p * part, (p + 1) * part)
        out = jnp.dot(act, down_ref[:, here], preferred_element_type=F32) * coef
        near_ref[:, here] = out[: rows // 2]
        far_ref[:, here] = out[rows // 2 :].astype(BF)


def run_experts(n, n_ep, me, blocks, gate, up, down):
    rows = n * STEPS
    units, width = down.shape
    return pl.pallas_call(
        functools.partial(expert_kernel, n, n_ep),
        in_specs=[pl.BlockSpec(memory_space=pltpu.SMEM)]
        + [pl.BlockSpec(memory_space=pltpu.VMEM)] * (len(blocks) + 2)
        + [pl.BlockSpec(memory_space=pl.ANY)],
        out_shape=[jax.ShapeDtypeStruct((rows // 2, width), dtype) for dtype in (F32, BF)],
        scratch_shapes=[pltpu.VMEM(down.shape, BF), pltpu.SemaphoreType.DMA((8,))],
        compiler_params=pltpu.CompilerParams(vmem_limit_bytes=EXPERT_LIMIT * 1024 * 1024),
        cost_estimate=pl.CostEstimate(
            flops=6 * rows * width * units,
            bytes_accessed=6 * width * units,
            transcendentals=rows * units,
        ),
        name="experts",
    )(me, *blocks, gate, up, down)


def single(kernel, n, out_shape, scalars, arrays, name, flops):
    return pl.pallas_call(
        functools.partial(kernel, n),
        in_specs=[pl.BlockSpec(memory_space=pltpu.SMEM)] * len(scalars)
        + [pl.BlockSpec(memory_space=pltpu.VMEM)] * len(arrays),
        out_shape=out_shape,
        compiler_params=pltpu.CompilerParams(vmem_limit_bytes=VMEM_LIMIT),
        cost_estimate=pl.CostEstimate(
            flops=flops, bytes_accessed=sum(2 * a.size for a in arrays), transcendentals=0
        ),
        name=name,
    )(*scalars, *arrays)


def reduce_rows(near, far, n, beside=lambda rows: rows):
    firsts, seconds = (len(masks) for masks in partners(n)[0])
    width = near.shape[1]
    total = near + swap_core(far, n).astype(F32)
    total = total.reshape(firsts, seconds * STEPS, width)
    got = [swap(total[i].astype(BF), n, 0, i) for i in range(1, firsts)]
    kept = beside(total[0])
    for term in reversed(got):
        kept = kept + term.astype(F32)
    kept = kept.reshape(seconds, STEPS, width)
    return [kept[0]] + [swap(kept[j].astype(BF), n, 1, j) for j in range(1, seconds)]


def per_device(
    queries,
    new_latent,
    cache_latent,
    cache_len,
    route_ids,
    route_scores,
    residual,
    norm_gain,
    w_uv,
    w_out,
    w_gate,
    w_up,
    w_down,
):
    n_ep = lax.axis_size("ep")
    n = lax.axis_size("sec") * n_ep
    heads = queries.shape[2]
    width = residual.shape[2]
    rows = n * STEPS
    me_one = lax.axis_index(AXES).astype(jnp.int32).reshape(1)

    with jax.named_scope("attention"):
        latents = attend(
            n,
            cache_len,
            queries[0].reshape(STEPS * heads, queries.shape[3]),
            new_latent[0],
            jnp.swapaxes(cache_latent[0], 0, 1),
        )

    with jax.named_scope("heads"):
        latents = lax.all_to_all(latents, AXES, 0, 0, tiled=True)
        near, far = single(
            heads_kernel,
            n,
            [jax.ShapeDtypeStruct((rows // 2, width), dtype) for dtype in (F32, BF)],
            [me_one],
            [latents.reshape(rows, LAT), w_uv[0], w_out[0]],
            "heads",
            2 * rows * VDIM * (LAT + width),
        )
        loaded = []

        def load_beside(rows):
            rows, *weights = load(n, rows, [w_gate[0], w_up[0]])
            loaded.extend(weights)
            return rows

        parts = reduce_rows(near, far, n, load_beside)

    with jax.named_scope("norm"):
        high = route_scores[0].astype(BF)
        low = (route_scores[0] - high.astype(F32)).astype(BF)
        routes = jnp.concatenate([route_ids[0].astype(BF), high, low], axis=1)
        routes = jnp.pad(routes, ((0, 0), (0, 128 - 3 * TOPK)))
        hidden, normed = single(
            norm_kernel,
            n,
            [
                jax.ShapeDtypeStruct((STEPS, width), F32),
                jax.ShapeDtypeStruct((STEPS, width + 128), BF),
            ],
            [],
            parts + [residual[0], norm_gain.reshape(1, width), routes],
            "norm",
            8 * STEPS * width,
        )

    with jax.named_scope("spread"):
        along = [normed] + [swap(normed, n, 1, j) for j in range(1, n // SPAN)]
        along = jnp.concatenate(along, axis=0)
        blocks = [along] + [swap(along, n, 0, i) for i in range(1, 4)]
        blocks = blocks + [swap_core(x, n) for x in blocks]

    with jax.named_scope("experts"):
        near, far = run_experts(n, n_ep, me_one, blocks, *loaded, w_down[0])

    with jax.named_scope("collect"):
        result = hidden
        for term in reduce_rows(near, far, n):
            result = result + term.astype(F32)
        return result.astype(BF)[None]


def solution(mesh):
    placed = (
        P(("sec", "ep"), None, None, None),
        P(("sec", "ep"), None, None),
        P(("sec", "ep"), None, None),
        P(("sec", "ep")),
        P(("sec", "ep"), None, None),
        P(("sec", "ep"), None, None),
        P(("sec", "ep"), None, None),
        P(),
        P(("sec", "ep"), None, None),
        P(("sec", "ep"), None, None),
        P("ep", None, "sec"),
        P("ep", None, "sec"),
        P("ep", "sec", None),
    )
    return jax.shard_map(
        per_device,
        mesh=mesh,
        in_specs=placed,
        out_specs=P(("sec", "ep"), None, None),
        check_vma=False,
    )
```

```python
import functools
import math

import jax
import jax.numpy as jnp
from jax import lax
from jax.experimental import pallas as pl
from jax.experimental.pallas import tpu as pltpu
from jax.sharding import PartitionSpec as P

LAT = 512
ROPE = 64
VDIM = 128
STEPS = 4
TOPK = 8
BLK = 2048
SPAN = 8
AXES = ("sec", "ep")
NT = (((1,), (1,)), ((), ()))
BF = jnp.bfloat16
F32 = jnp.float32
VMEM_LIMIT = 16 * 1024 * 1024
LOAD_LIMIT = 28


def partners(n):
    chips = [(q >> 1) * (n // 2) + (q & 1) * 2 for q in range(4)]
    planes = [k * 4 for k in range(n // SPAN)]
    return [(chips, planes), (planes, chips) if len(planes) == 4 else (chips, planes)]


def swap(x, n, stage, i):
    return lax.ppermute(x, AXES, [(d, d ^ partners(n)[d & 1][stage][i]) for d in range(n)])


def swap_core(x, n):
    return lax.ppermute(x, AXES, [(d, d ^ 1) for d in range(n)])


def iota2(shape, axis):
    return lax.broadcasted_iota(jnp.int32, shape, axis)


def one_hot(columns, count):
    return (iota2(columns.shape, 1) == columns).astype(BF)


def pick(matrix, rows):
    return jnp.dot(matrix, rows, preferred_element_type=F32)


def attend_kernel(n, len_ref, me_ref, q_hbm, new_hbm, keys_hbm, keep_ref, give_ref, q_ref, new_ref, keys_ref, m_ref, l_ref, acc_ref, small_sem, sem):
    rows = q_ref.shape[0]
    heads = rows // STEPS
    factor_base2 = (VDIM + ROPE) ** (-0.5) * math.log2(math.e)
    length = len_ref[0]
    blk = min(BLK, keys_ref.shape[1])

    def block_at(i):
        return pl.ds(pl.multiple_of(i * blk, blk), blk)

    def block_copy(i):
        return pltpu.make_async_copy(
            keys_hbm.at[:, block_at(i)], keys_ref.at[:, block_at(i)], sem.at[i]
        )

    def start(i):
        @pl.when(i * blk < length)
        def _():
            block_copy(i).start()

    q_copy = pltpu.make_async_copy(q_hbm, q_ref, small_sem.at[0])
    new_copy = pltpu.make_async_copy(new_hbm, new_ref, small_sem.at[1])
    q_copy.start()
    new_copy.start()
    start(0)
    start(1)
    r = iota2((rows, rows), 0)
    head = (r // STEPS) % (n // 2) * 2 + (r // (rows // 2) ^ (me_ref[0] & 1))
    order = one_hot((r % STEPS) * heads + head, rows)
    q_copy.wait()
    new_copy.wait()

    new = new_ref[...]
    s = lax.dot_general(q_ref[...], new, NT, preferred_element_type=F32)
    step = iota2(s.shape, 0) // heads
    s = jnp.where(iota2(s.shape, 1) <= step, s, -1e30)
    m = jnp.max(s, axis=1, keepdims=True)
    p = jnp.exp2((s - m) * factor_base2)
    m_ref[...] = m
    l_ref[...] = jnp.sum(p, axis=1, keepdims=True)
    acc_ref[...] = jnp.dot(p.astype(BF), new[:, :LAT], preferred_element_type=F32)

    def update(i, masked):
        start(i + 2)
        block_copy(i).wait()
        keys = keys_ref[:, block_at(i)]
        s = jnp.dot(q_ref[...], keys, preferred_element_type=F32)
        if masked:
            s = jnp.where(iota2(s.shape, 1) < length - i * blk, s, -1e30)
        m_old = m_ref[...]
        m = jnp.maximum(m_old, jnp.max(s, axis=1, keepdims=True))
        factor = jnp.exp2((m_old - m) * factor_base2)
        p = jnp.exp2((s - m) * factor_base2)
        m_ref[...] = m
        l_ref[...] = l_ref[...] * factor + jnp.sum(p, axis=1, keepdims=True)
        acc_ref[...] = acc_ref[...] * factor + lax.dot_general(
            p.astype(BF), keys[:LAT], NT, preferred_element_type=F32
        )

    full = length // blk

    @pl.loop(0, full)
    def _(i):
        update(i, False)

    @pl.when(full * blk < length)
    def _():
        update(full, True)

    out = (acc_ref[...] / l_ref[...]).astype(BF)
    out = pick(order, out)
    keep_ref[...] = out[: rows // 2].reshape(keep_ref.shape).astype(BF)
    give_ref[...] = out[rows // 2 :].reshape(give_ref.shape).astype(BF)


def attend(n, length, me, q, new, keys):
    rows, width = q.shape
    cached = keys.shape[1]
    blocks = cached // min(BLK, cached)
    return pl.pallas_call(
        functools.partial(attend_kernel, n),
        in_specs=[pl.BlockSpec(memory_space=pltpu.SMEM)] * 2
        + [pl.BlockSpec(memory_space=pl.ANY)] * 3,
        out_specs=[pl.BlockSpec(memory_space=pltpu.VMEM)] * 2,
        scratch_shapes=[
            pltpu.VMEM(q.shape, BF),
            pltpu.VMEM(new.shape, BF),
            pltpu.VMEM(keys.shape, BF),
            pltpu.VMEM((rows, 1), F32),
            pltpu.VMEM((rows, 1), F32),
            pltpu.VMEM((rows, LAT), F32),
            pltpu.SemaphoreType.DMA((2,)),
            pltpu.SemaphoreType.DMA((blocks,)),
        ],
        out_shape=[jax.ShapeDtypeStruct((rows // STEPS // 2, STEPS, LAT), BF)] * 2,
        compiler_params=pltpu.CompilerParams(vmem_limit_bytes=56 * 1024 * 1024),
        cost_estimate=pl.CostEstimate(
            flops=2 * rows * cached * (width + LAT),
            bytes_accessed=2 * cached * width,
            transcendentals=rows * cached,
        ),
        name="attend",
    )(length, me, q, new, keys)


def source_rows(n, me, rows):
    r = iota2((rows, rows), 0)
    other = r // (rows // 2)
    masks = []
    for firsts, seconds in partners(n):
        i, j = (r // (len(seconds) * STEPS)) % len(firsts), (r // STEPS) % len(seconds)
        mask = jnp.zeros_like(r)
        for index, options in ((i, firsts), (j, seconds)):
            for value, option in enumerate(options):
                mask = mask | jnp.where(index == value, option, 0)
        masks.append(mask)
    mask = jnp.where((me & 1) ^ other == 0, masks[0], masks[1])
    device = me ^ mask ^ other
    return (device >> 1) * 2 * STEPS + ((device ^ me) & 1) * STEPS + r % STEPS


def heads_kernel(n, me_ref, latents_ref, uv_ref, out_ref, near_ref, far_ref):
    rows = n * STEPS
    values = jnp.dot(latents_ref[...], uv_ref[...], preferred_element_type=F32).astype(BF)
    values = pick(one_hot(source_rows(n, me_ref[0], rows), rows), values).astype(BF)
    part = out_ref.shape[1] // SPAN
    for p in range(SPAN):
        here = slice(p * part, (p + 1) * part)
        out = jnp.dot(values, out_ref[:, here], preferred_element_type=F32)
        near_ref[:, here] = out[: rows // 2]
        far_ref[:, here] = out[rows // 2 :].astype(BF)


def norm_kernel(n, *refs):
    parts, (residual_ref, gain_ref, routes_ref, hidden_ref, out_ref) = refs[:-5], refs[-5:]
    hidden = residual_ref[...].astype(F32)
    for ref in parts:
        hidden += ref[...].astype(F32)
    hidden_ref[...] = hidden
    width = hidden.shape[1]
    mean_square = jnp.sum(hidden * hidden, axis=1, keepdims=True) / width
    normed = hidden * lax.rsqrt(mean_square + 1e-06) * gain_ref[...].astype(F32)
    out_ref[:, :width] = normed.astype(BF)
    out_ref[:, width:] = routes_ref[...]


def load_kernel(n, *refs):
    sources, targets, sem = refs[1:4], refs[5:8], refs[8]
    copies = [pltpu.make_async_copy(refs[0], refs[4], sem.at[24])]
    for i in range(3):
        step = sources[i].shape[0] // 8
        for j in range(8):
            here = pl.ds(j * step, step)
            copies.append(
                pltpu.make_async_copy(sources[i].at[here], targets[i].at[here], sem.at[8 * i + j])
            )
    for copy in copies:
        copy.start()
    for copy in copies:
        copy.wait()


def load(n, passed, arrays):
    return pl.pallas_call(
        functools.partial(load_kernel, n),
        in_specs=[pl.BlockSpec(memory_space=pltpu.VMEM)] + [pl.BlockSpec(memory_space=pl.ANY)] * 3,
        out_specs=[pl.BlockSpec(memory_space=pltpu.VMEM)] * 4,
        out_shape=[jax.ShapeDtypeStruct(a.shape, a.dtype) for a in [passed] + arrays],
        scratch_shapes=[pltpu.SemaphoreType.DMA((25,))],
        compiler_params=pltpu.CompilerParams(vmem_limit_bytes=LOAD_LIMIT * 1024 * 1024),
        cost_estimate=pl.CostEstimate(
            flops=0, bytes_accessed=sum(4 * a.size for a in arrays), transcendentals=0
        ),
        name="load_experts",
    )(passed, *arrays)


def expert_kernel(n, me_ref, *refs, n_ep):
    blocks, (gate_ref, up_ref, down_ref, near_ref, far_ref) = refs[:8], refs[8:]
    rows = n * STEPS
    width, units = gate_ref.shape
    part = width // SPAN
    gate = jnp.zeros((rows, units), F32)
    up = jnp.zeros((rows, units), F32)
    for p in range(SPAN):
        here = slice(p * part, (p + 1) * part)
        x = jnp.concatenate([ref[:, here] for ref in blocks], axis=0)
        gate += jnp.dot(x, gate_ref[here], preferred_element_type=F32)
        up += jnp.dot(x, up_ref[here], preferred_element_type=F32)
    act = (gate * jax.nn.sigmoid(gate) * up).astype(BF)
    routes = jnp.concatenate([ref[:, width:] for ref in blocks], axis=0).astype(F32)
    scores = routes[:, TOPK : 2 * TOPK] + routes[:, 2 * TOPK : 3 * TOPK]
    chosen = jnp.where(routes[:, :TOPK] == (me_ref[0] % n_ep).astype(F32), scores, 0.0)
    coef = jnp.sum(chosen, axis=1, keepdims=True) / jnp.sum(scores, axis=1, keepdims=True) * 2.5
    for p in range(SPAN):
        here = slice(p * part, (p + 1) * part)
        out = jnp.dot(act, down_ref[:, here], preferred_element_type=F32) * coef
        near_ref[:, here] = out[: rows // 2]
        far_ref[:, here] = out[rows // 2 :].astype(BF)


def single(kernel, n, out_shape, scalars, arrays, name, flops):
    return pl.pallas_call(
        functools.partial(kernel, n),
        in_specs=[pl.BlockSpec(memory_space=pltpu.SMEM)] * len(scalars)
        + [pl.BlockSpec(memory_space=pltpu.VMEM)] * len(arrays),
        out_shape=out_shape,
        compiler_params=pltpu.CompilerParams(vmem_limit_bytes=VMEM_LIMIT),
        cost_estimate=pl.CostEstimate(
            flops=flops, bytes_accessed=sum(2 * a.size for a in arrays), transcendentals=0
        ),
        name=name,
    )(*scalars, *arrays)


def reduce_rows(near, far, n, beside=lambda rows: rows):
    firsts, seconds = (len(masks) for masks in partners(n)[0])
    width = near.shape[1]
    total = near + swap_core(far, n).astype(F32)
    total = total.reshape(firsts, seconds * STEPS, width)
    got = [swap(total[i].astype(BF), n, 0, i) for i in range(1, firsts)]
    kept = beside(total[0])
    for term in reversed(got):
        kept = kept + term.astype(F32)
    kept = kept.reshape(seconds, STEPS, width)
    return [kept[0]] + [swap(kept[j].astype(BF), n, 1, j) for j in range(1, seconds)]


def per_device(
    queries,
    new_latent,
    cache_latent,
    cache_len,
    route_ids,
    route_scores,
    residual,
    norm_gain,
    w_uv,
    w_out,
    w_gate,
    w_up,
    w_down,
):
    n_ep = lax.axis_size("ep")
    n = lax.axis_size("sec") * n_ep
    heads = queries.shape[2]
    width = residual.shape[2]
    rows = n * STEPS
    me_one = lax.axis_index(AXES).astype(jnp.int32).reshape(1)

    with jax.named_scope("attention"):
        latents, others = attend(
            n,
            cache_len,
            me_one,
            queries[0].reshape(STEPS * heads, queries.shape[3]),
            new_latent[0],
            jnp.swapaxes(cache_latent[0], 0, 1),
        )

    with jax.named_scope("heads"):
        latents = jnp.concatenate([latents, swap_core(others, n)], axis=1)
        cores = [[2 * chip + core for chip in range(n // 2)] for core in range(2)]
        latents = lax.all_to_all(latents, AXES, 0, 0, axis_index_groups=cores, tiled=True)
        near, far = single(
            heads_kernel,
            n,
            [jax.ShapeDtypeStruct((rows // 2, width), dtype) for dtype in (F32, BF)],
            [me_one],
            [latents.reshape(rows, LAT), w_uv[0], w_out[0]],
            "heads",
            2 * rows * VDIM * (LAT + width),
        )
        loaded = []

        def load_beside(rows):
            rows, *weights = load(n, rows, [w_gate[0], w_up[0], w_down[0]])
            loaded.extend(weights)
            return rows

        parts = reduce_rows(near, far, n, load_beside)

    with jax.named_scope("norm"):
        high = route_scores[0].astype(BF)
        low = (route_scores[0] - high.astype(F32)).astype(BF)
        routes = jnp.concatenate([route_ids[0].astype(BF), high, low], axis=1)
        routes = jnp.pad(routes, ((0, 0), (0, 128 - 3 * TOPK)))
        hidden, normed = single(
            norm_kernel,
            n,
            [
                jax.ShapeDtypeStruct((STEPS, width), F32),
                jax.ShapeDtypeStruct((STEPS, width + 128), BF),
            ],
            [],
            parts + [residual[0], norm_gain.reshape(1, width), routes],
            "norm",
            8 * STEPS * width,
        )

    with jax.named_scope("spread"):
        along = [normed] + [swap(normed, n, 1, j) for j in range(1, n // SPAN)]
        along = jnp.concatenate(along, axis=0)
        blocks = [along] + [swap(along, n, 0, i) for i in range(1, 4)]
        blocks = blocks + [swap_core(x, n) for x in blocks]

    with jax.named_scope("experts"):
        near, far = single(
            functools.partial(expert_kernel, n_ep=n_ep),
            n,
            [jax.ShapeDtypeStruct((rows // 2, width), dtype) for dtype in (F32, BF)],
            [me_one],
            blocks + loaded,
            "experts",
            6 * rows * width * w_gate.shape[2],
        )

    with jax.named_scope("collect"):
        result = hidden
        for term in reduce_rows(near, far, n):
            result = result + term.astype(F32)
        return result.astype(BF)[None]


def solution(mesh):
    placed = (
        P(("sec", "ep"), None, None, None),
        P(("sec", "ep"), None, None),
        P(("sec", "ep"), None, None),
        P(("sec", "ep")),
        P(("sec", "ep"), None, None),
        P(("sec", "ep"), None, None),
        P(("sec", "ep"), None, None),
        P(),
        P(("sec", "ep"), None, None),
        P(("sec", "ep"), None, None),
        P("ep", None, "sec"),
        P("ep", None, "sec"),
        P("ep", "sec", None),
    )
    return jax.shard_map(
        per_device,
        mesh=mesh,
        in_specs=placed,
        out_specs=P(("sec", "ep"), None, None),
        check_vma=False,
    )
```

```python
import functools
import math

import jax
import jax.numpy as jnp
from jax import lax
from jax.experimental import pallas as pl
from jax.experimental.pallas import tpu as pltpu
from jax.sharding import PartitionSpec as P

LAT = 512
ROPE = 64
VDIM = 128
STEPS = 4
TOPK = 8
BLK = 2048
SPAN = 8
AXES = ("sec", "ep")
NT = (((1,), (1,)), ((), ()))
BF = jnp.bfloat16
F32 = jnp.float32
VMEM_LIMIT = 16 * 1024 * 1024
LOAD_LIMIT = 28


def partners(n):
    chips = [(q >> 1) * (n // 2) + (q & 1) * 2 for q in range(4)]
    planes = [k * 4 for k in range(n // SPAN)]
    return [(chips, planes), (planes, chips) if len(planes) == 4 else (chips, planes)]


def swap(x, n, stage, i):
    return lax.ppermute(x, AXES, [(d, d ^ partners(n)[d & 1][stage][i]) for d in range(n)])


def swap_core(x, n):
    return lax.ppermute(x, AXES, [(d, d ^ 1) for d in range(n)])


def iota2(shape, axis):
    return lax.broadcasted_iota(jnp.int32, shape, axis)


def one_hot(columns, count):
    return (iota2(columns.shape, 1) == columns).astype(BF)


def pick(matrix, rows):
    return jnp.dot(matrix, rows, preferred_element_type=F32)


def attend_kernel(n, len_ref, q_hbm, new_hbm, keys_hbm, out_ref, q_ref, new_ref, keys_ref, m_ref, l_ref, acc_ref, small_sem, sem):
    rows = q_ref.shape[0]
    heads = rows // STEPS
    factor_base2 = (VDIM + ROPE) ** (-0.5) * math.log2(math.e)
    length = len_ref[0]
    blk = min(BLK, keys_ref.shape[1])

    def block_at(i):
        return pl.ds(pl.multiple_of(i * blk, blk), blk)

    def block_copy(i):
        return pltpu.make_async_copy(
            keys_hbm.at[:, block_at(i)], keys_ref.at[:, block_at(i)], sem.at[i]
        )

    def start(i):
        @pl.when(i * blk < length)
        def _():
            block_copy(i).start()

    q_copy = pltpu.make_async_copy(q_hbm, q_ref, small_sem.at[0])
    new_copy = pltpu.make_async_copy(new_hbm, new_ref, small_sem.at[1])
    q_copy.start()
    new_copy.start()
    start(0)
    start(1)
    r = iota2((rows, rows), 0)
    order = one_hot((r % STEPS) * heads + r // STEPS, rows)
    q_copy.wait()
    new_copy.wait()

    new = new_ref[...]
    s = lax.dot_general(q_ref[...], new, NT, preferred_element_type=F32)
    step = iota2(s.shape, 0) // heads
    s = jnp.where(iota2(s.shape, 1) <= step, s, -1e30)
    m = jnp.max(s, axis=1, keepdims=True)
    p = jnp.exp2((s - m) * factor_base2)
    m_ref[...] = m
    l_ref[...] = jnp.sum(p, axis=1, keepdims=True)
    acc_ref[...] = jnp.dot(p.astype(BF), new[:, :LAT], preferred_element_type=F32)

    def update(i, masked):
        start(i + 2)
        block_copy(i).wait()
        keys = keys_ref[:, block_at(i)]
        s = jnp.dot(q_ref[...], keys, preferred_element_type=F32)
        if masked:
            s = jnp.where(iota2(s.shape, 1) < length - i * blk, s, -1e30)
        m_old = m_ref[...]
        m = jnp.maximum(m_old, jnp.max(s, axis=1, keepdims=True))
        factor = jnp.exp2((m_old - m) * factor_base2)
        p = jnp.exp2((s - m) * factor_base2)
        m_ref[...] = m
        l_ref[...] = l_ref[...] * factor + jnp.sum(p, axis=1, keepdims=True)
        acc_ref[...] = acc_ref[...] * factor + lax.dot_general(
            p.astype(BF), keys[:LAT], NT, preferred_element_type=F32
        )

    full = length // blk

    @pl.loop(0, full)
    def _(i):
        update(i, False)

    @pl.when(full * blk < length)
    def _():
        update(full, True)

    out = (acc_ref[...] / l_ref[...]).astype(BF)
    out_ref[...] = pick(order, out).reshape(out_ref.shape).astype(BF)


def attend(n, length, q, new, keys):
    rows, width = q.shape
    cached = keys.shape[1]
    blocks = cached // min(BLK, cached)
    return pl.pallas_call(
        functools.partial(attend_kernel, n),
        in_specs=[pl.BlockSpec(memory_space=pltpu.SMEM)]
        + [pl.BlockSpec(memory_space=pl.ANY)] * 3,
        out_specs=pl.BlockSpec(memory_space=pltpu.VMEM),
        scratch_shapes=[
            pltpu.VMEM(q.shape, BF),
            pltpu.VMEM(new.shape, BF),
            pltpu.VMEM(keys.shape, BF),
            pltpu.VMEM((rows, 1), F32),
            pltpu.VMEM((rows, 1), F32),
            pltpu.VMEM((rows, LAT), F32),
            pltpu.SemaphoreType.DMA((2,)),
            pltpu.SemaphoreType.DMA((blocks,)),
        ],
        out_shape=jax.ShapeDtypeStruct((rows // STEPS, STEPS, LAT), BF),
        compiler_params=pltpu.CompilerParams(vmem_limit_bytes=56 * 1024 * 1024),
        cost_estimate=pl.CostEstimate(
            flops=2 * rows * cached * (width + LAT),
            bytes_accessed=2 * cached * width,
            transcendentals=rows * cached,
        ),
        name="attend",
    )(length, q, new, keys)


def source_rows(n, me, rows):
    r = iota2((rows, rows), 0)
    other = r // (rows // 2)
    masks = []
    for firsts, seconds in partners(n):
        i, j = (r // (len(seconds) * STEPS)) % len(firsts), (r // STEPS) % len(seconds)
        mask = jnp.zeros_like(r)
        for index, options in ((i, firsts), (j, seconds)):
            for value, option in enumerate(options):
                mask = mask | jnp.where(index == value, option, 0)
        masks.append(mask)
    mask = jnp.where((me & 1) ^ other == 0, masks[0], masks[1])
    return (me ^ mask ^ other) * STEPS + r % STEPS


def heads_kernel(n, me_ref, latents_ref, uv_ref, out_ref, near_ref, far_ref):
    rows = n * STEPS
    values = jnp.dot(latents_ref[...], uv_ref[...], preferred_element_type=F32).astype(BF)
    values = pick(one_hot(source_rows(n, me_ref[0], rows), rows), values).astype(BF)
    part = out_ref.shape[1] // SPAN
    for p in range(SPAN):
        here = slice(p * part, (p + 1) * part)
        out = jnp.dot(values, out_ref[:, here], preferred_element_type=F32)
        near_ref[:, here] = out[: rows // 2]
        far_ref[:, here] = out[rows // 2 :].astype(BF)


def carry_kernel(n, *refs):
    terms, (residual_ref, routes_ref, mine_ref, sent_ref) = refs[:-4], refs[-4:]
    width = residual_ref.shape[1]
    total = terms[0][...]
    for ref in terms[1:]:
        total += ref[...].astype(F32)
    mine_ref[:, :width] = total
    mine_ref[:STEPS, :width] = total[:STEPS] + residual_ref[...].astype(F32)
    mine_ref[:, width:] = jnp.zeros((total.shape[0], mine_ref.shape[1] - width), F32)
    mine_ref[:STEPS, width:] = routes_ref[...].astype(F32)
    sent_ref[...] = mine_ref[...].astype(BF)


def norm_kernel(n, mine_ref, *refs):
    got, (gain_ref, hidden_ref, out_ref) = refs[:-3], refs[-3:]
    width = gain_ref.shape[1]
    total = mine_ref[...]
    for j, ref in enumerate(got, 1):
        rows = ref[...].astype(F32)
        parts = [(j ^ b) * STEPS for b in range(len(got) + 1)]
        total += jnp.concatenate([rows[first : first + STEPS] for first in parts], axis=0)
    hidden = total[:, :width]
    hidden_ref[...] = hidden[:STEPS]
    mean_square = jnp.sum(hidden * hidden, axis=1, keepdims=True) / width
    normed = hidden * lax.rsqrt(mean_square + 1e-06) * gain_ref[...].astype(F32)
    out_ref[:, :width] = normed.astype(BF)
    out_ref[:, width:] = total[:, width:].astype(BF)


def load_kernel(n, *refs):
    sources, targets, sem = refs[1:4], refs[5:8], refs[8]
    copies = [pltpu.make_async_copy(refs[0], refs[4], sem.at[24])]
    for i in range(3):
        step = sources[i].shape[0] // 8
        for j in range(8):
            here = pl.ds(j * step, step)
            copies.append(
                pltpu.make_async_copy(sources[i].at[here], targets[i].at[here], sem.at[8 * i + j])
            )
    for copy in copies:
        copy.start()
    for copy in copies:
        copy.wait()


def load(n, passed, arrays):
    return pl.pallas_call(
        functools.partial(load_kernel, n),
        in_specs=[pl.BlockSpec(memory_space=pltpu.VMEM)] + [pl.BlockSpec(memory_space=pl.ANY)] * 3,
        out_specs=[pl.BlockSpec(memory_space=pltpu.VMEM)] * 4,
        out_shape=[jax.ShapeDtypeStruct(a.shape, a.dtype) for a in [passed] + arrays],
        scratch_shapes=[pltpu.SemaphoreType.DMA((25,))],
        compiler_params=pltpu.CompilerParams(vmem_limit_bytes=LOAD_LIMIT * 1024 * 1024),
        cost_estimate=pl.CostEstimate(
            flops=0, bytes_accessed=sum(4 * a.size for a in arrays), transcendentals=0
        ),
        name="load_experts",
    )(passed, *arrays)


def expert_kernel(n, me_ref, *refs, n_ep):
    blocks, (gate_ref, up_ref, down_ref, near_ref, far_ref) = refs[:8], refs[8:]
    rows = n * STEPS
    width, units = gate_ref.shape
    part = width // SPAN
    gate = jnp.zeros((rows, units), F32)
    up = jnp.zeros((rows, units), F32)
    for p in range(SPAN):
        here = slice(p * part, (p + 1) * part)
        x = jnp.concatenate([ref[:, here] for ref in blocks], axis=0)
        gate += jnp.dot(x, gate_ref[here], preferred_element_type=F32)
        up += jnp.dot(x, up_ref[here], preferred_element_type=F32)
    act = (gate * jax.nn.sigmoid(gate) * up).astype(BF)
    routes = jnp.concatenate([ref[:, width:] for ref in blocks], axis=0).astype(F32)
    scores = routes[:, TOPK : 2 * TOPK] + routes[:, 2 * TOPK : 3 * TOPK]
    chosen = jnp.where(routes[:, :TOPK] == (me_ref[0] % n_ep).astype(F32), scores, 0.0)
    coef = jnp.sum(chosen, axis=1, keepdims=True) / jnp.sum(scores, axis=1, keepdims=True) * 2.5
    for p in range(SPAN):
        here = slice(p * part, (p + 1) * part)
        out = jnp.dot(act, down_ref[:, here], preferred_element_type=F32) * coef
        near_ref[:, here] = out[: rows // 2]
        far_ref[:, here] = out[rows // 2 :].astype(BF)


def single(kernel, n, out_shape, scalars, arrays, name, flops):
    return pl.pallas_call(
        functools.partial(kernel, n),
        in_specs=[pl.BlockSpec(memory_space=pltpu.SMEM)] * len(scalars)
        + [pl.BlockSpec(memory_space=pltpu.VMEM)] * len(arrays),
        out_shape=out_shape,
        compiler_params=pltpu.CompilerParams(vmem_limit_bytes=VMEM_LIMIT),
        cost_estimate=pl.CostEstimate(
            flops=flops, bytes_accessed=sum(2 * a.size for a in arrays), transcendentals=0
        ),
        name=name,
    )(*scalars, *arrays)


def first_stage(near, far, n):
    firsts = len(partners(n)[0][0])
    total = near + swap_core(far, n).astype(F32)
    total = total.reshape(firsts, total.shape[0] // firsts, total.shape[1])
    return [total[0]] + [swap(total[i].astype(BF), n, 0, i) for i in range(1, firsts)]


def per_device(
    queries,
    new_latent,
    cache_latent,
    cache_len,
    route_ids,
    route_scores,
    residual,
    norm_gain,
    w_uv,
    w_out,
    w_gate,
    w_up,
    w_down,
):
    n_ep = lax.axis_size("ep")
    n = lax.axis_size("sec") * n_ep
    heads = queries.shape[2]
    width = residual.shape[2]
    rows = n * STEPS
    me_one = lax.axis_index(AXES).astype(jnp.int32).reshape(1)

    with jax.named_scope("attention"):
        latents = attend(
            n,
            cache_len,
            queries[0].reshape(STEPS * heads, queries.shape[3]),
            new_latent[0],
            jnp.swapaxes(cache_latent[0], 0, 1),
        )

    with jax.named_scope("heads"):
        latents = lax.all_to_all(latents, AXES, 0, 0, tiled=True)
        near, far = single(
            heads_kernel,
            n,
            [jax.ShapeDtypeStruct((rows // 2, width), dtype) for dtype in (F32, BF)],
            [me_one],
            [latents.reshape(rows, LAT), w_uv[0], w_out[0]],
            "heads",
            2 * rows * VDIM * (LAT + width),
        )
        terms = first_stage(near, far, n)

    with jax.named_scope("norm"):
        high = route_scores[0].astype(BF)
        low = (route_scores[0] - high.astype(F32)).astype(BF)
        routes = jnp.concatenate([route_ids[0].astype(BF), high, low], axis=1)
        routes = jnp.pad(routes, ((0, 0), (0, 128 - 3 * TOPK)))
        shape = (terms[0].shape[0], width + 128)
        mine, sent = single(
            carry_kernel,
            n,
            [jax.ShapeDtypeStruct(shape, dtype) for dtype in (F32, BF)],
            [],
            terms + [residual[0], routes],
            "carry",
            terms[0].size,
        )
        got = [swap(sent, n, 1, j) for j in range(1, n // SPAN)]
        mine, *loaded = load(n, mine, [w_gate[0], w_up[0], w_down[0]])
        hidden, along = single(
            norm_kernel,
            n,
            [jax.ShapeDtypeStruct((STEPS, width), F32), jax.ShapeDtypeStruct(shape, BF)],
            [],
            [mine] + got + [norm_gain.reshape(1, width)],
            "norm",
            8 * mine.size,
        )

    with jax.named_scope("spread"):
        blocks = [along] + [swap(along, n, 0, i) for i in range(1, 4)]
        blocks = blocks + [swap_core(x, n) for x in blocks]

    with jax.named_scope("experts"):
        near, far = single(
            functools.partial(expert_kernel, n_ep=n_ep),
            n,
            [jax.ShapeDtypeStruct((rows // 2, width), dtype) for dtype in (F32, BF)],
            [me_one],
            blocks + loaded,
            "experts",
            6 * rows * width * w_gate.shape[2],
        )

    with jax.named_scope("collect"):
        kept = 0.0
        for term in first_stage(near, far, n):
            kept = kept + term.astype(F32)
        kept = kept.reshape(n // SPAN, STEPS, width)
        result = hidden + kept[0]
        for j in range(1, n // SPAN):
            result = result + swap(kept[j].astype(BF), n, 1, j).astype(F32)
        return result.astype(BF)[None]


def solution(mesh):
    placed = (
        P(("sec", "ep"), None, None, None),
        P(("sec", "ep"), None, None),
        P(("sec", "ep"), None, None),
        P(("sec", "ep")),
        P(("sec", "ep"), None, None),
        P(("sec", "ep"), None, None),
        P(("sec", "ep"), None, None),
        P(),
        P(("sec", "ep"), None, None),
        P(("sec", "ep"), None, None),
        P("ep", None, "sec"),
        P("ep", None, "sec"),
        P("ep", "sec", None),
    )
    return jax.shard_map(
        per_device,
        mesh=mesh,
        in_specs=placed,
        out_specs=P(("sec", "ep"), None, None),
        check_vma=False,
    )
```

```python
import functools
import math

import jax
import jax.numpy as jnp
from jax import lax
from jax.experimental import pallas as pl
from jax.experimental.pallas import tpu as pltpu
from jax.sharding import PartitionSpec as P

LAT = 512
ROPE = 64
VDIM = 128
STEPS = 4
TOPK = 8
BLK = 2048
SPAN = 8
AXES = ("sec", "ep")
NT = (((1,), (1,)), ((), ()))
BF = jnp.bfloat16
F32 = jnp.float32
VMEM_LIMIT = 16 * 1024 * 1024
LOADS = 8
EARLY = 4
LOAD_LIMITS = (48, 35)


def partners(n):
    chips = [(q >> 1) * (n // 2) + (q & 1) * 2 for q in range(4)]
    planes = [k * 4 for k in range(n // SPAN)]
    return [(chips, planes), (planes, chips) if len(planes) == 4 else (chips, planes)]


def swap(x, n, stage, i):
    return lax.ppermute(x, AXES, [(d, d ^ partners(n)[d & 1][stage][i]) for d in range(n)])


def swap_core(x, n):
    return lax.ppermute(x, AXES, [(d, d ^ 1) for d in range(n)])


def iota2(shape, axis):
    return lax.broadcasted_iota(jnp.int32, shape, axis)


def one_hot(columns, count):
    return (iota2(columns.shape, 1) == columns).astype(BF)


def pick(matrix, rows):
    return jnp.dot(matrix, rows, preferred_element_type=F32)


def attend_kernel(n, len_ref, q_hbm, new_hbm, keys_hbm, out_ref, q_ref, new_ref, keys_ref, m_ref, l_ref, acc_ref, small_sem, sem):
    rows = q_ref.shape[0]
    heads = rows // STEPS
    factor_base2 = (VDIM + ROPE) ** (-0.5) * math.log2(math.e)
    length = len_ref[0]
    blk = min(BLK, keys_ref.shape[1])

    def block_at(i):
        return pl.ds(pl.multiple_of(i * blk, blk), blk)

    def block_copy(i):
        return pltpu.make_async_copy(
            keys_hbm.at[:, block_at(i)], keys_ref.at[:, block_at(i)], sem.at[i]
        )

    def start(i):
        @pl.when(i * blk < length)
        def _():
            block_copy(i).start()

    q_copy = pltpu.make_async_copy(q_hbm, q_ref, small_sem.at[0])
    new_copy = pltpu.make_async_copy(new_hbm, new_ref, small_sem.at[1])
    q_copy.start()
    new_copy.start()
    start(0)
    start(1)
    r = iota2((rows, rows), 0)
    order = one_hot((r % STEPS) * heads + r // STEPS, rows)
    q_copy.wait()
    new_copy.wait()

    new = new_ref[...]
    s = lax.dot_general(q_ref[...], new, NT, preferred_element_type=F32)
    step = iota2(s.shape, 0) // heads
    s = jnp.where(iota2(s.shape, 1) <= step, s, -1e30)
    m = jnp.max(s, axis=1, keepdims=True)
    p = jnp.exp2((s - m) * factor_base2)
    m_ref[...] = m
    l_ref[...] = jnp.sum(p, axis=1, keepdims=True)
    acc_ref[...] = jnp.dot(p.astype(BF), new[:, :LAT], preferred_element_type=F32)

    def update(i, masked):
        start(i + 2)
        block_copy(i).wait()
        keys = keys_ref[:, block_at(i)]
        s = jnp.dot(q_ref[...], keys, preferred_element_type=F32)
        if masked:
            s = jnp.where(iota2(s.shape, 1) < length - i * blk, s, -1e30)
        m_old = m_ref[...]
        m = jnp.maximum(m_old, jnp.max(s, axis=1, keepdims=True))
        factor = jnp.exp2((m_old - m) * factor_base2)
        p = jnp.exp2((s - m) * factor_base2)
        m_ref[...] = m
        l_ref[...] = l_ref[...] * factor + jnp.sum(p, axis=1, keepdims=True)
        acc_ref[...] = acc_ref[...] * factor + lax.dot_general(
            p.astype(BF), keys[:LAT], NT, preferred_element_type=F32
        )

    full = length // blk

    @pl.loop(0, full)
    def _(i):
        update(i, False)

    @pl.when(full * blk < length)
    def _():
        update(full, True)

    out = (acc_ref[...] / l_ref[...]).astype(BF)
    out_ref[...] = pick(order, out).reshape(out_ref.shape).astype(BF)


def attend(n, length, q, new, keys):
    rows, width = q.shape
    cached = keys.shape[1]
    blocks = cached // min(BLK, cached)
    return pl.pallas_call(
        functools.partial(attend_kernel, n),
        in_specs=[pl.BlockSpec(memory_space=pltpu.SMEM)]
        + [pl.BlockSpec(memory_space=pl.ANY)] * 3,
        out_specs=pl.BlockSpec(memory_space=pltpu.VMEM),
        scratch_shapes=[
            pltpu.VMEM(q.shape, BF),
            pltpu.VMEM(new.shape, BF),
            pltpu.VMEM(keys.shape, BF),
            pltpu.VMEM((rows, 1), F32),
            pltpu.VMEM((rows, 1), F32),
            pltpu.VMEM((rows, LAT), F32),
            pltpu.SemaphoreType.DMA((2,)),
            pltpu.SemaphoreType.DMA((blocks,)),
        ],
        out_shape=jax.ShapeDtypeStruct((rows // STEPS, STEPS, LAT), BF),
        compiler_params=pltpu.CompilerParams(vmem_limit_bytes=56 * 1024 * 1024),
        cost_estimate=pl.CostEstimate(
            flops=2 * rows * cached * (width + LAT),
            bytes_accessed=2 * cached * width,
            transcendentals=rows * cached,
        ),
        name="attend",
    )(length, q, new, keys)


def source_rows(n, me, rows):
    r = iota2((rows, rows), 0)
    other = r // (rows // 2)
    masks = []
    for firsts, seconds in partners(n):
        i, j = (r // (len(seconds) * STEPS)) % len(firsts), (r // STEPS) % len(seconds)
        mask = jnp.zeros_like(r)
        for index, options in ((i, firsts), (j, seconds)):
            for value, option in enumerate(options):
                mask = mask | jnp.where(index == value, option, 0)
        masks.append(mask)
    mask = jnp.where((me & 1) ^ other == 0, masks[0], masks[1])
    return (me ^ mask ^ other) * STEPS + r % STEPS


def heads_kernel(n, me_ref, latents_ref, uv_ref, out_ref, near_ref, far_ref):
    rows = n * STEPS
    values = jnp.dot(latents_ref[...], uv_ref[...], preferred_element_type=F32).astype(BF)
    values = pick(one_hot(source_rows(n, me_ref[0], rows), rows), values).astype(BF)
    part = out_ref.shape[1] // SPAN
    for p in range(SPAN):
        here = slice(p * part, (p + 1) * part)
        out = jnp.dot(values, out_ref[:, here], preferred_element_type=F32)
        near_ref[:, here] = out[: rows // 2]
        far_ref[:, here] = out[rows // 2 :].astype(BF)


def carry_kernel(n, *refs):
    terms, (residual_ref, routes_ref, mine_ref, sent_ref) = refs[:-4], refs[-4:]
    width = residual_ref.shape[1]
    total = terms[0][...]
    for ref in terms[1:]:
        total += ref[...].astype(F32)
    mine_ref[:, :width] = total
    mine_ref[:STEPS, :width] = total[:STEPS] + residual_ref[...].astype(F32)
    mine_ref[:, width:] = jnp.zeros((total.shape[0], mine_ref.shape[1] - width), F32)
    mine_ref[:STEPS, width:] = routes_ref[...].astype(F32)
    sent_ref[...] = mine_ref[...].astype(BF)


def norm_kernel(n, mine_ref, *refs):
    got, (gain_ref, hidden_ref, out_ref) = refs[:-3], refs[-3:]
    width = gain_ref.shape[1]
    total = mine_ref[...]
    for j, ref in enumerate(got, 1):
        rows = ref[...].astype(F32)
        parts = [(j ^ b) * STEPS for b in range(len(got) + 1)]
        total += jnp.concatenate([rows[first : first + STEPS] for first in parts], axis=0)
    hidden = total[:, :width]
    hidden_ref[...] = hidden[:STEPS]
    mean_square = jnp.sum(hidden * hidden, axis=1, keepdims=True) / width
    normed = hidden * lax.rsqrt(mean_square + 1e-06) * gain_ref[...].astype(F32)
    out_ref[:, :width] = normed.astype(BF)
    out_ref[:, width:] = total[:, width:].astype(BF)


def load_kernel(n, ranges, *refs):
    count = len(ranges)
    sources, targets, sem = refs[1 : 1 + count], refs[2 + count : 2 + 2 * count], refs[-1]
    copies = [pltpu.make_async_copy(refs[0], refs[1 + count], sem.at[0])]
    for source, target, (first, rows) in zip(sources, targets, ranges):
        step = rows // LOADS
        for j in range(LOADS):
            there, here = pl.ds(first + j * step, step), pl.ds(j * step, step)
            copies.append(
                pltpu.make_async_copy(source.at[there], target.at[here], sem.at[len(copies)])
            )
    for copy in copies:
        copy.start()
    for copy in copies:
        copy.wait()


def load(n, passed, arrays, ranges, limit):
    shapes = [(rows, a.shape[1]) for a, (_, rows) in zip(arrays, ranges)]
    return pl.pallas_call(
        functools.partial(load_kernel, n, ranges),
        in_specs=[pl.BlockSpec(memory_space=pltpu.VMEM)]
        + [pl.BlockSpec(memory_space=pl.ANY)] * len(arrays),
        out_specs=[pl.BlockSpec(memory_space=pltpu.VMEM)] * (1 + len(arrays)),
        out_shape=[jax.ShapeDtypeStruct(passed.shape, passed.dtype)]
        + [jax.ShapeDtypeStruct(shape, BF) for shape in shapes],
        scratch_shapes=[pltpu.SemaphoreType.DMA((1 + LOADS * len(arrays),))],
        compiler_params=pltpu.CompilerParams(vmem_limit_bytes=limit * 1024 * 1024),
        cost_estimate=pl.CostEstimate(
            flops=0, bytes_accessed=sum(4 * r * c for r, c in shapes), transcendentals=0
        ),
        name="load",
    )(passed, *arrays)


def expert_kernel(n, me_ref, *refs, n_ep):
    blocks, (early_ref, gate_ref, up_ref, down_ref, near_ref, far_ref) = refs[:8], refs[8:]
    rows = n * STEPS
    width, units = up_ref.shape
    part = width // SPAN
    gate = jnp.zeros((rows, units), F32)
    up = jnp.zeros((rows, units), F32)
    for p in range(SPAN):
        here = slice(p * part, (p + 1) * part)
        x = jnp.concatenate([ref[:, here] for ref in blocks], axis=0)
        late = p - EARLY
        gate_part = early_ref[here] if late < 0 else gate_ref[late * part : (late + 1) * part]
        gate += jnp.dot(x, gate_part, preferred_element_type=F32)
        up += jnp.dot(x, up_ref[here], preferred_element_type=F32)
    act = (gate * jax.nn.sigmoid(gate) * up).astype(BF)
    routes = jnp.concatenate([ref[:, width:] for ref in blocks], axis=0).astype(F32)
    scores = routes[:, TOPK : 2 * TOPK] + routes[:, 2 * TOPK : 3 * TOPK]
    chosen = jnp.where(routes[:, :TOPK] == (me_ref[0] % n_ep).astype(F32), scores, 0.0)
    coef = jnp.sum(chosen, axis=1, keepdims=True) / jnp.sum(scores, axis=1, keepdims=True) * 2.5
    for p in range(SPAN):
        here = slice(p * part, (p + 1) * part)
        out = jnp.dot(act, down_ref[:, here], preferred_element_type=F32) * coef
        near_ref[:, here] = out[: rows // 2]
        far_ref[:, here] = out[rows // 2 :].astype(BF)


def single(kernel, n, out_shape, scalars, arrays, name, flops):
    return pl.pallas_call(
        functools.partial(kernel, n),
        in_specs=[pl.BlockSpec(memory_space=pltpu.SMEM)] * len(scalars)
        + [pl.BlockSpec(memory_space=pltpu.VMEM)] * len(arrays),
        out_shape=out_shape,
        compiler_params=pltpu.CompilerParams(vmem_limit_bytes=VMEM_LIMIT),
        cost_estimate=pl.CostEstimate(
            flops=flops, bytes_accessed=sum(2 * a.size for a in arrays), transcendentals=0
        ),
        name=name,
    )(*scalars, *arrays)


def first_stage(near, far, n, order, beside=lambda rows: rows):
    firsts = len(order) + 1
    total = near + swap_core(far, n).astype(F32)
    total = total.reshape(firsts, total.shape[0] // firsts, total.shape[1])
    got = [swap(total[i].astype(BF), n, 0, i) for i in order]
    return [beside(total[0])] + got


def per_device(
    queries,
    new_latent,
    cache_latent,
    cache_len,
    route_ids,
    route_scores,
    residual,
    norm_gain,
    w_uv,
    w_out,
    w_gate,
    w_up,
    w_down,
):
    n_ep = lax.axis_size("ep")
    n = lax.axis_size("sec") * n_ep
    heads = queries.shape[2]
    width = residual.shape[2]
    rows = n * STEPS
    me_one = lax.axis_index(AXES).astype(jnp.int32).reshape(1)

    with jax.named_scope("attention"):
        latents = attend(
            n,
            cache_len,
            queries[0].reshape(STEPS * heads, queries.shape[3]),
            new_latent[0],
            jnp.swapaxes(cache_latent[0], 0, 1),
        )

    with jax.named_scope("heads"):
        latents = lax.all_to_all(latents, AXES, 0, 0, tiled=True)
        near, far = single(
            heads_kernel,
            n,
            [jax.ShapeDtypeStruct((rows // 2, width), dtype) for dtype in (F32, BF)],
            [me_one],
            [latents.reshape(rows, LAT), w_uv[0], w_out[0]],
            "heads",
            2 * rows * VDIM * (LAT + width),
        )
        early = width // SPAN * EARLY
        loaded = []

        def load_early(rows):
            rows, *weights = load(n, rows, [w_gate[0]], [(0, early)], LOAD_LIMITS[0])
            loaded.extend(weights)
            return rows

        terms = first_stage(near, far, n, (1, 2, 3), load_early)

    with jax.named_scope("norm"):
        high = route_scores[0].astype(BF)
        low = (route_scores[0] - high.astype(F32)).astype(BF)
        routes = jnp.concatenate([route_ids[0].astype(BF), high, low], axis=1)
        routes = jnp.pad(routes, ((0, 0), (0, 128 - 3 * TOPK)))
        shape = (terms[0].shape[0], width + 128)
        mine, sent = single(
            carry_kernel,
            n,
            [jax.ShapeDtypeStruct(shape, dtype) for dtype in (F32, BF)],
            [],
            terms + [residual[0], routes],
            "carry",
            terms[0].size,
        )
        got = [swap(sent, n, 1, j) for j in range(1, n // SPAN)]
        rest = [(early, width - early), (0, width), (0, w_down.shape[1])]
        mine, *weights = load(n, mine, [w_gate[0], w_up[0], w_down[0]], rest, LOAD_LIMITS[1])
        loaded.extend(weights)
        hidden, along = single(
            norm_kernel,
            n,
            [jax.ShapeDtypeStruct((STEPS, width), F32), jax.ShapeDtypeStruct(shape, BF)],
            [],
            [mine] + got + [norm_gain.reshape(1, width)],
            "norm",
            8 * mine.size,
        )

    with jax.named_scope("spread"):
        blocks = [along] + [swap(along, n, 0, i) for i in range(1, 4)]
        blocks = blocks + [swap_core(x, n) for x in blocks]

    with jax.named_scope("experts"):
        near, far = single(
            functools.partial(expert_kernel, n_ep=n_ep),
            n,
            [jax.ShapeDtypeStruct((rows // 2, width), dtype) for dtype in (F32, BF)],
            [me_one],
            blocks + loaded,
            "experts",
            6 * rows * width * w_gate.shape[2],
        )

    with jax.named_scope("collect"):
        kept = 0.0
        for term in first_stage(near, far, n, (3, 2, 1)):
            kept = kept + term.astype(F32)
        kept = kept.reshape(n // SPAN, STEPS, width)
        result = hidden + kept[0]
        for j in reversed(range(1, n // SPAN)):
            result = result + swap(kept[j].astype(BF), n, 1, j).astype(F32)
        return result.astype(BF)[None]


def solution(mesh):
    placed = (
        P(("sec", "ep"), None, None, None),
        P(("sec", "ep"), None, None),
        P(("sec", "ep"), None, None),
        P(("sec", "ep")),
        P(("sec", "ep"), None, None),
        P(("sec", "ep"), None, None),
        P(("sec", "ep"), None, None),
        P(),
        P(("sec", "ep"), None, None),
        P(("sec", "ep"), None, None),
        P("ep", None, "sec"),
        P("ep", None, "sec"),
        P("ep", "sec", None),
    )
    return jax.shard_map(
        per_device,
        mesh=mesh,
        in_specs=placed,
        out_specs=P(("sec", "ep"), None, None),
        check_vma=False,
    )
```

```python
import functools
import math

import jax
import jax.numpy as jnp
from jax import lax
from jax.experimental import pallas as pl
from jax.experimental.pallas import tpu as pltpu
from jax.sharding import PartitionSpec as P

LAT = 512
ROPE = 64
VDIM = 128
STEPS = 4
TOPK = 8
BLK = 2048
SPAN = 8
AXES = ("sec", "ep")
NT = (((1,), (1,)), ((), ()))
BF = jnp.bfloat16
F32 = jnp.float32
VMEM_LIMIT = 16 * 1024 * 1024
LOADS = 8
EARLY = 4
LOAD_LIMITS = (48, 35)


def partners(n):
    chips = [(q >> 1) * (n // 2) + (q & 1) * 2 for q in range(4)]
    planes = [k * 4 for k in range(n // SPAN)]
    return [(chips, planes), (planes, chips) if len(planes) == 4 else (chips, planes)]


def swap(x, n, stage, i):
    return lax.ppermute(x, AXES, [(d, d ^ partners(n)[d & 1][stage][i]) for d in range(n)])


def swap_core(x, n):
    return lax.ppermute(x, AXES, [(d, d ^ 1) for d in range(n)])


def iota2(shape, axis):
    return lax.broadcasted_iota(jnp.int32, shape, axis)


def one_hot(columns, count):
    return (iota2(columns.shape, 1) == columns).astype(BF)


def pick(matrix, rows):
    return jnp.dot(matrix, rows, preferred_element_type=F32)


def attend_kernel(n, len_ref, q_hbm, new_hbm, keys_hbm, out_ref, q_ref, new_ref, keys_ref, m_ref, l_ref, acc_ref, small_sem, sem):
    rows = q_ref.shape[0]
    heads = rows // STEPS
    factor_base2 = (VDIM + ROPE) ** (-0.5) * math.log2(math.e)
    length = len_ref[0]
    blk = min(BLK, keys_ref.shape[1])

    def block_at(i):
        return pl.ds(pl.multiple_of(i * blk, blk), blk)

    def block_copy(i):
        return pltpu.make_async_copy(
            keys_hbm.at[:, block_at(i)], keys_ref.at[:, block_at(i)], sem.at[i]
        )

    def start(i):
        @pl.when(i * blk < length)
        def _():
            block_copy(i).start()

    q_copy = pltpu.make_async_copy(q_hbm, q_ref, small_sem.at[0])
    new_copy = pltpu.make_async_copy(new_hbm, new_ref, small_sem.at[1])
    q_copy.start()
    new_copy.start()
    start(0)
    r = iota2((rows, rows), 0)
    order = one_hot((r % STEPS) * heads + r // STEPS, rows)
    q_copy.wait()
    new_copy.wait()

    new = new_ref[...]
    s = lax.dot_general(q_ref[...], new, NT, preferred_element_type=F32)
    step = iota2(s.shape, 0) // heads
    s = jnp.where(iota2(s.shape, 1) <= step, s, -1e30)
    m = jnp.max(s, axis=1, keepdims=True)
    p = jnp.exp2((s - m) * factor_base2)
    m_ref[...] = m
    l_ref[...] = jnp.sum(p, axis=1, keepdims=True)
    acc = jnp.dot(p.astype(BF), new[:, :LAT], preferred_element_type=F32)
    acc_ref[...] = jnp.transpose(acc)

    def as_row(column):
        same = iota2((rows, rows), 0) == iota2((rows, rows), 1)
        return jnp.sum(jnp.where(same, column, 0.0), axis=0, keepdims=True)


    start(1)

    def update(i, masked):
        start(i + 2)
        block_copy(i).wait()
        keys = keys_ref[:, block_at(i)]
        s = jnp.dot(q_ref[...], keys, preferred_element_type=F32)
        if masked:
            s = jnp.where(iota2(s.shape, 1) < length - i * blk, s, -1e30)
        m_old = m_ref[...]
        m = jnp.maximum(m_old, jnp.max(s, axis=1, keepdims=True))
        factor = jnp.exp2((m_old - m) * factor_base2)
        p = jnp.exp2((s - m) * factor_base2)
        m_ref[...] = m
        l_ref[...] = l_ref[...] * factor + jnp.sum(p, axis=1, keepdims=True)
        acc_ref[...] = acc_ref[...] * as_row(factor) + lax.dot_general(
            keys[:LAT], p.astype(BF), NT, preferred_element_type=F32
        )

    full = length // blk

    @pl.loop(0, full)
    def _(i):
        update(i, False)

    @pl.when(full * blk < length)
    def _():
        update(full, True)

    out = (acc_ref[...] * as_row(1.0 / l_ref[...])).astype(BF)
    moved = lax.dot_general(order, out, NT, preferred_element_type=F32)
    out_ref[...] = moved.reshape(out_ref.shape).astype(BF)


def attend(n, length, q, new, keys):
    rows, width = q.shape
    cached = keys.shape[1]
    blocks = cached // min(BLK, cached)
    return pl.pallas_call(
        functools.partial(attend_kernel, n),
        in_specs=[pl.BlockSpec(memory_space=pltpu.SMEM)]
        + [pl.BlockSpec(memory_space=pl.ANY)] * 3,
        out_specs=pl.BlockSpec(memory_space=pltpu.VMEM),
        scratch_shapes=[
            pltpu.VMEM(q.shape, BF),
            pltpu.VMEM(new.shape, BF),
            pltpu.VMEM(keys.shape, BF),
            pltpu.VMEM((rows, 1), F32),
            pltpu.VMEM((rows, 1), F32),
            pltpu.VMEM((LAT, rows), F32),
            pltpu.SemaphoreType.DMA((2,)),
            pltpu.SemaphoreType.DMA((blocks,)),
        ],
        out_shape=jax.ShapeDtypeStruct((rows // STEPS, STEPS, LAT), BF),
        compiler_params=pltpu.CompilerParams(vmem_limit_bytes=56 * 1024 * 1024),
        cost_estimate=pl.CostEstimate(
            flops=2 * rows * cached * (width + LAT),
            bytes_accessed=2 * cached * width,
            transcendentals=rows * cached,
        ),
        name="attend",
    )(length, q, new, keys)


def source_rows(n, me, rows):
    r = iota2((rows, rows), 0)
    other = r // (rows // 2)
    masks = []
    for firsts, seconds in partners(n):
        i, j = (r // (len(seconds) * STEPS)) % len(firsts), (r // STEPS) % len(seconds)
        mask = jnp.zeros_like(r)
        for index, options in ((i, firsts), (j, seconds)):
            for value, option in enumerate(options):
                mask = mask | jnp.where(index == value, option, 0)
        masks.append(mask)
    mask = jnp.where((me & 1) ^ other == 0, masks[0], masks[1])
    return (me ^ mask ^ other) * STEPS + r % STEPS


def heads_kernel(n, me_ref, latents_ref, uv_ref, out_ref, near_ref, far_ref):
    rows = n * STEPS
    values = jnp.dot(latents_ref[...], uv_ref[...], preferred_element_type=F32).astype(BF)
    values = pick(one_hot(source_rows(n, me_ref[0], rows), rows), values).astype(BF)
    part = out_ref.shape[1] // SPAN
    for p in range(SPAN):
        here = slice(p * part, (p + 1) * part)
        out = jnp.dot(values, out_ref[:, here], preferred_element_type=F32)
        near_ref[:, here] = out[: rows // 2]
        far_ref[:, here] = out[rows // 2 :].astype(BF)


def carry_kernel(n, *refs):
    terms, (residual_ref, routes_ref, mine_ref, sent_ref) = refs[:-4], refs[-4:]
    width = residual_ref.shape[1]
    total = terms[0][...]
    for ref in terms[1:]:
        total += ref[...].astype(F32)
    mine_ref[:, :width] = total
    mine_ref[:STEPS, :width] = total[:STEPS] + residual_ref[...].astype(F32)
    mine_ref[:, width:] = jnp.zeros((total.shape[0], mine_ref.shape[1] - width), F32)
    mine_ref[:STEPS, width:] = routes_ref[...].astype(F32)
    sent_ref[...] = mine_ref[...].astype(BF)


def norm_kernel(n, mine_ref, *refs):
    got, (gain_ref, hidden_ref, out_ref) = refs[:-3], refs[-3:]
    width = gain_ref.shape[1]
    total = mine_ref[...]
    for j, ref in enumerate(got, 1):
        rows = ref[...].astype(F32)
        parts = [(j ^ b) * STEPS for b in range(len(got) + 1)]
        total += jnp.concatenate([rows[first : first + STEPS] for first in parts], axis=0)
    hidden = total[:, :width]
    hidden_ref[...] = hidden[:STEPS]
    mean_square = jnp.sum(hidden * hidden, axis=1, keepdims=True) / width
    normed = hidden * lax.rsqrt(mean_square + 1e-06) * gain_ref[...].astype(F32)
    out_ref[:, :width] = normed.astype(BF)
    out_ref[:, width:] = total[:, width:].astype(BF)


def load_kernel(n, ranges, *refs):
    count = len(ranges)
    sources, targets, sem = refs[1 : 1 + count], refs[2 + count : 2 + 2 * count], refs[-1]
    copies = [pltpu.make_async_copy(refs[0], refs[1 + count], sem.at[0])]
    for source, target, (first, rows) in zip(sources, targets, ranges):
        step = rows // LOADS
        for j in range(LOADS):
            there, here = pl.ds(first + j * step, step), pl.ds(j * step, step)
            copies.append(
                pltpu.make_async_copy(source.at[there], target.at[here], sem.at[len(copies)])
            )
    for copy in copies:
        copy.start()
    for copy in copies:
        copy.wait()


def load(n, passed, arrays, ranges, limit):
    shapes = [(rows, a.shape[1]) for a, (_, rows) in zip(arrays, ranges)]
    return pl.pallas_call(
        functools.partial(load_kernel, n, ranges),
        in_specs=[pl.BlockSpec(memory_space=pltpu.VMEM)]
        + [pl.BlockSpec(memory_space=pl.ANY)] * len(arrays),
        out_specs=[pl.BlockSpec(memory_space=pltpu.VMEM)] * (1 + len(arrays)),
        out_shape=[jax.ShapeDtypeStruct(passed.shape, passed.dtype)]
        + [jax.ShapeDtypeStruct(shape, BF) for shape in shapes],
        scratch_shapes=[pltpu.SemaphoreType.DMA((1 + LOADS * len(arrays),))],
        compiler_params=pltpu.CompilerParams(vmem_limit_bytes=limit * 1024 * 1024),
        cost_estimate=pl.CostEstimate(
            flops=0, bytes_accessed=sum(4 * r * c for r, c in shapes), transcendentals=0
        ),
        name="load",
    )(passed, *arrays)


def expert_kernel(n, me_ref, *refs, n_ep):
    blocks, (early_ref, gate_ref, up_ref, down_ref, near_ref, far_ref) = refs[:8], refs[8:]
    rows = n * STEPS
    width, units = up_ref.shape
    part = width // SPAN
    gate = jnp.zeros((rows, units), F32)
    up = jnp.zeros((rows, units), F32)
    for p in range(SPAN):
        here = slice(p * part, (p + 1) * part)
        x = jnp.concatenate([ref[:, here] for ref in blocks], axis=0)
        late = p - EARLY
        gate_part = early_ref[here] if late < 0 else gate_ref[late * part : (late + 1) * part]
        gate += jnp.dot(x, gate_part, preferred_element_type=F32)
        up += jnp.dot(x, up_ref[here], preferred_element_type=F32)
    act = (gate * jax.nn.sigmoid(gate) * up).astype(BF)
    routes = jnp.concatenate([ref[:, width:] for ref in blocks], axis=0).astype(F32)
    scores = routes[:, TOPK : 2 * TOPK] + routes[:, 2 * TOPK : 3 * TOPK]
    chosen = jnp.where(routes[:, :TOPK] == (me_ref[0] % n_ep).astype(F32), scores, 0.0)
    coef = jnp.sum(chosen, axis=1, keepdims=True) / jnp.sum(scores, axis=1, keepdims=True) * 2.5
    for p in range(SPAN):
        here = slice(p * part, (p + 1) * part)
        out = jnp.dot(act, down_ref[:, here], preferred_element_type=F32) * coef
        near_ref[:, here] = out[: rows // 2]
        far_ref[:, here] = out[rows // 2 :].astype(BF)


def single(kernel, n, out_shape, scalars, arrays, name, flops):
    return pl.pallas_call(
        functools.partial(kernel, n),
        in_specs=[pl.BlockSpec(memory_space=pltpu.SMEM)] * len(scalars)
        + [pl.BlockSpec(memory_space=pltpu.VMEM)] * len(arrays),
        out_shape=out_shape,
        compiler_params=pltpu.CompilerParams(vmem_limit_bytes=VMEM_LIMIT),
        cost_estimate=pl.CostEstimate(
            flops=flops, bytes_accessed=sum(2 * a.size for a in arrays), transcendentals=0
        ),
        name=name,
    )(*scalars, *arrays)


def first_stage(near, far, n, order, beside=lambda rows: rows):
    firsts = len(order) + 1
    total = near + swap_core(far, n).astype(F32)
    total = total.reshape(firsts, total.shape[0] // firsts, total.shape[1])
    got = [swap(total[i].astype(BF), n, 0, i) for i in order]
    return [beside(total[0])] + got


def per_device(
    queries,
    new_latent,
    cache_latent,
    cache_len,
    route_ids,
    route_scores,
    residual,
    norm_gain,
    w_uv,
    w_out,
    w_gate,
    w_up,
    w_down,
):
    n_ep = lax.axis_size("ep")
    n = lax.axis_size("sec") * n_ep
    heads = queries.shape[2]
    width = residual.shape[2]
    rows = n * STEPS
    me_one = lax.axis_index(AXES).astype(jnp.int32).reshape(1)

    with jax.named_scope("attention"):
        latents = attend(
            n,
            cache_len,
            queries[0].reshape(STEPS * heads, queries.shape[3]),
            new_latent[0],
            jnp.swapaxes(cache_latent[0], 0, 1),
        )

    with jax.named_scope("heads"):
        latents = lax.all_to_all(latents, AXES, 0, 0, tiled=True)
        near, far = single(
            heads_kernel,
            n,
            [jax.ShapeDtypeStruct((rows // 2, width), dtype) for dtype in (F32, BF)],
            [me_one],
            [latents.reshape(rows, LAT), w_uv[0], w_out[0]],
            "heads",
            2 * rows * VDIM * (LAT + width),
        )
        early = width // SPAN * EARLY
        loaded = []

        def load_early(rows):
            rows, *weights = load(n, rows, [w_gate[0]], [(0, early)], LOAD_LIMITS[0])
            loaded.extend(weights)
            return rows

        terms = first_stage(near, far, n, (1, 2, 3), load_early)

    with jax.named_scope("norm"):
        high = route_scores[0].astype(BF)
        low = (route_scores[0] - high.astype(F32)).astype(BF)
        routes = jnp.concatenate([route_ids[0].astype(BF), high, low], axis=1)
        routes = jnp.pad(routes, ((0, 0), (0, 128 - 3 * TOPK)))
        shape = (terms[0].shape[0], width + 128)
        mine, sent = single(
            carry_kernel,
            n,
            [jax.ShapeDtypeStruct(shape, dtype) for dtype in (F32, BF)],
            [],
            terms + [residual[0], routes],
            "carry",
            terms[0].size,
        )
        got = [swap(sent, n, 1, j) for j in range(1, n // SPAN)]
        rest = [(early, width - early), (0, width), (0, w_down.shape[1])]
        mine, *weights = load(n, mine, [w_gate[0], w_up[0], w_down[0]], rest, LOAD_LIMITS[1])
        loaded.extend(weights)
        hidden, along = single(
            norm_kernel,
            n,
            [jax.ShapeDtypeStruct((STEPS, width), F32), jax.ShapeDtypeStruct(shape, BF)],
            [],
            [mine] + got + [norm_gain.reshape(1, width)],
            "norm",
            8 * mine.size,
        )

    with jax.named_scope("spread"):
        blocks = [along] + [swap(along, n, 0, i) for i in range(1, 4)]
        blocks = blocks + [swap_core(x, n) for x in blocks]

    with jax.named_scope("experts"):
        near, far = single(
            functools.partial(expert_kernel, n_ep=n_ep),
            n,
            [jax.ShapeDtypeStruct((rows // 2, width), dtype) for dtype in (F32, BF)],
            [me_one],
            blocks + loaded,
            "experts",
            6 * rows * width * w_gate.shape[2],
        )

    with jax.named_scope("collect"):
        kept = 0.0
        for term in first_stage(near, far, n, (3, 2, 1)):
            kept = kept + term.astype(F32)
        kept = kept.reshape(n // SPAN, STEPS, width)
        result = hidden + kept[0]
        for j in reversed(range(1, n // SPAN)):
            result = result + swap(kept[j].astype(BF), n, 1, j).astype(F32)
        return result.astype(BF)[None]


def solution(mesh):
    placed = (
        P(("sec", "ep"), None, None, None),
        P(("sec", "ep"), None, None),
        P(("sec", "ep"), None, None),
        P(("sec", "ep")),
        P(("sec", "ep"), None, None),
        P(("sec", "ep"), None, None),
        P(("sec", "ep"), None, None),
        P(),
        P(("sec", "ep"), None, None),
        P(("sec", "ep"), None, None),
        P("ep", None, "sec"),
        P("ep", None, "sec"),
        P("ep", "sec", None),
    )
    return jax.shard_map(
        per_device,
        mesh=mesh,
        in_specs=placed,
        out_specs=P(("sec", "ep"), None, None),
        check_vma=False,
    )
```

```python
import functools
import math

import jax
import jax.numpy as jnp
from jax import lax
from jax.experimental import pallas as pl
from jax.experimental.pallas import tpu as pltpu
from jax.sharding import PartitionSpec as P

LAT = 512
ROPE = 64
VDIM = 128
STEPS = 4
TOPK = 8
BLK = 2048
KEY_COPIES = 6
SPAN = 8
AXES = ("sec", "ep")
NT = (((1,), (1,)), ((), ()))
BF = jnp.bfloat16
F32 = jnp.float32
VMEM_LIMIT = 16 * 1024 * 1024
LOADS = 8
EARLY = 4
LOAD_LIMITS = (48, 35)


def partners(n):
    chips = [(q >> 1) * (n // 2) + (q & 1) * 2 for q in range(4)]
    planes = [k * 4 for k in range(n // SPAN)]
    return [(chips, planes), (planes, chips) if len(planes) == 4 else (chips, planes)]


def swap(x, n, stage, i):
    return lax.ppermute(x, AXES, [(d, d ^ partners(n)[d & 1][stage][i]) for d in range(n)])


def swap_core(x, n):
    return lax.ppermute(x, AXES, [(d, d ^ 1) for d in range(n)])


def iota2(shape, axis):
    return lax.broadcasted_iota(jnp.int32, shape, axis)


def one_hot(columns, count):
    return (iota2(columns.shape, 1) == columns).astype(BF)


def pick(matrix, rows):
    return jnp.dot(matrix, rows, preferred_element_type=F32)


def attend_kernel(n, len_ref, q_hbm, new_hbm, keys_hbm, out_ref, q_ref, new_ref, keys_ref, m_ref, l_ref, acc_ref, small_sem, sem):
    rows = q_ref.shape[0]
    heads = rows // STEPS
    factor_base2 = (VDIM + ROPE) ** (-0.5) * math.log2(math.e)
    length = len_ref[0]
    blk = min(BLK, keys_ref.shape[1])

    def block_at(i):
        return pl.ds(pl.multiple_of(i * blk, blk), blk)

    step = keys_ref.shape[0] // KEY_COPIES

    def block_copies(i):
        copies = []
        for part in range(KEY_COPIES):
            here = (pl.ds(part * step, step), block_at(i))
            copies.append(
                pltpu.make_async_copy(keys_hbm.at[here], keys_ref.at[here], sem.at[i, part])
            )
        return copies

    def start(i):
        @pl.when(i * blk < length)
        def _():
            for copy in block_copies(i):
                copy.start()

    q_copy = pltpu.make_async_copy(q_hbm, q_ref, small_sem.at[0])
    new_copy = pltpu.make_async_copy(new_hbm, new_ref, small_sem.at[1])
    q_copy.start()
    new_copy.start()
    start(0)
    r = iota2((rows, rows), 0)
    order = one_hot((r % STEPS) * heads + r // STEPS, rows)
    q_copy.wait()
    new_copy.wait()

    new = new_ref[...]
    s = lax.dot_general(q_ref[...], new, NT, preferred_element_type=F32)
    query_step = iota2(s.shape, 0) // heads
    s = jnp.where(iota2(s.shape, 1) <= query_step, s, -1e30)
    m = jnp.max(s, axis=1, keepdims=True)
    p = jnp.exp2((s - m) * factor_base2)
    m_ref[...] = m
    l_ref[...] = jnp.sum(p, axis=1, keepdims=True)
    acc = jnp.dot(p.astype(BF), new[:, :LAT], preferred_element_type=F32)
    acc_ref[...] = jnp.transpose(acc)

    def as_row(column):
        same = iota2((rows, rows), 0) == iota2((rows, rows), 1)
        return jnp.sum(jnp.where(same, column, 0.0), axis=0, keepdims=True)


    start(1)

    def update(i, masked):
        start(i + 2)
        for copy in block_copies(i):
            copy.wait()
        keys = keys_ref[:, block_at(i)]
        s = jnp.dot(q_ref[...], keys, preferred_element_type=F32)
        if masked:
            s = jnp.where(iota2(s.shape, 1) < length - i * blk, s, -1e30)
        m_old = m_ref[...]
        m = jnp.maximum(m_old, jnp.max(s, axis=1, keepdims=True))
        factor = jnp.exp2((m_old - m) * factor_base2)
        p = jnp.exp2((s - m) * factor_base2)
        m_ref[...] = m
        l_ref[...] = l_ref[...] * factor + jnp.sum(p, axis=1, keepdims=True)
        acc_ref[...] = acc_ref[...] * as_row(factor) + lax.dot_general(
            keys[:LAT], p.astype(BF), NT, preferred_element_type=F32
        )

    full = length // blk

    @pl.loop(0, full)
    def _(i):
        update(i, False)

    @pl.when(full * blk < length)
    def _():
        update(full, True)

    out = (acc_ref[...] * as_row(1.0 / l_ref[...])).astype(BF)
    moved = lax.dot_general(order, out, NT, preferred_element_type=F32)
    out_ref[...] = moved.reshape(out_ref.shape).astype(BF)


def attend(n, length, q, new, keys):
    rows, width = q.shape
    cached = keys.shape[1]
    blocks = cached // min(BLK, cached)
    return pl.pallas_call(
        functools.partial(attend_kernel, n),
        in_specs=[pl.BlockSpec(memory_space=pltpu.SMEM)]
        + [pl.BlockSpec(memory_space=pl.ANY)] * 3,
        out_specs=pl.BlockSpec(memory_space=pltpu.VMEM),
        scratch_shapes=[
            pltpu.VMEM(q.shape, BF),
            pltpu.VMEM(new.shape, BF),
            pltpu.VMEM(keys.shape, BF),
            pltpu.VMEM((rows, 1), F32),
            pltpu.VMEM((rows, 1), F32),
            pltpu.VMEM((LAT, rows), F32),
            pltpu.SemaphoreType.DMA((2,)),
            pltpu.SemaphoreType.DMA((blocks, KEY_COPIES)),
        ],
        out_shape=jax.ShapeDtypeStruct((rows // STEPS, STEPS, LAT), BF),
        compiler_params=pltpu.CompilerParams(vmem_limit_bytes=56 * 1024 * 1024),
        cost_estimate=pl.CostEstimate(
            flops=2 * rows * cached * (width + LAT),
            bytes_accessed=2 * cached * width,
            transcendentals=rows * cached,
        ),
        name="attend",
    )(length, q, new, keys)


def source_rows(n, me, rows):
    r = iota2((rows, rows), 0)
    other = r // (rows // 2)
    masks = []
    for firsts, seconds in partners(n):
        i, j = (r // (len(seconds) * STEPS)) % len(firsts), (r // STEPS) % len(seconds)
        mask = jnp.zeros_like(r)
        for index, options in ((i, firsts), (j, seconds)):
            for value, option in enumerate(options):
                mask = mask | jnp.where(index == value, option, 0)
        masks.append(mask)
    mask = jnp.where((me & 1) ^ other == 0, masks[0], masks[1])
    return (me ^ mask ^ other) * STEPS + r % STEPS


def heads_kernel(n, me_ref, latents_ref, uv_ref, out_ref, near_ref, far_ref):
    rows = n * STEPS
    values = jnp.dot(latents_ref[...], uv_ref[...], preferred_element_type=F32).astype(BF)
    values = pick(one_hot(source_rows(n, me_ref[0], rows), rows), values).astype(BF)
    part = out_ref.shape[1] // SPAN
    for p in range(SPAN):
        here = slice(p * part, (p + 1) * part)
        out = jnp.dot(values, out_ref[:, here], preferred_element_type=F32)
        near_ref[:, here] = out[: rows // 2]
        far_ref[:, here] = out[rows // 2 :].astype(BF)


def carry_kernel(n, *refs):
    terms, (residual_ref, routes_ref, mine_ref, sent_ref) = refs[:-4], refs[-4:]
    width = residual_ref.shape[1]
    total = terms[0][...]
    for ref in terms[1:]:
        total += ref[...].astype(F32)
    mine_ref[:, :width] = total
    mine_ref[:STEPS, :width] = total[:STEPS] + residual_ref[...].astype(F32)
    mine_ref[:, width:] = jnp.zeros((total.shape[0], mine_ref.shape[1] - width), F32)
    mine_ref[:STEPS, width:] = routes_ref[...].astype(F32)
    sent_ref[...] = mine_ref[...].astype(BF)


def norm_kernel(n, mine_ref, *refs):
    got, (gain_ref, hidden_ref, out_ref) = refs[:-3], refs[-3:]
    width = gain_ref.shape[1]
    total = mine_ref[...]
    for j, ref in enumerate(got, 1):
        rows = ref[...].astype(F32)
        parts = [(j ^ b) * STEPS for b in range(len(got) + 1)]
        total += jnp.concatenate([rows[first : first + STEPS] for first in parts], axis=0)
    hidden = total[:, :width]
    hidden_ref[...] = hidden[:STEPS]
    mean_square = jnp.sum(hidden * hidden, axis=1, keepdims=True) / width
    normed = hidden * lax.rsqrt(mean_square + 1e-06) * gain_ref[...].astype(F32)
    out_ref[:, :width] = normed.astype(BF)
    out_ref[:, width:] = total[:, width:].astype(BF)


def load_kernel(n, ranges, *refs):
    count = len(ranges)
    sources, targets, sem = refs[1 : 1 + count], refs[2 + count : 2 + 2 * count], refs[-1]
    copies = [pltpu.make_async_copy(refs[0], refs[1 + count], sem.at[0])]
    for source, target, (first, rows) in zip(sources, targets, ranges):
        step = rows // LOADS
        for j in range(LOADS):
            there, here = pl.ds(first + j * step, step), pl.ds(j * step, step)
            copies.append(
                pltpu.make_async_copy(source.at[there], target.at[here], sem.at[len(copies)])
            )
    for copy in copies:
        copy.start()
    for copy in copies:
        copy.wait()


def load(n, passed, arrays, ranges, limit):
    shapes = [(rows, a.shape[1]) for a, (_, rows) in zip(arrays, ranges)]
    return pl.pallas_call(
        functools.partial(load_kernel, n, ranges),
        in_specs=[pl.BlockSpec(memory_space=pltpu.VMEM)]
        + [pl.BlockSpec(memory_space=pl.ANY)] * len(arrays),
        out_specs=[pl.BlockSpec(memory_space=pltpu.VMEM)] * (1 + len(arrays)),
        out_shape=[jax.ShapeDtypeStruct(passed.shape, passed.dtype)]
        + [jax.ShapeDtypeStruct(shape, BF) for shape in shapes],
        scratch_shapes=[pltpu.SemaphoreType.DMA((1 + LOADS * len(arrays),))],
        compiler_params=pltpu.CompilerParams(vmem_limit_bytes=limit * 1024 * 1024),
        cost_estimate=pl.CostEstimate(
            flops=0, bytes_accessed=sum(4 * r * c for r, c in shapes), transcendentals=0
        ),
        name="load",
    )(passed, *arrays)


def expert_kernel(n, me_ref, *refs, n_ep):
    blocks, (early_ref, gate_ref, up_ref, down_ref, near_ref, far_ref) = refs[:8], refs[8:]
    rows = n * STEPS
    width, units = up_ref.shape
    part = width // SPAN
    gate = jnp.zeros((rows, units), F32)
    up = jnp.zeros((rows, units), F32)
    for p in range(SPAN):
        here = slice(p * part, (p + 1) * part)
        x = jnp.concatenate([ref[:, here] for ref in blocks], axis=0)
        late = p - EARLY
        gate_part = early_ref[here] if late < 0 else gate_ref[late * part : (late + 1) * part]
        gate += jnp.dot(x, gate_part, preferred_element_type=F32)
        up += jnp.dot(x, up_ref[here], preferred_element_type=F32)
    act = (gate * jax.nn.sigmoid(gate) * up).astype(BF)
    routes = jnp.concatenate([ref[:, width:] for ref in blocks], axis=0).astype(F32)
    scores = routes[:, TOPK : 2 * TOPK] + routes[:, 2 * TOPK : 3 * TOPK]
    chosen = jnp.where(routes[:, :TOPK] == (me_ref[0] % n_ep).astype(F32), scores, 0.0)
    coef = jnp.sum(chosen, axis=1, keepdims=True) / jnp.sum(scores, axis=1, keepdims=True) * 2.5
    for p in range(SPAN):
        here = slice(p * part, (p + 1) * part)
        out = jnp.dot(act, down_ref[:, here], preferred_element_type=F32) * coef
        near_ref[:, here] = out[: rows // 2]
        far_ref[:, here] = out[rows // 2 :].astype(BF)


def single(kernel, n, out_shape, scalars, arrays, name, flops):
    return pl.pallas_call(
        functools.partial(kernel, n),
        in_specs=[pl.BlockSpec(memory_space=pltpu.SMEM)] * len(scalars)
        + [pl.BlockSpec(memory_space=pltpu.VMEM)] * len(arrays),
        out_shape=out_shape,
        compiler_params=pltpu.CompilerParams(vmem_limit_bytes=VMEM_LIMIT),
        cost_estimate=pl.CostEstimate(
            flops=flops, bytes_accessed=sum(2 * a.size for a in arrays), transcendentals=0
        ),
        name=name,
    )(*scalars, *arrays)


def first_stage(near, far, n, order, beside=lambda rows: rows):
    firsts = len(order) + 1
    total = near + swap_core(far, n).astype(F32)
    total = total.reshape(firsts, total.shape[0] // firsts, total.shape[1])
    got = [swap(total[i].astype(BF), n, 0, i) for i in order]
    return [beside(total[0])] + got


def per_device(
    queries,
    new_latent,
    cache_latent,
    cache_len,
    route_ids,
    route_scores,
    residual,
    norm_gain,
    w_uv,
    w_out,
    w_gate,
    w_up,
    w_down,
):
    n_ep = lax.axis_size("ep")
    n = lax.axis_size("sec") * n_ep
    heads = queries.shape[2]
    width = residual.shape[2]
    rows = n * STEPS
    me_one = lax.axis_index(AXES).astype(jnp.int32).reshape(1)

    with jax.named_scope("attention"):
        latents = attend(
            n,
            cache_len,
            queries[0].reshape(STEPS * heads, queries.shape[3]),
            new_latent[0],
            jnp.swapaxes(cache_latent[0], 0, 1),
        )

    with jax.named_scope("heads"):
        latents = lax.all_to_all(latents, AXES, 0, 0, tiled=True)
        near, far = single(
            heads_kernel,
            n,
            [jax.ShapeDtypeStruct((rows // 2, width), dtype) for dtype in (F32, BF)],
            [me_one],
            [latents.reshape(rows, LAT), w_uv[0], w_out[0]],
            "heads",
            2 * rows * VDIM * (LAT + width),
        )
        early = width // SPAN * EARLY
        loaded = []

        def load_early(rows):
            rows, *weights = load(n, rows, [w_gate[0]], [(0, early)], LOAD_LIMITS[0])
            loaded.extend(weights)
            return rows

        terms = first_stage(near, far, n, (1, 2, 3), load_early)

    with jax.named_scope("norm"):
        high = route_scores[0].astype(BF)
        low = (route_scores[0] - high.astype(F32)).astype(BF)
        routes = jnp.concatenate([route_ids[0].astype(BF), high, low], axis=1)
        routes = jnp.pad(routes, ((0, 0), (0, 128 - 3 * TOPK)))
        shape = (terms[0].shape[0], width + 128)
        mine, sent = single(
            carry_kernel,
            n,
            [jax.ShapeDtypeStruct(shape, dtype) for dtype in (F32, BF)],
            [],
            terms + [residual[0], routes],
            "carry",
            terms[0].size,
        )
        got = [swap(sent, n, 1, j) for j in range(1, n // SPAN)]
        rest = [(early, width - early), (0, width), (0, w_down.shape[1])]
        mine, *weights = load(n, mine, [w_gate[0], w_up[0], w_down[0]], rest, LOAD_LIMITS[1])
        loaded.extend(weights)
        hidden, along = single(
            norm_kernel,
            n,
            [jax.ShapeDtypeStruct((STEPS, width), F32), jax.ShapeDtypeStruct(shape, BF)],
            [],
            [mine] + got + [norm_gain.reshape(1, width)],
            "norm",
            8 * mine.size,
        )

    with jax.named_scope("spread"):
        blocks = [along] + [swap(along, n, 0, i) for i in range(1, 4)]
        blocks = blocks + [swap_core(x, n) for x in blocks]

    with jax.named_scope("experts"):
        near, far = single(
            functools.partial(expert_kernel, n_ep=n_ep),
            n,
            [jax.ShapeDtypeStruct((rows // 2, width), dtype) for dtype in (F32, BF)],
            [me_one],
            blocks + loaded,
            "experts",
            6 * rows * width * w_gate.shape[2],
        )

    with jax.named_scope("collect"):
        kept = 0.0
        for term in first_stage(near, far, n, (3, 2, 1)):
            kept = kept + term.astype(F32)
        kept = kept.reshape(n // SPAN, STEPS, width)
        result = hidden + kept[0]
        for j in reversed(range(1, n // SPAN)):
            result = result + swap(kept[j].astype(BF), n, 1, j).astype(F32)
        return result.astype(BF)[None]


def solution(mesh):
    placed = (
        P(("sec", "ep"), None, None, None),
        P(("sec", "ep"), None, None),
        P(("sec", "ep"), None, None),
        P(("sec", "ep")),
        P(("sec", "ep"), None, None),
        P(("sec", "ep"), None, None),
        P(("sec", "ep"), None, None),
        P(),
        P(("sec", "ep"), None, None),
        P(("sec", "ep"), None, None),
        P("ep", None, "sec"),
        P("ep", None, "sec"),
        P("ep", "sec", None),
    )
    return jax.shard_map(
        per_device,
        mesh=mesh,
        in_specs=placed,
        out_specs=P(("sec", "ep"), None, None),
        check_vma=False,
    )
```

```python
import functools
import math

import jax
import jax.numpy as jnp
from jax import lax
from jax.experimental import pallas as pl
from jax.experimental.pallas import tpu as pltpu
from jax.sharding import PartitionSpec as P

LAT = 512
ROPE = 64
VDIM = 128
STEPS = 4
TOPK = 8
BLK = 2048
SPAN = 8
AXES = ("sec", "ep")
NT = (((1,), (1,)), ((), ()))
BF = jnp.bfloat16
F32 = jnp.float32
VMEM_LIMIT = 16 * 1024 * 1024
LOADS = 8
EARLY = 4
LOAD_LIMITS = (48, 35)


def partners(n):
    chips = [(q >> 1) * (n // 2) + (q & 1) * 2 for q in range(4)]
    planes = [k * 4 for k in range(n // SPAN)]
    return [(chips, planes), (planes, chips) if len(planes) == 4 else (chips, planes)]


def swap(x, n, stage, i):
    return lax.ppermute(x, AXES, [(d, d ^ partners(n)[d & 1][stage][i]) for d in range(n)])


def swap_core(x, n):
    return lax.ppermute(x, AXES, [(d, d ^ 1) for d in range(n)])


def iota2(shape, axis):
    return lax.broadcasted_iota(jnp.int32, shape, axis)


def one_hot(columns, count):
    return (iota2(columns.shape, 1) == columns).astype(BF)


def pick(matrix, rows):
    return jnp.dot(matrix, rows, preferred_element_type=F32)


def attend_kernel(n, len_ref, q_hbm, new_hbm, keys_hbm, out_ref, q_ref, new_ref, keys_ref, m_ref, l_ref, acc_ref, small_sem, sem):
    rows = q_ref.shape[0]
    heads = rows // STEPS
    factor_base2 = (VDIM + ROPE) ** (-0.5) * math.log2(math.e)
    length = len_ref[0]
    blk = min(BLK, keys_ref.shape[1])

    half = blk // 2

    def half_at(i, part):
        return pl.ds(pl.multiple_of(i * blk + part * half, half), half)

    def half_copy(i, part):
        here = half_at(i, part)
        return pltpu.make_async_copy(keys_hbm.at[:, here], keys_ref.at[:, here], sem.at[i, part])

    def start(i):
        @pl.when(i * blk < length)
        def _():
            half_copy(i, 0).start()
            half_copy(i, 1).start()

    q_copy = pltpu.make_async_copy(q_hbm, q_ref, small_sem.at[0])
    new_copy = pltpu.make_async_copy(new_hbm, new_ref, small_sem.at[1])
    q_copy.start()
    new_copy.start()
    start(0)
    r = iota2((rows, rows), 0)
    order = one_hot((r % STEPS) * heads + r // STEPS, rows)
    q_copy.wait()
    new_copy.wait()

    new = new_ref[...]
    s = lax.dot_general(q_ref[...], new, NT, preferred_element_type=F32)
    step = iota2(s.shape, 0) // heads
    s = jnp.where(iota2(s.shape, 1) <= step, s, -1e30)
    m = jnp.max(s, axis=1, keepdims=True)
    p = jnp.exp2((s - m) * factor_base2)
    m_ref[...] = m
    l_ref[...] = jnp.sum(p, axis=1, keepdims=True)
    acc = jnp.dot(p.astype(BF), new[:, :LAT], preferred_element_type=F32)
    acc_ref[...] = jnp.transpose(acc)

    def as_row(column):
        same = iota2((rows, rows), 0) == iota2((rows, rows), 1)
        return jnp.sum(jnp.where(same, column, 0.0), axis=0, keepdims=True)


    start(1)

    def update(i, masked):
        start(i + 2)
        scores = []
        for part in range(2):
            half_copy(i, part).wait()
            s = jnp.dot(q_ref[...], keys_ref[:, half_at(i, part)], preferred_element_type=F32)
            if masked:
                left = length - i * blk - part * half
                s = jnp.where(iota2(s.shape, 1) < left, s, -1e30)
            scores.append(s)
        m_old = m_ref[...]
        m = m_old
        for s in scores:
            m = jnp.maximum(m, jnp.max(s, axis=1, keepdims=True))
        factor = jnp.exp2((m_old - m) * factor_base2)
        m_ref[...] = m
        total = l_ref[...] * factor
        acc = acc_ref[...] * as_row(factor)
        for part, s in enumerate(scores):
            p = jnp.exp2((s - m) * factor_base2)
            total += jnp.sum(p, axis=1, keepdims=True)
            values = keys_ref[:LAT, half_at(i, part)]
            acc += lax.dot_general(values, p.astype(BF), NT, preferred_element_type=F32)
        l_ref[...] = total
        acc_ref[...] = acc

    full = length // blk

    @pl.loop(0, full)
    def _(i):
        update(i, False)

    @pl.when(full * blk < length)
    def _():
        update(full, True)

    out = (acc_ref[...] * as_row(1.0 / l_ref[...])).astype(BF)
    moved = lax.dot_general(order, out, NT, preferred_element_type=F32)
    out_ref[...] = moved.reshape(out_ref.shape).astype(BF)


def attend(n, length, q, new, keys):
    rows, width = q.shape
    cached = keys.shape[1]
    blocks = cached // min(BLK, cached)
    return pl.pallas_call(
        functools.partial(attend_kernel, n),
        in_specs=[pl.BlockSpec(memory_space=pltpu.SMEM)]
        + [pl.BlockSpec(memory_space=pl.ANY)] * 3,
        out_specs=pl.BlockSpec(memory_space=pltpu.VMEM),
        scratch_shapes=[
            pltpu.VMEM(q.shape, BF),
            pltpu.VMEM(new.shape, BF),
            pltpu.VMEM(keys.shape, BF),
            pltpu.VMEM((rows, 1), F32),
            pltpu.VMEM((rows, 1), F32),
            pltpu.VMEM((LAT, rows), F32),
            pltpu.SemaphoreType.DMA((2,)),
            pltpu.SemaphoreType.DMA((blocks, 2)),
        ],
        out_shape=jax.ShapeDtypeStruct((rows // STEPS, STEPS, LAT), BF),
        compiler_params=pltpu.CompilerParams(vmem_limit_bytes=56 * 1024 * 1024),
        cost_estimate=pl.CostEstimate(
            flops=2 * rows * cached * (width + LAT),
            bytes_accessed=2 * cached * width,
            transcendentals=rows * cached,
        ),
        name="attend",
    )(length, q, new, keys)


def source_rows(n, me, rows):
    r = iota2((rows, rows), 0)
    other = r // (rows // 2)
    masks = []
    for firsts, seconds in partners(n):
        i, j = (r // (len(seconds) * STEPS)) % len(firsts), (r // STEPS) % len(seconds)
        mask = jnp.zeros_like(r)
        for index, options in ((i, firsts), (j, seconds)):
            for value, option in enumerate(options):
                mask = mask | jnp.where(index == value, option, 0)
        masks.append(mask)
    mask = jnp.where((me & 1) ^ other == 0, masks[0], masks[1])
    return (me ^ mask ^ other) * STEPS + r % STEPS


def heads_kernel(n, me_ref, latents_ref, uv_ref, out_ref, near_ref, far_ref):
    rows = n * STEPS
    values = jnp.dot(latents_ref[...], uv_ref[...], preferred_element_type=F32).astype(BF)
    values = pick(one_hot(source_rows(n, me_ref[0], rows), rows), values).astype(BF)
    part = out_ref.shape[1] // SPAN
    for p in range(SPAN):
        here = slice(p * part, (p + 1) * part)
        out = jnp.dot(values, out_ref[:, here], preferred_element_type=F32)
        near_ref[:, here] = out[: rows // 2]
        far_ref[:, here] = out[rows // 2 :].astype(BF)


def carry_kernel(n, *refs):
    terms, (residual_ref, routes_ref, mine_ref, sent_ref) = refs[:-4], refs[-4:]
    width = residual_ref.shape[1]
    total = terms[0][...]
    for ref in terms[1:]:
        total += ref[...].astype(F32)
    mine_ref[:, :width] = total
    mine_ref[:STEPS, :width] = total[:STEPS] + residual_ref[...].astype(F32)
    mine_ref[:, width:] = jnp.zeros((total.shape[0], mine_ref.shape[1] - width), F32)
    mine_ref[:STEPS, width:] = routes_ref[...].astype(F32)
    sent_ref[...] = mine_ref[...].astype(BF)


def norm_kernel(n, mine_ref, *refs):
    got, (gain_ref, hidden_ref, out_ref) = refs[:-3], refs[-3:]
    width = gain_ref.shape[1]
    total = mine_ref[...]
    for j, ref in enumerate(got, 1):
        rows = ref[...].astype(F32)
        parts = [(j ^ b) * STEPS for b in range(len(got) + 1)]
        total += jnp.concatenate([rows[first : first + STEPS] for first in parts], axis=0)
    hidden = total[:, :width]
    hidden_ref[...] = hidden[:STEPS]
    mean_square = jnp.sum(hidden * hidden, axis=1, keepdims=True) / width
    normed = hidden * lax.rsqrt(mean_square + 1e-06) * gain_ref[...].astype(F32)
    out_ref[:, :width] = normed.astype(BF)
    out_ref[:, width:] = total[:, width:].astype(BF)


def load_kernel(n, ranges, *refs):
    count = len(ranges)
    sources, targets, sem = refs[1 : 1 + count], refs[2 + count : 2 + 2 * count], refs[-1]
    copies = [pltpu.make_async_copy(refs[0], refs[1 + count], sem.at[0])]
    for source, target, (first, rows) in zip(sources, targets, ranges):
        step = rows // LOADS
        for j in range(LOADS):
            there, here = pl.ds(first + j * step, step), pl.ds(j * step, step)
            copies.append(
                pltpu.make_async_copy(source.at[there], target.at[here], sem.at[len(copies)])
            )
    for copy in copies:
        copy.start()
    for copy in copies:
        copy.wait()


def load(n, passed, arrays, ranges, limit):
    shapes = [(rows, a.shape[1]) for a, (_, rows) in zip(arrays, ranges)]
    return pl.pallas_call(
        functools.partial(load_kernel, n, ranges),
        in_specs=[pl.BlockSpec(memory_space=pltpu.VMEM)]
        + [pl.BlockSpec(memory_space=pl.ANY)] * len(arrays),
        out_specs=[pl.BlockSpec(memory_space=pltpu.VMEM)] * (1 + len(arrays)),
        out_shape=[jax.ShapeDtypeStruct(passed.shape, passed.dtype)]
        + [jax.ShapeDtypeStruct(shape, BF) for shape in shapes],
        scratch_shapes=[pltpu.SemaphoreType.DMA((1 + LOADS * len(arrays),))],
        compiler_params=pltpu.CompilerParams(vmem_limit_bytes=limit * 1024 * 1024),
        cost_estimate=pl.CostEstimate(
            flops=0, bytes_accessed=sum(4 * r * c for r, c in shapes), transcendentals=0
        ),
        name="load",
    )(passed, *arrays)


def expert_kernel(n, me_ref, *refs, n_ep):
    blocks, (early_ref, gate_ref, up_ref, down_ref, near_ref, far_ref) = refs[:8], refs[8:]
    rows = n * STEPS
    width, units = up_ref.shape
    part = width // SPAN
    gate = jnp.zeros((rows, units), F32)
    up = jnp.zeros((rows, units), F32)
    for p in range(SPAN):
        here = slice(p * part, (p + 1) * part)
        x = jnp.concatenate([ref[:, here] for ref in blocks], axis=0)
        late = p - EARLY
        gate_part = early_ref[here] if late < 0 else gate_ref[late * part : (late + 1) * part]
        gate += jnp.dot(x, gate_part, preferred_element_type=F32)
        up += jnp.dot(x, up_ref[here], preferred_element_type=F32)
    act = (gate * jax.nn.sigmoid(gate) * up).astype(BF)
    routes = jnp.concatenate([ref[:, width:] for ref in blocks], axis=0).astype(F32)
    scores = routes[:, TOPK : 2 * TOPK] + routes[:, 2 * TOPK : 3 * TOPK]
    chosen = jnp.where(routes[:, :TOPK] == (me_ref[0] % n_ep).astype(F32), scores, 0.0)
    coef = jnp.sum(chosen, axis=1, keepdims=True) / jnp.sum(scores, axis=1, keepdims=True) * 2.5
    for p in range(SPAN):
        here = slice(p * part, (p + 1) * part)
        out = jnp.dot(act, down_ref[:, here], preferred_element_type=F32) * coef
        near_ref[:, here] = out[: rows // 2]
        far_ref[:, here] = out[rows // 2 :].astype(BF)


def single(kernel, n, out_shape, scalars, arrays, name, flops):
    return pl.pallas_call(
        functools.partial(kernel, n),
        in_specs=[pl.BlockSpec(memory_space=pltpu.SMEM)] * len(scalars)
        + [pl.BlockSpec(memory_space=pltpu.VMEM)] * len(arrays),
        out_shape=out_shape,
        compiler_params=pltpu.CompilerParams(vmem_limit_bytes=VMEM_LIMIT),
        cost_estimate=pl.CostEstimate(
            flops=flops, bytes_accessed=sum(2 * a.size for a in arrays), transcendentals=0
        ),
        name=name,
    )(*scalars, *arrays)


def first_stage(near, far, n, order, beside=lambda rows: rows):
    firsts = len(order) + 1
    total = near + swap_core(far, n).astype(F32)
    total = total.reshape(firsts, total.shape[0] // firsts, total.shape[1])
    got = [swap(total[i].astype(BF), n, 0, i) for i in order]
    return [beside(total[0])] + got


def per_device(
    queries,
    new_latent,
    cache_latent,
    cache_len,
    route_ids,
    route_scores,
    residual,
    norm_gain,
    w_uv,
    w_out,
    w_gate,
    w_up,
    w_down,
):
    n_ep = lax.axis_size("ep")
    n = lax.axis_size("sec") * n_ep
    heads = queries.shape[2]
    width = residual.shape[2]
    rows = n * STEPS
    me_one = lax.axis_index(AXES).astype(jnp.int32).reshape(1)

    with jax.named_scope("attention"):
        latents = attend(
            n,
            cache_len,
            queries[0].reshape(STEPS * heads, queries.shape[3]),
            new_latent[0],
            jnp.swapaxes(cache_latent[0], 0, 1),
        )

    with jax.named_scope("heads"):
        latents = lax.all_to_all(latents, AXES, 0, 0, tiled=True)
        near, far = single(
            heads_kernel,
            n,
            [jax.ShapeDtypeStruct((rows // 2, width), dtype) for dtype in (F32, BF)],
            [me_one],
            [latents.reshape(rows, LAT), w_uv[0], w_out[0]],
            "heads",
            2 * rows * VDIM * (LAT + width),
        )
        early = width // SPAN * EARLY
        loaded = []

        def load_early(rows):
            rows, *weights = load(n, rows, [w_gate[0]], [(0, early)], LOAD_LIMITS[0])
            loaded.extend(weights)
            return rows

        terms = first_stage(near, far, n, (1, 2, 3), load_early)

    with jax.named_scope("norm"):
        high = route_scores[0].astype(BF)
        low = (route_scores[0] - high.astype(F32)).astype(BF)
        routes = jnp.concatenate([route_ids[0].astype(BF), high, low], axis=1)
        routes = jnp.pad(routes, ((0, 0), (0, 128 - 3 * TOPK)))
        shape = (terms[0].shape[0], width + 128)
        mine, sent = single(
            carry_kernel,
            n,
            [jax.ShapeDtypeStruct(shape, dtype) for dtype in (F32, BF)],
            [],
            terms + [residual[0], routes],
            "carry",
            terms[0].size,
        )
        got = [swap(sent, n, 1, j) for j in range(1, n // SPAN)]
        rest = [(early, width - early), (0, width), (0, w_down.shape[1])]
        mine, *weights = load(n, mine, [w_gate[0], w_up[0], w_down[0]], rest, LOAD_LIMITS[1])
        loaded.extend(weights)
        hidden, along = single(
            norm_kernel,
            n,
            [jax.ShapeDtypeStruct((STEPS, width), F32), jax.ShapeDtypeStruct(shape, BF)],
            [],
            [mine] + got + [norm_gain.reshape(1, width)],
            "norm",
            8 * mine.size,
        )

    with jax.named_scope("spread"):
        blocks = [along] + [swap(along, n, 0, i) for i in range(1, 4)]
        blocks = blocks + [swap_core(x, n) for x in blocks]

    with jax.named_scope("experts"):
        near, far = single(
            functools.partial(expert_kernel, n_ep=n_ep),
            n,
            [jax.ShapeDtypeStruct((rows // 2, width), dtype) for dtype in (F32, BF)],
            [me_one],
            blocks + loaded,
            "experts",
            6 * rows * width * w_gate.shape[2],
        )

    with jax.named_scope("collect"):
        kept = 0.0
        for term in first_stage(near, far, n, (3, 2, 1)):
            kept = kept + term.astype(F32)
        kept = kept.reshape(n // SPAN, STEPS, width)
        result = hidden + kept[0]
        for j in reversed(range(1, n // SPAN)):
            result = result + swap(kept[j].astype(BF), n, 1, j).astype(F32)
        return result.astype(BF)[None]


def solution(mesh):
    placed = (
        P(("sec", "ep"), None, None, None),
        P(("sec", "ep"), None, None),
        P(("sec", "ep"), None, None),
        P(("sec", "ep")),
        P(("sec", "ep"), None, None),
        P(("sec", "ep"), None, None),
        P(("sec", "ep"), None, None),
        P(),
        P(("sec", "ep"), None, None),
        P(("sec", "ep"), None, None),
        P("ep", None, "sec"),
        P("ep", None, "sec"),
        P("ep", "sec", None),
    )
    return jax.shard_map(
        per_device,
        mesh=mesh,
        in_specs=placed,
        out_specs=P(("sec", "ep"), None, None),
        check_vma=False,
    )
```
